32 devices in a mesh: groups: 2 (over y), freq: 4 (over z), read: 2 (over x), pair: 2 (over core).
Axes of the slice: x: 2, y: 2, z: 4, core: 2. Of those that a mesh axis runs over, the one named last changes fastest.
Arguments:
- exposures: float32 [8, 2048, 2048], P(('groups', 'read', 'pair'), 'freq'), parts along dimension 0, may hold values from -6 to 6
- stamps: float32 [8, 16, 16], P('groups'), parts along dimension 0, may hold values from -1 to 1, as said below
- zero_point: float32 [8], P('groups'), parts along dimension 0, may hold values from 0.5 to 2
- noise_var: float32 [8], P('groups'), parts along dimension 0, may hold values from 0.25 to 4
- footprint: int32 [8, 2], P('groups'), parts along dimension 0, may hold values from 0 to 2048, as said below
- accept: int32 [8], P('groups'), parts along dimension 0, may hold values from 0 to 1, as said below
- assign: int32 [8], P('groups'), parts along dimension 0, may hold values from 0 to 3, each once
Outputs:
- coadd: float32 [2, 4096, 1024], P(None, ('groups', 'read', 'pair'), 'freq'), parts along dimension 1
The draws below stay inside these ranges and needn't reach their ends.
There are 2 independent parts, one for each index of `groups`. The reference program is written for one: setup_inputs(seed, part) draws one part's arguments, and reference() takes and returns one part's arrays. A program takes and returns all parts, laid end to end along the dimension named above; each array names one. Nothing has to cross between parts.
Inputs may be any that keep to these rules, and one draw needn't show every extreme that they name: `stamps`: each stamp is 1 at row 8 and column 8, and the absolute values of its other entries sum to at most 0.9. For every exposure footprint[e, 0] < footprint[e, 1] and the two differ by at least 512; some exposure covers all 2048 rows. `accept`: at least one exposure is rejected, and at least one exposure that covers all 2048 rows is accepted. `assign`: each exposure sits in exactly one slot.
All inputs are finite; a program needn't handle non-finite values.
Results may differ from the reference program's by a relative error of at most 0.0001.
Values sent between devices are 32-bit elements; how exact they have to be, the bound alone decides.
A program may use at most 64 MiB of HBM per device.

```python
import math
import jax
import jax.numpy as jnp

HEIGHT = 2048
WIDTH = 2048
STAMP = 16
EXPOSURES = 4


def draw_stamps(key, part):
    sign_key = jax.random.fold_in(key, 11)
    size_key = jax.random.fold_in(key, 12)
    shape_all = (EXPOSURES, STAMP, STAMP)
    signs = jnp.where(jax.random.bernoulli(sign_key, 0.5, shape_all), 1.0, -1.0)
    magnitude = jax.random.uniform(size_key, shape_all, jnp.float32, 0.5, 1.0)
    wings = signs * magnitude * (0.9 / (STAMP * STAMP - 1))
    row_ids = jnp.arange(STAMP)
    centre = (row_ids[:, None] == STAMP // 2) & (row_ids[None, :] == STAMP // 2)
    return jnp.where(centre[None], 1.0, wings).astype(jnp.float32)


def full_exposure(key):
    return jax.random.randint(jax.random.fold_in(key, 23), (), 0, EXPOSURES)


def draw_footprint(key, part):
    span_key = jax.random.fold_in(key, 21)
    start_key = jax.random.fold_in(key, 22)
    full_one = full_exposure(key)
    span_rows = jax.random.randint(span_key, (EXPOSURES,), HEIGHT // 4, HEIGHT + 1)
    start_rows = jax.random.randint(start_key, (EXPOSURES,), 0, HEIGHT - span_rows + 1)
    picked = jnp.arange(EXPOSURES) == full_one
    span_rows = jnp.where(picked, HEIGHT, span_rows)
    start_rows = jnp.where(picked, 0, start_rows)
    return jnp.stack([start_rows, start_rows + span_rows], axis=1).astype(jnp.int32)


def draw_accept(key, part):
    flag_key = jax.random.fold_in(key, 31)
    step_key = jax.random.fold_in(key, 33)
    flags = (jax.random.randint(flag_key, (EXPOSURES,), 0, 4) > 0).astype(jnp.int32)
    forced_yes = full_exposure(key)
    forced_no = (forced_yes + 1 + jax.random.randint(step_key, (), 0, EXPOSURES - 1)) % EXPOSURES
    labels = jnp.arange(EXPOSURES)
    flags = jnp.where(labels == forced_yes, 1, flags)
    flags = jnp.where(labels == forced_no, 0, flags)
    return flags.astype(jnp.int32)


def shard_levels(stream_key, dims, split, smallest, top_value):
    factor_of = 1.0
    for axis_at, blocks in split:
        draws = jax.random.uniform(jax.random.fold_in(jax.random.fold_in(stream_key, 6), axis_at), (blocks,), jnp.float32, smallest / len(split), top_value / len(split))
        factor_of = factor_of * jnp.repeat(jnp.exp(draws), dims[axis_at] // blocks).reshape((-1,) + (1,) * (len(dims) - 1 - axis_at))
    return factor_of


def bell_draw(rng, shape, spread, reach, pieces=(), held_as=jnp.bfloat16):
    array = jax.random.normal(rng, shape, jnp.float32) * spread
    if len(pieces) > 0:
        array = shard_levels(rng, shape, pieces, -0.22, 0.18) * array
    return jnp.clip(array, min=-reach, max=reach).astype(held_as)


def setup_inputs(seed: int = 0, part: int = 0) -> dict:
    splits = jax.random.split(jax.random.key(seed), 8)
    part_splits = jax.random.split(jax.random.fold_in(splits[7], part), 8)
    return {
        "exposures": bell_draw(part_splits[0], (EXPOSURES, HEIGHT, WIDTH), 1.0, 6.0, ((0, 4), (1, 4)), jnp.float32),
        "stamps": draw_stamps(jax.random.fold_in(jax.random.fold_in(splits[7], part), 71), part),
        "zero_point": jnp.clip(jnp.exp(jax.random.uniform(part_splits[2], (EXPOSURES,), jnp.float32, math.log(0.5), math.log(2.0))), 0.5, 2.0),
        "noise_var": jnp.clip(jnp.exp(jax.random.uniform(part_splits[3], (EXPOSURES,), jnp.float32, math.log(0.25), math.log(4.0))), 0.25, 4.0),
        "footprint": draw_footprint(jax.random.fold_in(jax.random.fold_in(splits[7], part), 71), part),
        "accept": draw_accept(jax.random.fold_in(jax.random.fold_in(splits[7], part), 71), part),
        "assign": jax.random.permutation(part_splits[6], EXPOSURES).astype(jnp.int32),
    }


def psf_spectrum_full(stamp_set):
    placed = jnp.zeros((HEIGHT, WIDTH), jnp.float32).at[:STAMP, :STAMP].set(stamp_set)
    placed = jnp.roll(placed, (-(STAMP // 2), -(STAMP // 2)), axis=(0, 1))
    return jnp.fft.fft2(placed)[:, :WIDTH // 2]

def reference(exposures, stamps, zero_point, noise_var, footprint, accept, assign):
    half_width = WIDTH // 2
    accepted = accept.astype(jnp.float32)
    numer_weight = accepted * zero_point / noise_var
    denom_weight = accepted * zero_point * zero_point / noise_var
    row_ids = jnp.arange(HEIGHT, dtype=jnp.int32)
    numer_real = jnp.zeros((HEIGHT, half_width), jnp.float32)
    numer_imag = jnp.zeros((HEIGHT, half_width), jnp.float32)
    denom = jnp.zeros((HEIGHT, half_width), jnp.float32)
    for slot_no in range(EXPOSURES):
        exp_id = assign[slot_no]
        frame = exposures[slot_no]
        padded = jnp.pad(frame, 1)
        beside = padded[:-2, 1:-1] + padded[2:, 1:-1] + padded[1:-1, :-2] + padded[1:-1, 2:]
        inside = (row_ids >= footprint[exp_id, 0]) & (row_ids < footprint[exp_id, 1])
        cleaned = jnp.where(inside[:, None], frame - 0.25 * beside, 0.0)
        spectrum = jnp.fft.fft2(cleaned)[:, :half_width]
        kernel = psf_spectrum_full(stamps[exp_id])
        weight = numer_weight[exp_id]
        numer_real = numer_real + weight * (kernel.real * spectrum.real + kernel.imag * spectrum.imag)
        numer_imag = numer_imag + weight * (kernel.real * spectrum.imag - kernel.imag * spectrum.real)
        own_kernel = psf_spectrum_full(stamps[slot_no])
        denom = denom + denom_weight[slot_no] * (own_kernel.real * own_kernel.real + own_kernel.imag * own_kernel.imag)
    scale = 1.0 / math.sqrt(HEIGHT * WIDTH)
    root = jnp.sqrt(denom)
    return jnp.stack([numer_real / root * scale, numer_imag / root * scale])
```

```python
import functools
import math

import jax
import jax.numpy as jnp
import ml_dtypes
import numpy as np
from jax import lax
from jax.experimental import pallas as pl
from jax.experimental.pallas import tpu as pltpu
from jax.sharding import PartitionSpec as P

HIGHEST = lax.Precision.HIGHEST
TWO_PI = 2.0 * math.pi
HALO = 16
TILE = 128
BF16 = jnp.bfloat16
F32 = jnp.float32
READERS = ("read", "pair")


def split_np(table):
    hi = table.astype(np.float32).astype(ml_dtypes.bfloat16)
    lo = (table - hi.astype(np.float64)).astype(np.float32).astype(ml_dtypes.bfloat16)
    return hi, lo


def split(value):
    hi = value.astype(BF16)
    return hi, (value - hi.astype(F32)).astype(BF16)


def angles(left, right, modulus):
    return (np.outer(left, right) % modulus).astype(np.float64) * (TWO_PI / modulus)


def dot(left, right):
    return jnp.dot(left, right, preferred_element_type=F32)


def column_order(width, freqs, readers):
    share = width // 2 // freqs // readers
    parity = np.arange(2)[:, None, None, None]
    reader = np.arange(readers)[None, :, None, None]
    freq = np.arange(freqs)[None, None, :, None]
    inner = np.arange(share // 2)[None, None, None, :]
    ids = freq * (share * readers) + reader * share + 2 * inner + parity
    return ids.reshape(2, -1, TILE)


def row_tables(ids, width):
    half = np.arange(width // 2)
    parts = []
    for tile in range(ids.shape[1]):
        both = []
        for parity in range(2):
            phase = angles(half, ids[parity, tile], width)
            both.append(np.concatenate([np.cos(phase), -np.sin(phase)], axis=1))
        parts.append(np.stack(both))
    return split_np(np.stack(parts))


def front_kernel(info, low, block, high, taps, th, tl, out, ext, ch, cl, grid):
    rows, width = block.shape
    half = width // 2
    height = info[3]

    @pl.when(pl.program_id(0) == 0)
    def _():
        ext[:HALO] = low[...]
        ext[HALO : HALO + rows] = block[...]
        ext[HALO + rows :] = high[...]
        cols = lax.broadcasted_iota(jnp.int32, (16, width), 1)

        def clean(i, carry):
            at = pl.multiple_of(i * 16, 16)
            piece = ext[pl.ds(at, 32), :]
            mid = piece[8:24]
            ids = info[0] - 8 + at + lax.broadcasted_iota(jnp.int32, (16, 1), 0)
            ids = jnp.where(ids < 0, ids + height, ids)
            ids = jnp.where(ids >= height, ids - height, ids)
            up = jnp.where(ids == 0, 0.0, piece[7:23])
            down = jnp.where(ids == height - 1, 0.0, piece[9:25])
            left = jnp.where(cols == 0, 0.0, pltpu.roll(mid, 1, 1))
            right = jnp.where(cols == width - 1, 0.0, pltpu.roll(mid, width - 1, 1))
            inside = (ids >= info[1]) & (ids < info[2])
            cell = jnp.where(inside, mid - 0.25 * (up + down + left + right), 0.0)
            for parity in range(2):
                if parity == 0:
                    fold = cell[:, :half] + cell[:, half:]
                else:
                    fold = cell[:, :half] - cell[:, half:]
                hi, lo = split(fold)
                ch[parity, pl.ds(at, 16), :] = hi
                cl[parity, pl.ds(at, 16), :] = lo
            return carry

        lax.fori_loop(0, (rows + 16) // 16, clean, 0)

    for parity in range(2):
        grid[parity] = (
            dot(ch[parity], th[0, parity])
            + dot(ch[parity], tl[0, parity])
            + dot(cl[parity], th[0, parity])
        )

    def fir(i, carry):
        at = pl.multiple_of(i * 32, 32)
        for parity in range(2):
            re = grid[parity, pl.ds(at, 48), :TILE]
            im = grid[parity, pl.ds(at, 48), TILE:]
            sum_re = jnp.zeros((32, TILE), F32)
            sum_im = jnp.zeros((32, TILE), F32)
            for k in range(8):
                shift_re = re[k : k + 40]
                shift_im = im[k : k + 40]
                for a in (k, k + 8):
                    qr = taps[0, parity, 0, a : a + 1, :]
                    qi = taps[0, parity, 1, a : a + 1, :]
                    xr = shift_re[a - k : a - k + 32]
                    xi = shift_im[a - k : a - k + 32]
                    sum_re = sum_re + (qr * xr + qi * xi)
                    sum_im = sum_im + (qr * xi - qi * xr)
            lane = parity * 2 * TILE
            out[0, pl.ds(at, 32), lane : lane + TILE] = sum_re
            out[0, pl.ds(at, 32), lane + TILE : lane + 2 * TILE] = sum_im
        return carry

    lax.fori_loop(0, rows // 32, fir, 0)


def front(info, low, block, high, taps, tables):
    rows, width = block.shape
    tiles = tables[0].shape[0]
    whole = lambda shape: pl.BlockSpec(shape, lambda t: (0,) * len(shape))
    table_spec = pl.BlockSpec((1, 2, width // 2, 2 * TILE), lambda t: (t, 0, 0, 0))
    return pl.pallas_call(
        front_kernel,
        grid=(tiles,),
        out_shape=jax.ShapeDtypeStruct((tiles, rows, 4 * TILE), F32),
        in_specs=[
            pl.BlockSpec(memory_space=pltpu.SMEM),
            whole((HALO, width)),
            whole((rows, width)),
            whole((HALO, width)),
            pl.BlockSpec((1, 2, 2, taps.shape[3], TILE), lambda t: (t, 0, 0, 0, 0)),
            table_spec,
            table_spec,
        ],
        out_specs=pl.BlockSpec((1, rows, 4 * TILE), lambda t: (t, 0, 0)),
        scratch_shapes=[
            pltpu.VMEM((rows + 2 * HALO, width), F32),
            pltpu.VMEM((2, rows + 16, width // 2), BF16),
            pltpu.VMEM((2, rows + 16, width // 2), BF16),
            pltpu.VMEM((2, rows + 16, 2 * TILE), F32),
        ],
        compiler_params=pltpu.CompilerParams(vmem_limit_bytes=48 * 1024 * 1024),
        name="front",
    )(info, low, block, high, taps, *tables)


MESH = pl.DeviceIdType.MESH
CHUNKS = 4
LANES = 128


def joint_columns(width):
    per_freq = width // 2 // 4
    freq = np.arange(4)[:, None] * per_freq
    inner = np.arange(32)[None, :]
    groups = []
    for k in range(2):
        for rd in range(2):
            for pd in range(2):
                if k == 0:
                    ids = freq + 4 * (32 * rd + inner) + 2 * pd
                else:
                    ids = freq + 64 * (2 * rd + pd) + 2 * inner + 1
                groups.append(ids.reshape(-1))
    return np.stack(groups)


def joint_row_tables(ids, width):
    even, odd = [], []
    for t in range(8):
        depth = width // 4 if t < 4 else width // 2
        phase = angles(np.arange(depth), ids[t], width)
        table = np.concatenate([np.cos(phase), -np.sin(phase)], axis=1)
        (even if t < 4 else odd).append(table)
    return split_np(np.stack(even)) + split_np(np.stack(odd))


def joint_column_tables(height):
    inner = np.arange(256)
    parts = []
    for g in range(8):
        phase = angles(np.arange(256), 8 * inner + g, height)
        parts.append(np.concatenate([np.cos(phase), np.sin(phase)], axis=1))
    return split_np(np.stack(parts))


def joint_twiddles():
    lane = np.arange(LANES)
    table = np.zeros((4, 8, LANES), np.float32)
    for gg in range(4):
        angle = np.where(lane >= 64, TWO_PI * gg / 8, 0.0)
        real = lane % 64 < 32
        table[gg, 0] = np.cos(angle)
        table[gg, 1] = np.where(real, np.sin(angle), 0.0)
        table[gg, 2] = np.where(real, 0.0, -np.sin(angle))
        table[gg, 3] = np.where(lane < 64, 1.0, -1.0)
    return table


def joint_order(ids, width):
    per_freq = width // 2 // 4
    table = np.zeros((256, 256), np.float32)
    for k in range(2):
        for reader in range(4):
            for i in range(32):
                table[k * LANES + reader * 32 + i, ids[4 * k + reader, i] % per_freq] = 1.0
    return table.astype(ml_dtypes.bfloat16)


def joint_psf_tables(height, width, stamp_len):
    offsets = np.arange(stamp_len) - stamp_len // 2
    all_u = angles(np.arange(height), offsets, height)
    hi, lo = split_np(np.concatenate([np.cos(all_u), np.sin(all_u)], axis=1))
    rows = np.concatenate([hi, lo, hi, np.zeros_like(hi)], axis=1).reshape(4, height // 4, LANES)
    all_v = angles(offsets, np.arange(width // 2), width).reshape(stamp_len, 4, -1)
    cols = np.concatenate([np.cos(all_v), -np.sin(all_v)], axis=2).astype(np.float32)
    return rows, cols.transpose(1, 0, 2)


def joint_tap_table(ids, width, stamp_len):
    offsets = np.arange(stamp_len) - stamp_len // 2
    phase = [angles(offsets, ids[t], width) for t in range(8)]
    return np.stack(
        [np.concatenate([np.cos(x), -np.sin(x)], axis=1) for x in phase]
    ).astype(np.float32)


def turn(quads, lanes):
    low = lanes < 64
    first = [None] * 4
    for q in range(2):
        first[q] = jnp.where(low, quads[q], pltpu.roll(quads[q + 2], 64, 1))
        first[q + 2] = jnp.where(low, pltpu.roll(quads[q], 64, 1), quads[q + 2])
    even = lanes % 64 < 32
    result = [None] * 4
    for q in (0, 2):
        result[q] = jnp.where(even, first[q], pltpu.roll(first[q + 1], 32, 1))
        result[q + 1] = jnp.where(even, pltpu.roll(first[q], 96, 1), first[q + 1])
    return result


def joint_kernel(
    zero_point, noise_var, footprint, accept, assign, stamps, block, tap_table,
    th0, tl0, th1, tl1, cth, ctl, twiddle, order, psf_rows, psf_cols, out,
    ext, ch0, cl0, ch1, cl1, grid, taps,
    bh0, bl0, bh1, bl1, ch_tab, cl_tab, prow, inverse,
    work, pair_in, read_in, freq_out, freq_in, mixed, col_out, col_in,
    block_sem, table_sem, halo_send, halo_recv, pair_send, pair_recv,
    read_send, read_recv, freq_send, freq_recv, col_send, col_recv,
):
    rows, width = block.shape
    freqs = 4
    height = rows * freqs
    quarter = width // 4
    half = width // 2
    r = lax.axis_index("read")
    p = lax.axis_index("pair")
    f = lax.axis_index("freq")
    me = 2 * r + p

    def group_at(s):
        rd = jnp.where(s < 2, 1 - r, r)
        pd = jnp.where(s % 2 == 0, 1 - p, p)
        return rd * 2 + pd

    def block_copy(n):
        size = rows // 4
        return pltpu.make_async_copy(
            block.at[pl.ds(n * size, size)], ext.at[pl.ds(HALO + n * size, size)], block_sem.at[n]
        )

    def row_table_copies(k, s):
        t = group_at(s)
        pairs = ((th0, bh0), (tl0, bl0)) if k == 0 else ((th1, bh1), (tl1, bl1))
        return [
            pltpu.make_async_copy(a.at[t], b.at[s], table_sem.at[k, n, s])
            for n, (a, b) in enumerate(pairs)
        ]

    def column_table_copies():
        return (
            pltpu.make_async_copy(cth, ch_tab, table_sem.at[2, 0, 0]),
            pltpu.make_async_copy(ctl, cl_tab, table_sem.at[2, 0, 1]),
        )

    def psf_copy():
        return pltpu.make_async_copy(psf_rows.at[me], prow, table_sem.at[2, 0, 2])

    def halo_copies():
        up = lax.rem(f + 1, freqs)
        down = lax.rem(f + freqs - 1, freqs)
        return (
            pltpu.make_async_remote_copy(
                src_ref=block.at[pl.ds(rows - HALO, HALO)], dst_ref=ext.at[pl.ds(0, HALO)],
                send_sem=halo_send.at[0], recv_sem=halo_recv.at[0],
                device_id={"freq": up}, device_id_type=MESH,
            ),
            pltpu.make_async_remote_copy(
                src_ref=block.at[pl.ds(0, HALO)], dst_ref=ext.at[pl.ds(HALO + rows, HALO)],
                send_sem=halo_send.at[1], recv_sem=halo_recv.at[1],
                device_id={"freq": down}, device_id_type=MESH,
            ),
        )

    chunk = rows // CHUNKS

    def pair_copy(k, n, c):
        part = pl.ds(pl.multiple_of(c * chunk, chunk), chunk)
        return pltpu.make_async_remote_copy(
            src_ref=work.at[k, 2 * n, part], dst_ref=pair_in.at[k, n, part],
            send_sem=pair_send.at[k, n, c], recv_sem=pair_recv.at[k, n, c],
            device_id={"pair": 1 - p}, device_id_type=MESH,
        )

    def read_copy(k, c):
        part = pl.ds(pl.multiple_of(c * chunk, chunk), chunk)
        return pltpu.make_async_remote_copy(
            src_ref=work.at[k, 1, part], dst_ref=read_in.at[k, part],
            send_sem=read_send.at[k, c], recv_sem=read_recv.at[k, c],
            device_id={"read": 1 - r}, device_id_type=MESH,
        )

    def freq_copy(k, d, c):
        part = pl.ds(2 * c, 2)
        to = lax.rem(f + d, freqs)
        return pltpu.make_async_remote_copy(
            src_ref=freq_out.at[k, to, part], dst_ref=freq_in.at[k, f, part],
            send_sem=freq_send.at[k, d - 1, c], recv_sem=freq_recv.at[k, d - 1, c],
            device_id={"freq": to}, device_id_type=MESH,
        )

    def col_copy(k, n):
        rd = 1 - r if n > 0 else r
        pd = p if n == 1 else 1 - p
        return pltpu.make_async_remote_copy(
            src_ref=col_out.at[k, 2 * rd + pd], dst_ref=col_in.at[k, me],
            send_sem=col_send.at[k, n], recv_sem=col_recv.at[k, n],
            device_id={"read": rd, "pair": pd}, device_id_type=MESH,
        )

    barrier = pltpu.get_barrier_semaphore()
    for d in range(1, freqs):
        pl.semaphore_signal(
            barrier, inc=1, device_id={"freq": lax.rem(f + d, freqs)}, device_id_type=MESH
        )
    for rd, pd in ((r, 1 - p), (1 - r, p), (1 - r, 1 - p)):
        pl.semaphore_signal(
            barrier, inc=1, device_id={"read": rd, "pair": pd}, device_id_type=MESH
        )
    for n in range(4):
        block_copy(n).start()
    for k in range(2):
        for s in range(4):
            for copy in row_table_copies(k, s):
                copy.start()
    for copy in column_table_copies():
        copy.start()
    psf_copy().start()

    mine = assign[me]
    first_row = footprint[0, mine]
    last_row = footprint[1, mine]
    scale = 1.0 / math.sqrt(height * width)
    top = accept[mine].astype(F32) * zero_point[mine] * scale
    side = stamps.shape[1]
    stamp = stamps[mine] * (jnp.full((side, side), top, F32) / jnp.full((side, side), noise_var[mine], F32))
    for t in range(8):
        both = jnp.dot(stamp, tap_table[t], precision=HIGHEST, preferred_element_type=F32)
        taps[t, 0] = both[:, :LANES]
        taps[t, 1] = both[:, LANES:]

    pl.semaphore_wait(barrier, freqs + 2)
    for copy in halo_copies():
        copy.start()

    cols = lax.broadcasted_iota(jnp.int32, (16, width), 1)

    def clean(i, carry):
        at = pl.multiple_of(i * 16, 16)
        piece = ext[pl.ds(at, 32), :]
        mid = piece[8:24]
        ids = f * rows - 8 + at + lax.broadcasted_iota(jnp.int32, (16, 1), 0)
        ids = jnp.where(ids < 0, ids + height, ids)
        ids = jnp.where(ids >= height, ids - height, ids)
        up = jnp.where(ids == 0, 0.0, piece[7:23])
        down = jnp.where(ids == height - 1, 0.0, piece[9:25])
        left = jnp.where(cols == 0, 0.0, pltpu.roll(mid, 1, 1))
        right = jnp.where(cols == width - 1, 0.0, pltpu.roll(mid, width - 1, 1))
        inside = (ids >= first_row) & (ids < last_row)
        cell = jnp.where(inside, mid - 0.25 * (up + down + left + right), 0.0)
        total = cell[:, :half] + cell[:, half:]
        here = pl.ds(at, 16)
        hi, lo = split(cell[:, :half] - cell[:, half:])
        ch1[here, :] = hi
        cl1[here, :] = lo
        hi, lo = split(total[:, :quarter] + total[:, quarter:])
        ch0[0, here, :] = hi
        cl0[0, here, :] = lo
        hi, lo = split(total[:, :quarter] - total[:, quarter:])
        ch0[1, here, :] = hi
        cl0[1, here, :] = lo
        return carry

    for n in range(4):
        block_copy(n).wait()
    lax.fori_loop(1, rows // 16, clean, 0)
    for copy in halo_copies():
        copy.wait_recv()
    clean(0, 0)
    clean(rows // 16, 0)

    lanes = lax.broadcasted_iota(jnp.int32, (32, LANES), 1)

    def pack(k, c):
        read_copy(k, c).wait_recv()
        pair_copy(k, 1, c).wait_recv()

        def body(n, carry):
            b = 2 * c + n
            quads = []
            for g in range(2):
                here = pl.ds(pl.multiple_of(b * 64 + g * 32, 32), 32)
                total = work[k, 3, here, :] + pair_in[k, 1, here, :] + read_in[k, here, :]
                quads += [total[:, :LANES], total[:, LANES:]]
            for to, value in enumerate(turn(quads, lanes)):
                freq_out[k, to, b] = value.reshape(4, 8, LANES)
            return carry

        lax.fori_loop(0, 2, body, 0)
        for d in range(1, freqs):
            freq_copy(k, d, c).start()

    def groups(k):
        def step(s, carry):
            for copy in row_table_copies(k, s):
                copy.wait()
            t = group_at(s)
            if k == 0:
                xh, xl, wh, wl = ch0[t % 2], cl0[t % 2], bh0[s], bl0[s]
            else:
                xh, xl, wh, wl = ch1[...], cl1[...], bh1[s], bl1[s]
            both = dot(xh, wh) + dot(xh, wl) + dot(xl, wh)
            grid[0] = both[:, :LANES]
            grid[1] = both[:, LANES:]

            def fir(c, inner):
                for n in range(2):
                    at = pl.multiple_of(c * chunk + n * 64, 64)
                    sums = [[jnp.zeros((8, LANES), F32), jnp.zeros((8, LANES), F32)] for _ in range(8)]
                    for a in range(16):
                        qr = taps[4 * k + t, 0, a : a + 1, :]
                        qi = taps[4 * k + t, 1, a : a + 1, :]
                        for g in range(8):
                            here = pl.ds(at + g + a, 8, stride=8)
                            xr = grid[0, here, :]
                            xi = grid[1, here, :]
                            sums[g][0] = sums[g][0] + (qr * xr + qi * xi)
                            sums[g][1] = sums[g][1] + (qr * xi - qi * xr)
                    for g in range(8):
                        work[k, s, pl.ds(at + 8 * g, 8), :LANES] = sums[g][0]
                        work[k, s, pl.ds(at + 8 * g, 8), LANES:] = sums[g][1]

                @pl.when(s == 0)
                def _():
                    pair_copy(k, 0, c).start()

                @pl.when(s == 2)
                def _():
                    pair_copy(k, 1, c).start()

                @pl.when(s == 1)
                def _():
                    pair_copy(k, 0, c).wait_recv()
                    part = pl.ds(pl.multiple_of(c * chunk, chunk), chunk)
                    work[k, 1, part, :] = work[k, 1, part, :] + pair_in[k, 0, part, :]
                    read_copy(k, c).start()

                return inner

            lax.fori_loop(0, CHUNKS, fir, 0)
            if k == 1:

                @pl.when(s < 3)
                def _():
                    pack(0, s + 1)

            return carry

        lax.fori_loop(0, 4, step, 0)

    def times_j(x, at):
        real = at % 64 < 32
        return jnp.where(real, pltpu.roll(x, 96, 1), -pltpu.roll(x, 32, 1))

    def columns(k):
        for d in range(1, freqs):
            for c in range(CHUNKS):
                freq_copy(k, d, c).wait_recv()
        freq_in[k, f] = freq_out[k, f]
        wide = lax.broadcasted_iota(jnp.int32, (256, LANES), 1)

        def body(gg, carry):
            x = freq_in[k, :, :, gg].reshape(256, LANES)
            hi, lo = split(jnp.concatenate([x, times_j(x, wide)], axis=0))
            rhs = jnp.concatenate([hi, lo], axis=1)
            sides = []
            for g in (gg, gg + 4):
                res = dot(ch_tab[g], rhs)
                sides.append(res[:, :LANES] + res[:, LANES:] + dot(cl_tab[g], hi))
            both = jnp.where(wide < 64, sides[0], sides[1])
            both = pltpu.roll(both, 64, 1) + both * twiddle[gg, 3:4, :]
            mixed[gg] = (
                both * twiddle[gg, 0:1, :]
                + pltpu.roll(both, 96, 1) * twiddle[gg, 1:2, :]
                + pltpu.roll(both, 32, 1) * twiddle[gg, 2:3, :]
            )
            return carry

        lax.fori_loop(0, 4, body, 0)

        def last(i, carry):
            here = pl.ds(pl.multiple_of(i * 32, 32), 32)
            e = [mixed[gg, here, :] for gg in range(4)]
            a, b = e[0] + e[2], e[1] + e[3]
            c, d = e[0] - e[2], times_j(e[1] - e[3], lanes)
            col_out[k, 0, here, :] = a + b
            col_out[k, 1, here, :] = c + d
            col_out[k, 2, here, :] = a - b
            col_out[k, 3, here, :] = c - d
            return carry

        lax.fori_loop(0, 8, last, 0)

    def denominator():
        psf_copy().wait()
        count = stamps.shape[0]
        sides = []
        weights = []
        for e in range(count):
            q = jnp.dot(stamps[e], psf_cols[f], precision=HIGHEST, preferred_element_type=F32)
            turned = jnp.concatenate([q[:, 256:], -q[:, :256]], axis=1)
            hi, lo = split(jnp.concatenate([q, turned], axis=0))
            sides.append(jnp.concatenate([hi, hi, lo, jnp.zeros_like(hi)], axis=0))
            value = accept[e].astype(F32) * zero_point[e] * zero_point[e]
            weights.append(jnp.full((1, 256), value, F32) / jnp.full((1, 256), noise_var[e], F32))
        for n in range(4):
            here = pl.ds(n * 128, 128)
            total = jnp.zeros((128, 256), F32)
            for e in range(count):
                psf = dot(prow[here, :], sides[e])
                re, im = psf[:, :256], psf[:, 256:]
                total = total + weights[e] * (re * re + im * im)
            inverse[here, :] = lax.rsqrt(total)

    groups(0)
    pack(0, 0)
    groups(1)
    denominator()
    for copy in column_table_copies():
        copy.wait()
    columns(0)
    col_copy(0, 0).start()

    def rest(c, carry):
        pack(1, c)
        return carry

    lax.fori_loop(0, CHUNKS, rest, 0)
    col_copy(0, 1).start()
    col_copy(0, 2).start()
    columns(1)
    for n in range(3):
        col_copy(1, n).start()
    for k in range(2):
        col_in[k, me] = col_out[k, me]
        for n in range(3):
            col_copy(k, n).wait_recv()

    wide = lax.broadcasted_iota(jnp.int32, (64, LANES), 1)

    def finish(i, carry):
        at = pl.multiple_of(i * 64, 64)
        parts = []
        for k in range(2):
            quads = [col_in[k, n, pl.ds(at, 64), :] for n in range(4)]
            parts.append(jnp.concatenate(turn(quads, wide), axis=0))
        hi, lo = split(jnp.concatenate(parts, axis=1))
        result = dot(hi, order[...]) + dot(lo, order[...])
        for q in range(4):
            here = pl.ds(256 * (q // 2) + at, 64)
            out[q % 2, here, :] = result[64 * q : 64 * (q + 1)] * inverse[here, :]
        return carry

    lax.fori_loop(0, 4, finish, 0)

    for copy in halo_copies():
        copy.wait_send()
    for k in range(2):
        for c in range(CHUNKS):
            for n in range(2):
                pair_copy(k, n, c).wait_send()
            read_copy(k, c).wait_send()
            for d in range(1, freqs):
                freq_copy(k, d, c).wait_send()
        for n in range(3):
            col_copy(k, n).wait_send()


def joint(block, stamps, zero_point, noise_var, footprint, accept, assign):
    rows, width = block.shape
    height = 4 * rows
    stamp_len = stamps.shape[1]
    ids = joint_columns(width)
    th0, tl0, th1, tl1 = joint_row_tables(ids, width)
    cth, ctl = joint_column_tables(height)
    psf_rows, psf_cols = joint_psf_tables(height, width, stamp_len)
    vmem = pl.BlockSpec(memory_space=pltpu.VMEM)
    smem = pl.BlockSpec(memory_space=pltpu.SMEM)
    anywhere = pl.BlockSpec(memory_space=pl.ANY)
    dma = pltpu.SemaphoreType.DMA
    half, quarter = width // 2, width // 4
    return pl.pallas_call(
        joint_kernel,
        out_shape=jax.ShapeDtypeStruct((2, rows, 256), F32),
        in_specs=[smem] * 5
        + [vmem, anywhere, vmem]
        + [anywhere] * 6
        + [vmem, vmem, anywhere, vmem],
        out_specs=vmem,
        scratch_shapes=[
            pltpu.VMEM((rows + 2 * HALO, width), F32),
            pltpu.VMEM((2, rows + 16, quarter), BF16),
            pltpu.VMEM((2, rows + 16, quarter), BF16),
            pltpu.VMEM((rows + 16, half), BF16),
            pltpu.VMEM((rows + 16, half), BF16),
            pltpu.VMEM((2, rows + 16, LANES), F32),
            pltpu.VMEM((8, 2, 16, LANES), F32),
            pltpu.VMEM((4, quarter, 256), BF16),
            pltpu.VMEM((4, quarter, 256), BF16),
            pltpu.VMEM((4, half, 256), BF16),
            pltpu.VMEM((4, half, 256), BF16),
            pltpu.VMEM((8, 256, 512), BF16),
            pltpu.VMEM((8, 256, 512), BF16),
            pltpu.VMEM((rows, LANES), BF16),
            pltpu.VMEM((rows, 256), F32),
            pltpu.VMEM((2, 4, rows, 256), F32),
            pltpu.VMEM((2, 2, rows, 256), F32),
            pltpu.VMEM((2, rows, 256), F32),
            pltpu.VMEM((2, 4, 8, 4, 8, LANES), F32),
            pltpu.VMEM((2, 4, 8, 4, 8, LANES), F32),
            pltpu.VMEM((4, 256, LANES), F32),
            pltpu.VMEM((2, 4, 256, LANES), F32),
            pltpu.VMEM((2, 4, 256, LANES), F32),
            dma((4,)),
            dma((3, 2, 4)),
            dma((2,)),
            dma((2,)),
            dma((2, 2, CHUNKS)),
            dma((2, 2, CHUNKS)),
            dma((2, CHUNKS)),
            dma((2, CHUNKS)),
            dma((2, 3, CHUNKS)),
            dma((2, 3, CHUNKS)),
            dma((2, 3)),
            dma((2, 3)),
        ],
        compiler_params=pltpu.CompilerParams(
            collective_id=0, has_side_effects=True, vmem_limit_bytes=56 * 1024 * 1024
        ),
        cost_estimate=pl.CostEstimate(flops=7 * 10**9, bytes_accessed=18 * 2**20, transcendentals=0),
        name="joint",
    )(
        zero_point, noise_var, footprint.T, accept, assign, stamps, block,
        joint_tap_table(ids, width, stamp_len),
        th0, tl0, th1, tl1, cth, ctl, joint_twiddles(), joint_order(ids, width), psf_rows, psf_cols,
    )


def column_tables(height):
    quarter = height // 4
    inner = np.arange(quarter)
    parts = []
    for j in range(4):
        phase = angles(4 * np.arange(quarter) + j, inner, height)
        parts.append(np.concatenate([np.cos(phase), np.sin(phase)], axis=1))
    return split_np(np.stack(parts))


def order_matrix(share):
    size = 2 * share
    table = np.zeros((size, 2 * size), np.float32)
    for part in range(2):
        for parity in range(2):
            for j in range(share // 2):
                source = part * share + parity * (share // 2) + j
                place = 2 * j + parity
                table[source, part * share + place] = 1.0
                table[source, size + (1 - part) * share + place] = -1.0 if part == 0 else 1.0
    return table.astype(ml_dtypes.bfloat16)


def column_kernel(x, order, th, tl, out):
    height, lanes = x.shape
    quarter = height // 4
    step = pl.program_id(0)
    for j in range(4):

        @pl.when(step == j)
        def _(j=j):
            parts = []
            for f in range(4):
                hi, lo = split(x[f * quarter : (f + 1) * quarter])
                parts.append(dot(hi, order[...]) + dot(lo, order[...]))
            if j % 2 == 0:
                even, odd = parts[0] + parts[2], parts[1] + parts[3]
                mix = even + odd if j == 0 else even - odd
                top, low = mix[:, :lanes], mix[:, lanes:]
            else:
                even, odd = parts[0] - parts[2], parts[1] - parts[3]
                sign = 1.0 if j == 1 else -1.0
                top = even[:, :lanes] + sign * odd[:, lanes:]
                low = even[:, lanes:] - sign * odd[:, :lanes]
            both = jnp.concatenate([top, low], axis=0)
            hi, lo = split(both)
            wide = dot(th[0], jnp.concatenate([hi, lo], axis=1))
            result = wide[:, :lanes] + wide[:, lanes:] + dot(tl[0], hi)
            out[pl.ds(j, quarter, stride=4), :] = result


def columns(x, order, tables):
    height, lanes = x.shape
    quarter = height // 4
    table_spec = pl.BlockSpec((1, quarter, 2 * quarter), lambda j: (j, 0, 0))
    return pl.pallas_call(
        column_kernel,
        grid=(4,),
        out_shape=jax.ShapeDtypeStruct((height, lanes), F32),
        in_specs=[
            pl.BlockSpec((height, lanes), lambda j: (0, 0)),
            pl.BlockSpec((lanes, 2 * lanes), lambda j: (0, 0)),
            table_spec,
            table_spec,
        ],
        out_specs=pl.BlockSpec((height, lanes), lambda j: (0, 0)),
        compiler_params=pltpu.CompilerParams(vmem_limit_bytes=48 * 1024 * 1024),
        name="columns",
    )(x, order, *tables)


def denom_kernel(weight, rows, cols, out):
    count = cols.shape[0]
    lanes = out.shape[1]
    total = jnp.zeros(out.shape, F32)
    rh, rl = split(rows[...])
    for e in range(count):
        chh, cll = split(cols[e])
        psf = dot(rh, chh) + dot(rh, cll) + dot(rl, chh)
        total = total + weight[e] * (psf[:, :lanes] * psf[:, :lanes] + psf[:, lanes:] * psf[:, lanes:])
    out[...] = lax.rsqrt(total)


def per_device(exposures, stamps, zero_point, noise_var, footprint, accept, assign):
    exp_dev, rows_dev, width = exposures.shape
    freqs = lax.axis_size("freq")
    readers = lax.axis_size(READERS)
    height = rows_dev * freqs
    per_freq = width // 2 // freqs
    share = per_freq // readers
    out_rows = height // readers
    stamp_len = stamps.shape[1]
    count_all = assign.shape[0]
    freq_at = lax.axis_index("freq")
    reader_at = lax.axis_index(READERS)
    sizes = (lax.axis_size("read"), lax.axis_size("pair"), freqs)
    if sizes == (2, 2, 4) and (rows_dev, width, stamp_len, count_all) == (512, 2048, 16, 4):
        return joint(exposures[0], stamps, zero_point, noise_var, footprint, accept, assign)
    ids = column_order(width, freqs, readers)
    tiles = ids.shape[1]
    offsets = np.arange(stamp_len) - stamp_len // 2

    block = exposures[0]
    forward = [(i, (i + 1) % freqs) for i in range(freqs)]
    backward = [(t, s) for s, t in forward]
    low = lax.ppermute(block[rows_dev - HALO :], "freq", forward)
    high = lax.ppermute(block[:HALO], "freq", backward)

    labels = jnp.arange(count_all, dtype=jnp.int32)
    owner = jnp.sum(jnp.where(labels == reader_at, assign, 0))
    chosen = labels == owner
    low_row = jnp.sum(jnp.where(chosen, footprint[:, 0], 0))
    high_row = jnp.sum(jnp.where(chosen, footprint[:, 1], 0))
    accepted = accept.astype(F32)
    numer_weight = accepted * zero_point / noise_var
    denom_weight = accepted * zero_point * zero_point / noise_var
    scale = 1.0 / math.sqrt(height * width)
    weight = jnp.sum(jnp.where(chosen, numer_weight, 0.0)) * scale
    stamp = jnp.sum(jnp.where(chosen[:, None, None], stamps, 0.0), axis=0) * weight
    tap_phase = angles(offsets, ids.reshape(-1), width)
    tap_table = np.stack([np.cos(tap_phase), -np.sin(tap_phase)]).astype(np.float32)
    taps = jnp.einsum("ab,cbp->cap", stamp, tap_table, precision=HIGHEST)
    taps = taps.reshape(2, stamp_len, 2, tiles, TILE).transpose(3, 2, 0, 1, 4)
    info = jnp.stack([freq_at * rows_dev, low_row, high_row, jnp.int32(height)]).astype(jnp.int32)

    tables = row_tables(ids, width)
    terms = front(info, low, block, high, taps, tables)
    if tiles != readers:
        terms = terms.reshape(tiles, rows_dev, 2, 2, readers // tiles, TILE * tiles // readers)
        terms = terms.transpose(0, 4, 1, 2, 3, 5).reshape(readers, rows_dev, -1)
    summed = lax.psum_scatter(terms, READERS, scatter_dimension=0, tiled=True)
    summed = summed.reshape(rows_dev, 2, 2, freqs, share // 2)
    summed = summed.transpose(3, 0, 2, 1, 4).reshape(freqs, rows_dev, 2 * share)
    gathered = lax.all_to_all(summed, "freq", split_axis=0, concat_axis=0, tiled=True)
    grid = columns(gathered.reshape(height, 2 * share), order_matrix(share), column_tables(height))
    grid = lax.all_to_all(
        grid.reshape(readers, out_rows, 2 * share), READERS, split_axis=0, concat_axis=0, tiled=True
    )
    numer = grid.reshape(readers, out_rows, 2, share).transpose(2, 1, 0, 3)
    numer = numer.reshape(2, out_rows, per_freq)

    all_u = angles(np.arange(height), offsets, height)
    all_rows = np.concatenate([np.cos(all_u), np.sin(all_u)], axis=1).astype(np.float32)
    psf_rows = lax.dynamic_slice_in_dim(jnp.asarray(all_rows), reader_at * out_rows, out_rows, 0)
    all_v = angles(offsets, np.arange(width // 2), width)
    all_cols = np.stack([np.cos(all_v), -np.sin(all_v)]).astype(np.float32)
    own_cols = lax.dynamic_slice_in_dim(jnp.asarray(all_cols), freq_at * per_freq, per_freq, 2)
    q = jnp.einsum("nab,cbp->cnap", stamps, own_cols, precision=HIGHEST)
    psf_cols = jnp.concatenate(
        [jnp.concatenate([q[0], q[1]], axis=2), jnp.concatenate([q[1], -q[0]], axis=2)], axis=1
    )
    inverse = pl.pallas_call(
        denom_kernel,
        out_shape=jax.ShapeDtypeStruct((out_rows, per_freq), F32),
        in_specs=[
            pl.BlockSpec(memory_space=pltpu.SMEM),
            pl.BlockSpec(memory_space=pltpu.VMEM),
            pl.BlockSpec(memory_space=pltpu.VMEM),
        ],
        out_specs=pl.BlockSpec(memory_space=pltpu.VMEM),
        compiler_params=pltpu.CompilerParams(vmem_limit_bytes=32 * 1024 * 1024),
        name="denom",
    )(denom_weight, psf_rows, psf_cols)
    return numer * inverse


def solution(mesh):
    in_specs = (
        P(("groups", "read", "pair"), "freq", None),
        P("groups", None, None),
        P("groups"),
        P("groups"),
        P("groups", None),
        P("groups"),
        P("groups"),
    )
    out_specs = P(None, ("groups", "read", "pair"), "freq")
    return jax.shard_map(
        per_device, mesh=mesh, in_specs=in_specs, out_specs=out_specs, check_vma=False
    )
```

```python
import functools
import math

import jax
import jax.numpy as jnp
import ml_dtypes
import numpy as np
from jax import lax
from jax.experimental import pallas as pl
from jax.experimental.pallas import tpu as pltpu
from jax.sharding import PartitionSpec as P

HIGHEST = lax.Precision.HIGHEST
TWO_PI = 2.0 * math.pi
HALO = 16
TILE = 128
BF16 = jnp.bfloat16
F32 = jnp.float32
READERS = ("read", "pair")


def split_np(table):
    hi = table.astype(np.float32).astype(ml_dtypes.bfloat16)
    lo = (table - hi.astype(np.float64)).astype(np.float32).astype(ml_dtypes.bfloat16)
    return hi, lo


def split(value):
    hi = value.astype(BF16)
    return hi, (value - hi.astype(F32)).astype(BF16)


def angles(left, right, modulus):
    return (np.outer(left, right) % modulus).astype(np.float64) * (TWO_PI / modulus)


def dot(left, right):
    return jnp.dot(left, right, preferred_element_type=F32)


def column_order(width, freqs, readers):
    share = width // 2 // freqs // readers
    parity = np.arange(2)[:, None, None, None]
    reader = np.arange(readers)[None, :, None, None]
    freq = np.arange(freqs)[None, None, :, None]
    inner = np.arange(share // 2)[None, None, None, :]
    ids = freq * (share * readers) + reader * share + 2 * inner + parity
    return ids.reshape(2, -1, TILE)


def row_tables(ids, width):
    half = np.arange(width // 2)
    parts = []
    for tile in range(ids.shape[1]):
        both = []
        for parity in range(2):
            phase = angles(half, ids[parity, tile], width)
            both.append(np.concatenate([np.cos(phase), -np.sin(phase)], axis=1))
        parts.append(np.stack(both))
    return split_np(np.stack(parts))


def front_kernel(info, low, block, high, taps, th, tl, out, ext, ch, cl, grid):
    rows, width = block.shape
    half = width // 2
    height = info[3]

    @pl.when(pl.program_id(0) == 0)
    def _():
        ext[:HALO] = low[...]
        ext[HALO : HALO + rows] = block[...]
        ext[HALO + rows :] = high[...]
        cols = lax.broadcasted_iota(jnp.int32, (16, width), 1)

        def clean(i, carry):
            at = pl.multiple_of(i * 16, 16)
            piece = ext[pl.ds(at, 32), :]
            mid = piece[8:24]
            ids = info[0] - 8 + at + lax.broadcasted_iota(jnp.int32, (16, 1), 0)
            ids = jnp.where(ids < 0, ids + height, ids)
            ids = jnp.where(ids >= height, ids - height, ids)
            up = jnp.where(ids == 0, 0.0, piece[7:23])
            down = jnp.where(ids == height - 1, 0.0, piece[9:25])
            left = jnp.where(cols == 0, 0.0, pltpu.roll(mid, 1, 1))
            right = jnp.where(cols == width - 1, 0.0, pltpu.roll(mid, width - 1, 1))
            inside = (ids >= info[1]) & (ids < info[2])
            cell = jnp.where(inside, mid - 0.25 * (up + down + left + right), 0.0)
            for parity in range(2):
                if parity == 0:
                    fold = cell[:, :half] + cell[:, half:]
                else:
                    fold = cell[:, :half] - cell[:, half:]
                hi, lo = split(fold)
                ch[parity, pl.ds(at, 16), :] = hi
                cl[parity, pl.ds(at, 16), :] = lo
            return carry

        lax.fori_loop(0, (rows + 16) // 16, clean, 0)

    for parity in range(2):
        grid[parity] = (
            dot(ch[parity], th[0, parity])
            + dot(ch[parity], tl[0, parity])
            + dot(cl[parity], th[0, parity])
        )

    def fir(i, carry):
        at = pl.multiple_of(i * 32, 32)
        for parity in range(2):
            re = grid[parity, pl.ds(at, 48), :TILE]
            im = grid[parity, pl.ds(at, 48), TILE:]
            sum_re = jnp.zeros((32, TILE), F32)
            sum_im = jnp.zeros((32, TILE), F32)
            for k in range(8):
                shift_re = re[k : k + 40]
                shift_im = im[k : k + 40]
                for a in (k, k + 8):
                    qr = taps[0, parity, 0, a : a + 1, :]
                    qi = taps[0, parity, 1, a : a + 1, :]
                    xr = shift_re[a - k : a - k + 32]
                    xi = shift_im[a - k : a - k + 32]
                    sum_re = sum_re + (qr * xr + qi * xi)
                    sum_im = sum_im + (qr * xi - qi * xr)
            lane = parity * 2 * TILE
            out[0, pl.ds(at, 32), lane : lane + TILE] = sum_re
            out[0, pl.ds(at, 32), lane + TILE : lane + 2 * TILE] = sum_im
        return carry

    lax.fori_loop(0, rows // 32, fir, 0)


def front(info, low, block, high, taps, tables):
    rows, width = block.shape
    tiles = tables[0].shape[0]
    whole = lambda shape: pl.BlockSpec(shape, lambda t: (0,) * len(shape))
    table_spec = pl.BlockSpec((1, 2, width // 2, 2 * TILE), lambda t: (t, 0, 0, 0))
    return pl.pallas_call(
        front_kernel,
        grid=(tiles,),
        out_shape=jax.ShapeDtypeStruct((tiles, rows, 4 * TILE), F32),
        in_specs=[
            pl.BlockSpec(memory_space=pltpu.SMEM),
            whole((HALO, width)),
            whole((rows, width)),
            whole((HALO, width)),
            pl.BlockSpec((1, 2, 2, taps.shape[3], TILE), lambda t: (t, 0, 0, 0, 0)),
            table_spec,
            table_spec,
        ],
        out_specs=pl.BlockSpec((1, rows, 4 * TILE), lambda t: (t, 0, 0)),
        scratch_shapes=[
            pltpu.VMEM((rows + 2 * HALO, width), F32),
            pltpu.VMEM((2, rows + 16, width // 2), BF16),
            pltpu.VMEM((2, rows + 16, width // 2), BF16),
            pltpu.VMEM((2, rows + 16, 2 * TILE), F32),
        ],
        compiler_params=pltpu.CompilerParams(vmem_limit_bytes=48 * 1024 * 1024),
        name="front",
    )(info, low, block, high, taps, *tables)


MESH = pl.DeviceIdType.MESH
CHUNKS = 4
LANES = 128


def joint_columns(width):
    per_freq = width // 2 // 4
    freq = np.arange(4)[:, None] * per_freq
    inner = np.arange(32)[None, :]
    groups = []
    for k in range(2):
        for rd in range(2):
            for pd in range(2):
                if k == 0:
                    ids = freq + 4 * (32 * rd + inner) + 2 * pd
                else:
                    ids = freq + 64 * (2 * rd + pd) + 2 * inner + 1
                groups.append(ids.reshape(-1))
    return np.stack(groups)


def joint_row_tables(ids, width):
    even, odd = [], []
    for t in range(8):
        depth = width // 4 if t < 4 else width // 2
        phase = angles(np.arange(depth), ids[t], width)
        table = np.concatenate([np.cos(phase), -np.sin(phase)], axis=1)
        (even if t < 4 else odd).append(table)
    return split_np(np.stack(even)) + split_np(np.stack(odd))


def joint_column_tables(height):
    inner = np.arange(256)
    parts = []
    for g in range(8):
        phase = angles(np.arange(256), 8 * inner + g, height)
        parts.append(np.concatenate([np.cos(phase), np.sin(phase)], axis=1))
    tables = np.stack(split_np(np.stack(parts).reshape(2, 4, 256, 512)))
    return tables.transpose(2, 0, 1, 3, 4).reshape(4, 1024, 512)


def joint_twiddles():
    lane = np.arange(LANES)
    table = np.zeros((4, 8, LANES), np.float32)
    for gg in range(4):
        angle = np.where(lane >= 64, TWO_PI * gg / 8, 0.0)
        real = lane % 64 < 32
        table[gg, 0] = np.cos(angle)
        table[gg, 1] = np.where(real, np.sin(angle), 0.0)
        table[gg, 2] = np.where(real, 0.0, -np.sin(angle))
        table[gg, 3] = np.where(lane < 64, 1.0, -1.0)
    return table


def joint_order(ids, width):
    per_freq = width // 2 // 4
    table = np.zeros((256, 256), np.float32)
    for k in range(2):
        for reader in range(4):
            for i in range(32):
                table[k * LANES + reader * 32 + i, ids[4 * k + reader, i] % per_freq] = 1.0
    return table.astype(ml_dtypes.bfloat16)


def joint_psf_tables(height, width, stamp_len):
    offsets = np.arange(stamp_len) - stamp_len // 2
    all_u = angles(np.arange(height), offsets, height)
    hi, lo = split_np(np.concatenate([np.cos(all_u), np.sin(all_u)], axis=1))
    rows = np.concatenate([hi, lo, hi, np.zeros_like(hi)], axis=1).reshape(4, height // 4, LANES)
    all_v = angles(offsets, np.arange(width // 2), width).reshape(stamp_len, 4, -1)
    cols = np.concatenate([np.cos(all_v), -np.sin(all_v)], axis=2).astype(np.float32)
    return rows, cols.transpose(1, 0, 2)


def joint_tap_table(ids, width, stamp_len):
    offsets = np.arange(stamp_len) - stamp_len // 2
    phase = [angles(offsets, ids[t], width) for t in range(8)]
    return np.concatenate(
        [np.concatenate([np.cos(x), -np.sin(x)], axis=1) for x in phase], axis=1
    ).astype(np.float32)


def turn(quads, lanes):
    low = lanes < 64
    first = [None] * 4
    for q in range(2):
        first[q] = jnp.where(low, quads[q], pltpu.roll(quads[q + 2], 64, 1))
        first[q + 2] = jnp.where(low, pltpu.roll(quads[q], 64, 1), quads[q + 2])
    even = lanes % 64 < 32
    result = [None] * 4
    for q in (0, 2):
        result[q] = jnp.where(even, first[q], pltpu.roll(first[q + 1], 32, 1))
        result[q + 1] = jnp.where(even, pltpu.roll(first[q], 96, 1), first[q + 1])
    return result


def joint_kernel(
    zero_point, noise_var, footprint, accept, assign, stamps, block, tap_table,
    th0, tl0, th1, tl1, ctab, twiddle, order, psf_rows, psf_cols, out,
    ext, even, odd, grid, taps,
    bh0, bl0, bh1, bl1, col_tab, prow, inverse,
    work, pair_in, read_in, freq_out, freq_in, mixed, col_out, col_in,
    block_sem, table_sem, halo_send, halo_recv, pair_send, pair_recv,
    read_send, read_recv, freq_send, freq_recv, col_send, col_recv,
):
    rows, width = block.shape
    freqs = 4
    height = rows * freqs
    quarter = width // 4
    half = width // 2
    r = lax.axis_index("read")
    p = lax.axis_index("pair")
    f = lax.axis_index("freq")
    me = 2 * r + p

    def group_at(s):
        rd = jnp.where(s < 2, 1 - r, r)
        pd = jnp.where(s % 2 == 0, 1 - p, p)
        return rd * 2 + pd

    def block_copy(n):
        size = rows // 4
        return pltpu.make_async_copy(
            block.at[pl.ds(n * size, size)], ext.at[pl.ds(HALO + n * size, size)], block_sem.at[n]
        )

    def row_table_copies(k, s):
        t = group_at(s)
        pairs = ((th0, bh0), (tl0, bl0)) if k == 0 else ((th1, bh1), (tl1, bl1))
        return [
            pltpu.make_async_copy(a.at[t], b.at[s], table_sem.at[k, n, s])
            for n, (a, b) in enumerate(pairs)
        ]

    def column_table_copy():
        return pltpu.make_async_copy(ctab, col_tab, table_sem.at[2, 0, 0])

    def psf_copy():
        return pltpu.make_async_copy(psf_rows.at[me], prow, table_sem.at[2, 0, 2])

    def halo_copies():
        up = lax.rem(f + 1, freqs)
        down = lax.rem(f + freqs - 1, freqs)
        return (
            pltpu.make_async_remote_copy(
                src_ref=block.at[pl.ds(rows - HALO, HALO)], dst_ref=ext.at[pl.ds(0, HALO)],
                send_sem=halo_send.at[0], recv_sem=halo_recv.at[0],
                device_id={"freq": up}, device_id_type=MESH,
            ),
            pltpu.make_async_remote_copy(
                src_ref=block.at[pl.ds(0, HALO)], dst_ref=ext.at[pl.ds(HALO + rows, HALO)],
                send_sem=halo_send.at[1], recv_sem=halo_recv.at[1],
                device_id={"freq": down}, device_id_type=MESH,
            ),
        )

    chunk = rows // CHUNKS

    def pair_copy(k, n, c):
        part = pl.ds(pl.multiple_of(c * chunk, chunk), chunk)
        return pltpu.make_async_remote_copy(
            src_ref=work.at[k, 2 * n, part], dst_ref=pair_in.at[k, n, part],
            send_sem=pair_send.at[k, n, c], recv_sem=pair_recv.at[k, n, c],
            device_id={"pair": 1 - p}, device_id_type=MESH,
        )

    def read_copy(k, c):
        part = pl.ds(pl.multiple_of(c * chunk, chunk), chunk)
        return pltpu.make_async_remote_copy(
            src_ref=work.at[k, 1, part], dst_ref=read_in.at[k, part],
            send_sem=read_send.at[k, c], recv_sem=read_recv.at[k, c],
            device_id={"read": 1 - r}, device_id_type=MESH,
        )

    def freq_copy(k, d, c):
        part = pl.ds(2 * c, 2)
        to = lax.rem(f + d, freqs)
        return pltpu.make_async_remote_copy(
            src_ref=freq_out.at[k, to, part], dst_ref=freq_in.at[k, f, part],
            send_sem=freq_send.at[k, d - 1, c], recv_sem=freq_recv.at[k, d - 1, c],
            device_id={"freq": to}, device_id_type=MESH,
        )

    def col_copy(k, n):
        rd = jnp.where(n > 0, 1 - r, r)
        pd = jnp.where(n == 1, p, 1 - p)
        return pltpu.make_async_remote_copy(
            src_ref=col_out.at[k, 2 * rd + pd], dst_ref=col_in.at[k, me],
            send_sem=col_send.at[k, n], recv_sem=col_recv.at[k, n],
            device_id={"read": rd, "pair": pd}, device_id_type=MESH,
        )

    barrier = pltpu.get_barrier_semaphore()
    for d in range(1, freqs):
        pl.semaphore_signal(
            barrier, inc=1, device_id={"freq": lax.rem(f + d, freqs)}, device_id_type=MESH
        )
    for rd, pd in ((r, 1 - p), (1 - r, p), (1 - r, 1 - p)):
        pl.semaphore_signal(
            barrier, inc=1, device_id={"read": rd, "pair": pd}, device_id_type=MESH
        )
    for n in range(4):
        block_copy(n).start()
    for s in range(2):
        for copy in row_table_copies(0, s):
            copy.start()

    mine = assign[me]
    first_row = footprint[0, mine]
    last_row = footprint[1, mine]
    scale = 1.0 / math.sqrt(height * width)
    top = accept[mine].astype(F32) * zero_point[mine] * scale
    side = stamps.shape[1]
    stamp = stamps[mine] * (jnp.full((side, side), top, F32) / jnp.full((side, side), noise_var[mine], F32))
    every = jnp.dot(stamp, tap_table[...], precision=HIGHEST, preferred_element_type=F32)
    for t in range(8):
        for n in range(2):
            taps[t, n] = every[:, (2 * t + n) * LANES : (2 * t + n + 1) * LANES]

    pl.semaphore_wait(barrier, freqs + 2)
    for copy in halo_copies():
        copy.start()

    edge = lax.broadcasted_iota(jnp.int32, (16, LANES), 1)
    last_lane = width - LANES

    def clean_at(at, rim):
        piece = ext[pl.ds(at, 32), :]
        mid = piece[8:24]
        ids = f * rows - 8 + at + lax.broadcasted_iota(jnp.int32, (16, 1), 0)
        up, down = piece[7:23], piece[9:25]
        if rim:
            ids = jnp.where(ids < 0, ids + height, ids)
            ids = jnp.where(ids >= height, ids - height, ids)
            up = jnp.where(ids == 0, 0.0, up)
            down = jnp.where(ids == height - 1, 0.0, down)
        left = pltpu.roll(mid, 1, 1)
        left = jnp.concatenate(
            [jnp.where(edge == 0, 0.0, left[:, :LANES]), left[:, LANES:]], axis=1
        )
        right = pltpu.roll(mid, width - 1, 1)
        right = jnp.concatenate(
            [right[:, :last_lane], jnp.where(edge == LANES - 1, 0.0, right[:, last_lane:])], axis=1
        )
        inside = (ids >= first_row) & (ids < last_row)
        cell = jnp.where(inside, mid - 0.25 * (up + down + left + right), 0.0)
        total = cell[:, :half] + cell[:, half:]
        here = pl.ds(at, 16)
        odd[0, here, :], odd[1, here, :] = split(cell[:, :half] - cell[:, half:])
        even[0, 0, here, :], even[0, 1, here, :] = split(total[:, :quarter] + total[:, quarter:])
        even[1, 0, here, :], even[1, 1, here, :] = split(total[:, :quarter] - total[:, quarter:])

    for n in range(4):
        block_copy(n).wait()
    for s in range(2, 4):
        for copy in row_table_copies(0, s):
            copy.start()
    for s in range(4):
        for copy in row_table_copies(1, s):
            copy.start()
    column_table_copy().start()
    psf_copy().start()

    lanes = lax.broadcasted_iota(jnp.int32, (32, LANES), 1)

    def pack(k, c):
        pair_copy(k, 1, c).wait_recv()

        def body(n, carry):
            b = 2 * c + n
            quads = []
            for g in range(2):
                here = pl.ds(pl.multiple_of(b * 64 + g * 32, 32), 32)
                total = work[k, 3, here, :] + pair_in[k, 1, here, :] + read_in[k, here, :]
                quads += [total[:, :LANES], total[:, LANES:]]
            for to, value in enumerate(turn(quads, lanes)):
                freq_out[k, to, b] = value.reshape(4, 8, LANES)
            return carry

        lax.fori_loop(0, 2, body, 0)
        for d in range(1, freqs):
            freq_copy(k, d, c).start()

    def wait_tables(k, s):
        for copy in row_table_copies(k, s):
            copy.wait()

    def store_grid(xh, xl, wh, wl):
        both = dot(xh, wh) + dot(xh, wl) + dot(xl, wh)
        grid[0] = both[:, :LANES]
        grid[1] = both[:, LANES:]

    def multiply(k, s):
        @pl.when(k == 0)
        def _():
            wait_tables(0, s)
            kind = group_at(s) % 2
            store_grid(even[kind, 0], even[kind, 1], bh0[s], bl0[s])

        @pl.when(k == 1)
        def _():
            wait_tables(1, s)
            store_grid(odd[0], odd[1], bh1[s], bl1[s])

    def fir(k, s, c):
        t = 4 * k + group_at(s)
        for n in range(2):
            at = pl.multiple_of(c * chunk + n * 64, 64)
            sums = [[jnp.zeros((8, LANES), F32), jnp.zeros((8, LANES), F32)] for _ in range(8)]
            for a in range(16):
                qr = taps[t, 0, a : a + 1, :]
                qi = taps[t, 1, a : a + 1, :]
                for g in range(8):
                    here = pl.ds(at + g + a, 8, stride=8)
                    xr = grid[0, here, :]
                    xi = grid[1, here, :]
                    sums[g][0] = sums[g][0] + (qr * xr + qi * xi)
                    sums[g][1] = sums[g][1] + (qr * xi - qi * xr)
            for g in range(8):
                work[k, s, pl.ds(at + 8 * g, 8), :LANES] = sums[g][0]
                work[k, s, pl.ds(at + 8 * g, 8), LANES:] = sums[g][1]

    def sum_pair(k, c):
        pair_copy(k, 0, c).wait_recv()
        part = pl.ds(pl.multiple_of(c * chunk, chunk), chunk)
        work[k, 1, part, :] = work[k, 1, part, :] + pair_in[k, 0, part, :]

    def group(n, carry):
        k, s = n // 4, n % 4
        multiply(k, s)

        def body(c, inner):
            fir(k, s, c)

            @pl.when(s % 2 == 0)
            def _():
                pair_copy(k, s // 2, c).start()

            @pl.when(s == 1)
            def _():
                sum_pair(k, c)

                @pl.when(c < 2)
                def _():
                    read_copy(k, c).start()

            return inner

        lax.fori_loop(0, CHUNKS, body, 0)

        @pl.when(n == 2)
        def _():
            read_copy(0, 2).wait_recv()
            read_copy(0, 0).start()

        @pl.when((n == 5) | (n == 6))
        def _():
            read_copy(0, lax.rem(n + 2, 4)).wait_recv()

        @pl.when((n > 2) & (n < 7))
        def _():
            pack(0, lax.rem(n + 2, 4))

        return carry

    def times_j(x, at):
        real = at % 64 < 32
        return jnp.where(real, pltpu.roll(x, 96, 1), -pltpu.roll(x, 32, 1))

    def columns(k):
        for d in range(1, freqs):
            for c in range(CHUNKS):
                freq_copy(k, d, c).wait_recv()
        freq_in[k, f] = freq_out[k, f]
        tall = lax.broadcasted_iota(jnp.int32, (256, LANES), 1)

        def residue(gg, carry):
            x = freq_in[k, :, :, gg].reshape(256, LANES)
            hi, lo = split(jnp.concatenate([x, times_j(x, tall)], axis=0))
            res = dot(col_tab[gg], jnp.concatenate([hi, lo], axis=1))
            sides = [
                res[n : n + 256, :LANES] + res[n : n + 256, LANES:] + res[n + 512 : n + 768, :LANES]
                for n in (0, 256)
            ]
            both = jnp.where(tall < 64, sides[0], sides[1])
            both = pltpu.roll(both, 64, 1) + both * twiddle[gg, 3:4, :]
            mixed[gg] = (
                both * twiddle[gg, 0:1, :]
                + pltpu.roll(both, 96, 1) * twiddle[gg, 1:2, :]
                + pltpu.roll(both, 32, 1) * twiddle[gg, 2:3, :]
            )
            return carry

        lax.fori_loop(0, 4, residue, 0)

        def last(i, carry):
            here = pl.ds(pl.multiple_of(i * 32, 32), 32)
            e = [mixed[gg, here, :] for gg in range(4)]
            a, b = e[0] + e[2], e[1] + e[3]
            c, d = e[0] - e[2], times_j(e[1] - e[3], lanes)
            col_out[k, 0, here, :] = a + b
            col_out[k, 1, here, :] = c + d
            col_out[k, 2, here, :] = a - b
            col_out[k, 3, here, :] = c - d
            return carry

        lax.fori_loop(0, 8, last, 0)

    def denominator():
        psf_copy().wait()
        count = stamps.shape[0]
        sides = []
        weights = []
        for e in range(count):
            q = jnp.dot(stamps[e], psf_cols[f], precision=HIGHEST, preferred_element_type=F32)
            turned = jnp.concatenate([q[:, 256:], -q[:, :256]], axis=1)
            hi, lo = split(jnp.concatenate([q, turned], axis=0))
            sides.append(jnp.concatenate([hi, hi, lo, jnp.zeros_like(hi)], axis=0))
            value = accept[e].astype(F32) * zero_point[e] * zero_point[e]
            weights.append(jnp.full((1, 256), value, F32) / jnp.full((1, 256), noise_var[e], F32))
        for n in range(4):
            here = pl.ds(n * 128, 128)
            total = jnp.zeros((128, 256), F32)
            for e in range(count):
                psf = dot(prow[here, :], sides[e])
                re, im = psf[:, :256], psf[:, 256:]
                total = total + weights[e] * (re * re + im * im)
            inverse[here, :] = lax.rsqrt(total)

    def open_half(i, carry):
        c0 = 1 + 2 * i

        def piece(t, inner):
            at = jnp.where(i == 0, 8 + t, jnp.where(t < 7, 25 + t, t - 6))
            clean_at(pl.multiple_of(at * 16, 16), False)
            return inner

        lax.fori_loop(0, 17 - 3 * i, piece, 0)

        @pl.when(i == 1)
        def _():
            for copy in halo_copies():
                copy.wait_recv()

            def rim(t, inner):
                clean_at(pl.multiple_of(t * rows, rows), True)
                return inner

            lax.fori_loop(0, 2, rim, 0)

        def two(s, inner):
            @pl.when(i == 0)
            def _():
                wait_tables(0, s)

            kind = group_at(s) % 2
            spots = [
                pl.ds(pl.multiple_of(lax.rem(c0 + n, CHUNKS) * chunk, chunk), chunk + 16)
                for n in range(2)
            ]
            xh = jnp.concatenate([even[kind, 0, here, :] for here in spots], axis=0)
            xl = jnp.concatenate([even[kind, 1, here, :] for here in spots], axis=0)
            both = dot(xh, bh0[s]) + dot(xh, bl0[s]) + dot(xl, bh0[s])
            for n, here in enumerate(spots):
                part = both[n * (chunk + 16) : (n + 1) * (chunk + 16)]
                grid[0, here, :] = part[:, :LANES]
                grid[1, here, :] = part[:, LANES:]

            def body(n, inner2):
                c = lax.rem(c0 + n, CHUNKS)
                fir(0, s, c)

                @pl.when(s == 0)
                def _():
                    pair_copy(0, 0, c).start()

                @pl.when(s == 1)
                def _():
                    sum_pair(0, c)

                    @pl.when(i == 0)
                    def _():
                        read_copy(0, c).start()

                return inner2

            lax.fori_loop(0, 2, body, 0)
            return inner

        lax.fori_loop(0, 2, two, 0)
        return carry

    lax.fori_loop(0, 2, open_half, 0)
    read_copy(0, 1).wait_recv()
    read_copy(0, 3).start()
    lax.fori_loop(2, 8, group, 0)

    def receive(c, carry):
        read_copy(1, c).wait_recv()

        @pl.when(c < 2)
        def _():
            read_copy(1, c + 2).start()

        @pl.when(c == 3)
        def _():
            col_copy(0, 1).start()
            col_copy(0, 2).start()

        pack(1, c)
        return carry

    column_table_copy().wait()

    def ending(k, carry):
        lax.fori_loop(2 * k, 2 * k + 2, receive, 0)

        @pl.when(k == 1)
        def _():
            denominator()

        columns(k)
        col_copy(k, 0).start()

        @pl.when(k == 1)
        def _():
            col_copy(1, 1).start()
            col_copy(1, 2).start()

        return carry

    lax.fori_loop(0, 2, ending, 0)
    for k in range(2):
        col_in[k, me] = col_out[k, me]
        for n in range(3):
            col_copy(k, n).wait_recv()

    wide = lax.broadcasted_iota(jnp.int32, (64, LANES), 1)

    def finish(i, carry):
        at = pl.multiple_of(i * 64, 64)
        parts = []
        for k in range(2):
            quads = [col_in[k, n, pl.ds(at, 64), :] for n in range(4)]
            parts.append(jnp.concatenate(turn(quads, wide), axis=0))
        hi, lo = split(jnp.concatenate(parts, axis=1))
        result = dot(hi, order[...]) + dot(lo, order[...])
        for q in range(4):
            here = pl.ds(256 * (q // 2) + at, 64)
            out[q % 2, here, :] = result[64 * q : 64 * (q + 1)] * inverse[here, :]
        return carry

    lax.fori_loop(0, 4, finish, 0)

    for copy in halo_copies():
        copy.wait_send()
    for k in range(2):
        for c in range(CHUNKS):
            for n in range(2):
                pair_copy(k, n, c).wait_send()
            read_copy(k, c).wait_send()
            for d in range(1, freqs):
                freq_copy(k, d, c).wait_send()
        for n in range(3):
            col_copy(k, n).wait_send()


def joint(block, stamps, zero_point, noise_var, footprint, accept, assign):
    rows, width = block.shape
    height = 4 * rows
    stamp_len = stamps.shape[1]
    ids = joint_columns(width)
    th0, tl0, th1, tl1 = joint_row_tables(ids, width)
    psf_rows, psf_cols = joint_psf_tables(height, width, stamp_len)
    vmem = pl.BlockSpec(memory_space=pltpu.VMEM)
    smem = pl.BlockSpec(memory_space=pltpu.SMEM)
    anywhere = pl.BlockSpec(memory_space=pltpu.HBM)
    dma = pltpu.SemaphoreType.DMA
    half, quarter = width // 2, width // 4
    return pl.pallas_call(
        joint_kernel,
        out_shape=jax.ShapeDtypeStruct((2, rows, 256), F32),
        in_specs=[smem] * 5
        + [vmem, anywhere, vmem]
        + [anywhere] * 5
        + [vmem, vmem, anywhere, vmem],
        out_specs=vmem,
        scratch_shapes=[
            pltpu.VMEM((rows + 2 * HALO, width), F32),
            pltpu.VMEM((2, 2, rows + 16, quarter), BF16),
            pltpu.VMEM((2, rows + 16, half), BF16),
            pltpu.VMEM((2, rows + 16, LANES), F32),
            pltpu.VMEM((8, 2, 16, LANES), F32),
            pltpu.VMEM((4, quarter, 256), BF16),
            pltpu.VMEM((4, quarter, 256), BF16),
            pltpu.VMEM((4, half, 256), BF16),
            pltpu.VMEM((4, half, 256), BF16),
            pltpu.VMEM((4, 1024, 512), BF16),
            pltpu.VMEM((rows, LANES), BF16),
            pltpu.VMEM((rows, 256), F32),
            pltpu.VMEM((2, 4, rows, 256), F32),
            pltpu.VMEM((2, 2, rows, 256), F32),
            pltpu.VMEM((2, rows, 256), F32),
            pltpu.VMEM((2, 4, 8, 4, 8, LANES), F32),
            pltpu.VMEM((2, 4, 8, 4, 8, LANES), F32),
            pltpu.VMEM((4, 256, LANES), F32),
            pltpu.VMEM((2, 4, 256, LANES), F32),
            pltpu.VMEM((2, 4, 256, LANES), F32),
            dma((4,)),
            dma((3, 2, 4)),
            dma((2,)),
            dma((2,)),
            dma((2, 2, CHUNKS)),
            dma((2, 2, CHUNKS)),
            dma((2, CHUNKS)),
            dma((2, CHUNKS)),
            dma((2, 3, CHUNKS)),
            dma((2, 3, CHUNKS)),
            dma((2, 3)),
            dma((2, 3)),
        ],
        compiler_params=pltpu.CompilerParams(
            collective_id=0, has_side_effects=True, vmem_limit_bytes=56 * 1024 * 1024
        ),
        cost_estimate=pl.CostEstimate(flops=7 * 10**9, bytes_accessed=18 * 2**20, transcendentals=0),
        name="joint",
    )(
        zero_point, noise_var, footprint.T, accept, assign, stamps, block,
        joint_tap_table(ids, width, stamp_len),
        th0, tl0, th1, tl1, joint_column_tables(height), joint_twiddles(), joint_order(ids, width), psf_rows, psf_cols,
    )


def column_tables(height):
    quarter = height // 4
    inner = np.arange(quarter)
    parts = []
    for j in range(4):
        phase = angles(4 * np.arange(quarter) + j, inner, height)
        parts.append(np.concatenate([np.cos(phase), np.sin(phase)], axis=1))
    return split_np(np.stack(parts))


def order_matrix(share):
    size = 2 * share
    table = np.zeros((size, 2 * size), np.float32)
    for part in range(2):
        for parity in range(2):
            for j in range(share // 2):
                source = part * share + parity * (share // 2) + j
                place = 2 * j + parity
                table[source, part * share + place] = 1.0
                table[source, size + (1 - part) * share + place] = -1.0 if part == 0 else 1.0
    return table.astype(ml_dtypes.bfloat16)


def column_kernel(x, order, th, tl, out):
    height, lanes = x.shape
    quarter = height // 4
    step = pl.program_id(0)
    for j in range(4):

        @pl.when(step == j)
        def _(j=j):
            parts = []
            for f in range(4):
                hi, lo = split(x[f * quarter : (f + 1) * quarter])
                parts.append(dot(hi, order[...]) + dot(lo, order[...]))
            if j % 2 == 0:
                even, odd = parts[0] + parts[2], parts[1] + parts[3]
                mix = even + odd if j == 0 else even - odd
                top, low = mix[:, :lanes], mix[:, lanes:]
            else:
                even, odd = parts[0] - parts[2], parts[1] - parts[3]
                sign = 1.0 if j == 1 else -1.0
                top = even[:, :lanes] + sign * odd[:, lanes:]
                low = even[:, lanes:] - sign * odd[:, :lanes]
            both = jnp.concatenate([top, low], axis=0)
            hi, lo = split(both)
            wide = dot(th[0], jnp.concatenate([hi, lo], axis=1))
            result = wide[:, :lanes] + wide[:, lanes:] + dot(tl[0], hi)
            out[pl.ds(j, quarter, stride=4), :] = result


def columns(x, order, tables):
    height, lanes = x.shape
    quarter = height // 4
    table_spec = pl.BlockSpec((1, quarter, 2 * quarter), lambda j: (j, 0, 0))
    return pl.pallas_call(
        column_kernel,
        grid=(4,),
        out_shape=jax.ShapeDtypeStruct((height, lanes), F32),
        in_specs=[
            pl.BlockSpec((height, lanes), lambda j: (0, 0)),
            pl.BlockSpec((lanes, 2 * lanes), lambda j: (0, 0)),
            table_spec,
            table_spec,
        ],
        out_specs=pl.BlockSpec((height, lanes), lambda j: (0, 0)),
        compiler_params=pltpu.CompilerParams(vmem_limit_bytes=48 * 1024 * 1024),
        name="columns",
    )(x, order, *tables)


def denom_kernel(weight, rows, cols, out):
    count = cols.shape[0]
    lanes = out.shape[1]
    total = jnp.zeros(out.shape, F32)
    rh, rl = split(rows[...])
    for e in range(count):
        chh, cll = split(cols[e])
        psf = dot(rh, chh) + dot(rh, cll) + dot(rl, chh)
        total = total + weight[e] * (psf[:, :lanes] * psf[:, :lanes] + psf[:, lanes:] * psf[:, lanes:])
    out[...] = lax.rsqrt(total)


def per_device(exposures, stamps, zero_point, noise_var, footprint, accept, assign):
    exp_dev, rows_dev, width = exposures.shape
    freqs = lax.axis_size("freq")
    readers = lax.axis_size(READERS)
    height = rows_dev * freqs
    per_freq = width // 2 // freqs
    share = per_freq // readers
    out_rows = height // readers
    stamp_len = stamps.shape[1]
    count_all = assign.shape[0]
    freq_at = lax.axis_index("freq")
    reader_at = lax.axis_index(READERS)
    sizes = (lax.axis_size("read"), lax.axis_size("pair"), freqs)
    if sizes == (2, 2, 4) and (rows_dev, width, stamp_len, count_all) == (512, 2048, 16, 4):
        return joint(exposures[0], stamps, zero_point, noise_var, footprint, accept, assign)
    ids = column_order(width, freqs, readers)
    tiles = ids.shape[1]
    offsets = np.arange(stamp_len) - stamp_len // 2

    block = exposures[0]
    forward = [(i, (i + 1) % freqs) for i in range(freqs)]
    backward = [(t, s) for s, t in forward]
    low = lax.ppermute(block[rows_dev - HALO :], "freq", forward)
    high = lax.ppermute(block[:HALO], "freq", backward)

    labels = jnp.arange(count_all, dtype=jnp.int32)
    owner = jnp.sum(jnp.where(labels == reader_at, assign, 0))
    chosen = labels == owner
    low_row = jnp.sum(jnp.where(chosen, footprint[:, 0], 0))
    high_row = jnp.sum(jnp.where(chosen, footprint[:, 1], 0))
    accepted = accept.astype(F32)
    numer_weight = accepted * zero_point / noise_var
    denom_weight = accepted * zero_point * zero_point / noise_var
    scale = 1.0 / math.sqrt(height * width)
    weight = jnp.sum(jnp.where(chosen, numer_weight, 0.0)) * scale
    stamp = jnp.sum(jnp.where(chosen[:, None, None], stamps, 0.0), axis=0) * weight
    tap_phase = angles(offsets, ids.reshape(-1), width)
    tap_table = np.stack([np.cos(tap_phase), -np.sin(tap_phase)]).astype(np.float32)
    taps = jnp.einsum("ab,cbp->cap", stamp, tap_table, precision=HIGHEST)
    taps = taps.reshape(2, stamp_len, 2, tiles, TILE).transpose(3, 2, 0, 1, 4)
    info = jnp.stack([freq_at * rows_dev, low_row, high_row, jnp.int32(height)]).astype(jnp.int32)

    tables = row_tables(ids, width)
    terms = front(info, low, block, high, taps, tables)
    if tiles != readers:
        terms = terms.reshape(tiles, rows_dev, 2, 2, readers // tiles, TILE * tiles // readers)
        terms = terms.transpose(0, 4, 1, 2, 3, 5).reshape(readers, rows_dev, -1)
    summed = lax.psum_scatter(terms, READERS, scatter_dimension=0, tiled=True)
    summed = summed.reshape(rows_dev, 2, 2, freqs, share // 2)
    summed = summed.transpose(3, 0, 2, 1, 4).reshape(freqs, rows_dev, 2 * share)
    gathered = lax.all_to_all(summed, "freq", split_axis=0, concat_axis=0, tiled=True)
    grid = columns(gathered.reshape(height, 2 * share), order_matrix(share), column_tables(height))
    grid = lax.all_to_all(
        grid.reshape(readers, out_rows, 2 * share), READERS, split_axis=0, concat_axis=0, tiled=True
    )
    numer = grid.reshape(readers, out_rows, 2, share).transpose(2, 1, 0, 3)
    numer = numer.reshape(2, out_rows, per_freq)

    all_u = angles(np.arange(height), offsets, height)
    all_rows = np.concatenate([np.cos(all_u), np.sin(all_u)], axis=1).astype(np.float32)
    psf_rows = lax.dynamic_slice_in_dim(jnp.asarray(all_rows), reader_at * out_rows, out_rows, 0)
    all_v = angles(offsets, np.arange(width // 2), width)
    all_cols = np.stack([np.cos(all_v), -np.sin(all_v)]).astype(np.float32)
    own_cols = lax.dynamic_slice_in_dim(jnp.asarray(all_cols), freq_at * per_freq, per_freq, 2)
    q = jnp.einsum("nab,cbp->cnap", stamps, own_cols, precision=HIGHEST)
    psf_cols = jnp.concatenate(
        [jnp.concatenate([q[0], q[1]], axis=2), jnp.concatenate([q[1], -q[0]], axis=2)], axis=1
    )
    inverse = pl.pallas_call(
        denom_kernel,
        out_shape=jax.ShapeDtypeStruct((out_rows, per_freq), F32),
        in_specs=[
            pl.BlockSpec(memory_space=pltpu.SMEM),
            pl.BlockSpec(memory_space=pltpu.VMEM),
            pl.BlockSpec(memory_space=pltpu.VMEM),
        ],
        out_specs=pl.BlockSpec(memory_space=pltpu.VMEM),
        compiler_params=pltpu.CompilerParams(vmem_limit_bytes=32 * 1024 * 1024),
        name="denom",
    )(denom_weight, psf_rows, psf_cols)
    return numer * inverse


def solution(mesh):
    in_specs = (
        P(("groups", "read", "pair"), "freq", None),
        P("groups", None, None),
        P("groups"),
        P("groups"),
        P("groups", None),
        P("groups"),
        P("groups"),
    )
    out_specs = P(None, ("groups", "read", "pair"), "freq")
    return jax.shard_map(
        per_device, mesh=mesh, in_specs=in_specs, out_specs=out_specs, check_vma=False
    )
```

```python
import functools
import math

import jax
import jax.numpy as jnp
import ml_dtypes
import numpy as np
from jax import lax
from jax.experimental import pallas as pl
from jax.experimental.pallas import tpu as pltpu
from jax.sharding import PartitionSpec as P

HIGHEST = lax.Precision.HIGHEST
TWO_PI = 2.0 * math.pi
HALO = 16
TILE = 128
BF16 = jnp.bfloat16
F32 = jnp.float32
READERS = ("read", "pair")


def split_np(table):
    hi = table.astype(np.float32).astype(ml_dtypes.bfloat16)
    lo = (table - hi.astype(np.float64)).astype(np.float32).astype(ml_dtypes.bfloat16)
    return hi, lo


def split(value):
    hi = value.astype(BF16)
    return hi, (value - hi.astype(F32)).astype(BF16)


def angles(left, right, modulus):
    return (np.outer(left, right) % modulus).astype(np.float64) * (TWO_PI / modulus)


def dot(left, right):
    return jnp.dot(left, right, preferred_element_type=F32)


def column_order(width, freqs, readers):
    share = width // 2 // freqs // readers
    parity = np.arange(2)[:, None, None, None]
    reader = np.arange(readers)[None, :, None, None]
    freq = np.arange(freqs)[None, None, :, None]
    inner = np.arange(share // 2)[None, None, None, :]
    ids = freq * (share * readers) + reader * share + 2 * inner + parity
    return ids.reshape(2, -1, TILE)


def row_tables(ids, width):
    half = np.arange(width // 2)
    parts = []
    for tile in range(ids.shape[1]):
        both = []
        for parity in range(2):
            phase = angles(half, ids[parity, tile], width)
            both.append(np.concatenate([np.cos(phase), -np.sin(phase)], axis=1))
        parts.append(np.stack(both))
    return split_np(np.stack(parts))


def front_kernel(info, low, block, high, taps, th, tl, out, ext, ch, cl, grid):
    rows, width = block.shape
    half = width // 2
    height = info[3]

    @pl.when(pl.program_id(0) == 0)
    def _():
        ext[:HALO] = low[...]
        ext[HALO : HALO + rows] = block[...]
        ext[HALO + rows :] = high[...]
        cols = lax.broadcasted_iota(jnp.int32, (16, width), 1)

        def clean(i, carry):
            at = pl.multiple_of(i * 16, 16)
            piece = ext[pl.ds(at, 32), :]
            mid = piece[8:24]
            ids = info[0] - 8 + at + lax.broadcasted_iota(jnp.int32, (16, 1), 0)
            ids = jnp.where(ids < 0, ids + height, ids)
            ids = jnp.where(ids >= height, ids - height, ids)
            up = jnp.where(ids == 0, 0.0, piece[7:23])
            down = jnp.where(ids == height - 1, 0.0, piece[9:25])
            left = jnp.where(cols == 0, 0.0, pltpu.roll(mid, 1, 1))
            right = jnp.where(cols == width - 1, 0.0, pltpu.roll(mid, width - 1, 1))
            inside = (ids >= info[1]) & (ids < info[2])
            cell = jnp.where(inside, mid - 0.25 * (up + down + left + right), 0.0)
            for parity in range(2):
                if parity == 0:
                    fold = cell[:, :half] + cell[:, half:]
                else:
                    fold = cell[:, :half] - cell[:, half:]
                hi, lo = split(fold)
                ch[parity, pl.ds(at, 16), :] = hi
                cl[parity, pl.ds(at, 16), :] = lo
            return carry

        lax.fori_loop(0, (rows + 16) // 16, clean, 0)

    for parity in range(2):
        grid[parity] = (
            dot(ch[parity], th[0, parity])
            + dot(ch[parity], tl[0, parity])
            + dot(cl[parity], th[0, parity])
        )

    def fir(i, carry):
        at = pl.multiple_of(i * 32, 32)
        for parity in range(2):
            re = grid[parity, pl.ds(at, 48), :TILE]
            im = grid[parity, pl.ds(at, 48), TILE:]
            sum_re = jnp.zeros((32, TILE), F32)
            sum_im = jnp.zeros((32, TILE), F32)
            for k in range(8):
                shift_re = re[k : k + 40]
                shift_im = im[k : k + 40]
                for a in (k, k + 8):
                    qr = taps[0, parity, 0, a : a + 1, :]
                    qi = taps[0, parity, 1, a : a + 1, :]
                    xr = shift_re[a - k : a - k + 32]
                    xi = shift_im[a - k : a - k + 32]
                    sum_re = sum_re + (qr * xr + qi * xi)
                    sum_im = sum_im + (qr * xi - qi * xr)
            lane = parity * 2 * TILE
            out[0, pl.ds(at, 32), lane : lane + TILE] = sum_re
            out[0, pl.ds(at, 32), lane + TILE : lane + 2 * TILE] = sum_im
        return carry

    lax.fori_loop(0, rows // 32, fir, 0)


def front(info, low, block, high, taps, tables):
    rows, width = block.shape
    tiles = tables[0].shape[0]
    whole = lambda shape: pl.BlockSpec(shape, lambda t: (0,) * len(shape))
    table_spec = pl.BlockSpec((1, 2, width // 2, 2 * TILE), lambda t: (t, 0, 0, 0))
    return pl.pallas_call(
        front_kernel,
        grid=(tiles,),
        out_shape=jax.ShapeDtypeStruct((tiles, rows, 4 * TILE), F32),
        in_specs=[
            pl.BlockSpec(memory_space=pltpu.SMEM),
            whole((HALO, width)),
            whole((rows, width)),
            whole((HALO, width)),
            pl.BlockSpec((1, 2, 2, taps.shape[3], TILE), lambda t: (t, 0, 0, 0, 0)),
            table_spec,
            table_spec,
        ],
        out_specs=pl.BlockSpec((1, rows, 4 * TILE), lambda t: (t, 0, 0)),
        scratch_shapes=[
            pltpu.VMEM((rows + 2 * HALO, width), F32),
            pltpu.VMEM((2, rows + 16, width // 2), BF16),
            pltpu.VMEM((2, rows + 16, width // 2), BF16),
            pltpu.VMEM((2, rows + 16, 2 * TILE), F32),
        ],
        compiler_params=pltpu.CompilerParams(vmem_limit_bytes=48 * 1024 * 1024),
        name="front",
    )(info, low, block, high, taps, *tables)


MESH = pl.DeviceIdType.MESH
CHUNKS = 4
LANES = 128


def joint_columns(width):
    per_freq = width // 2 // 4
    freq = np.arange(4)[:, None] * per_freq
    inner = np.arange(32)[None, :]
    groups = []
    for k in range(2):
        for rd in range(2):
            for pd in range(2):
                if k == 0:
                    ids = freq + 4 * (32 * rd + inner) + 2 * pd
                else:
                    ids = freq + 64 * (2 * rd + pd) + 2 * inner + 1
                groups.append(ids.reshape(-1))
    return np.stack(groups)


def joint_row_tables(ids, width):
    even, odd = [], []
    for t in range(8):
        depth = width // 4 if t < 4 else width // 2
        phase = angles(np.arange(depth), ids[t], width)
        table = np.concatenate([np.cos(phase), -np.sin(phase)], axis=1)
        (even if t < 4 else odd).append(table)
    return split_np(np.stack(even)) + split_np(np.stack(odd))


def joint_column_tables(height):
    inner = np.arange(256)
    parts = []
    for g in range(8):
        phase = angles(np.arange(256), 8 * inner + g, height)
        parts.append(np.concatenate([np.cos(phase), np.sin(phase)], axis=1))
    tables = np.stack(split_np(np.stack(parts).reshape(2, 4, 256, 512)))
    return tables.transpose(2, 0, 1, 3, 4).reshape(4, 1024, 512)


def joint_twiddles():
    lane = np.arange(LANES)
    table = np.zeros((4, 8, LANES), np.float32)
    for gg in range(4):
        angle = np.where(lane >= 64, TWO_PI * gg / 8, 0.0)
        real = lane % 64 < 32
        table[gg, 0] = np.cos(angle)
        table[gg, 1] = np.where(real, np.sin(angle), 0.0)
        table[gg, 2] = np.where(real, 0.0, -np.sin(angle))
        table[gg, 3] = np.where(lane < 64, 1.0, -1.0)
    return table


def joint_order(ids, width):
    per_freq = width // 2 // 4
    table = np.zeros((256, 256), np.float32)
    for k in range(2):
        for reader in range(4):
            for i in range(32):
                table[k * LANES + reader * 32 + i, ids[4 * k + reader, i] % per_freq] = 1.0
    return table.astype(ml_dtypes.bfloat16)


def joint_psf_tables(height, width, stamp_len):
    offsets = np.arange(stamp_len) - stamp_len // 2
    all_u = angles(np.arange(height), offsets, height)
    hi, lo = split_np(np.concatenate([np.cos(all_u), np.sin(all_u)], axis=1))
    rows = np.concatenate([hi, lo, hi, np.zeros_like(hi)], axis=1).reshape(4, height // 4, LANES)
    all_v = angles(offsets, np.arange(width // 2), width).reshape(stamp_len, 4, -1)
    cols = np.concatenate([np.cos(all_v), -np.sin(all_v)], axis=2).astype(np.float32)
    return rows, cols.transpose(1, 0, 2)


def joint_tap_table(ids, width, stamp_len):
    offsets = np.arange(stamp_len) - stamp_len // 2
    phase = [angles(offsets, ids[t], width) for t in range(8)]
    return np.concatenate(
        [np.concatenate([np.cos(x), -np.sin(x)], axis=1) for x in phase], axis=1
    ).astype(np.float32)


def turn(quads, lanes):
    low = lanes < 64
    first = [None] * 4
    for q in range(2):
        first[q] = jnp.where(low, quads[q], pltpu.roll(quads[q + 2], 64, 1))
        first[q + 2] = jnp.where(low, pltpu.roll(quads[q], 64, 1), quads[q + 2])
    even = lanes % 64 < 32
    result = [None] * 4
    for q in (0, 2):
        result[q] = jnp.where(even, first[q], pltpu.roll(first[q + 1], 32, 1))
        result[q + 1] = jnp.where(even, pltpu.roll(first[q], 96, 1), first[q + 1])
    return result


def joint_kernel(
    zero_point, noise_var, footprint, accept, assign, stamps, block, tap_table,
    th0, tl0, th1, tl1, ctab, twiddle, order, psf_rows, psf_cols, out,
    ext, even, odd, grid, taps,
    bh0, bl0, bh1, bl1, col_tab, prow, inverse,
    work, pair_in, read_in, freq_out, freq_in, mixed, col_out, col_in,
    block_sem, table_sem, halo_send, halo_recv, pair_send, pair_recv,
    read_send, read_recv, freq_send, freq_recv, col_send, col_recv,
):
    rows, width = block.shape
    freqs = 4
    height = rows * freqs
    quarter = width // 4
    half = width // 2
    r = lax.axis_index("read")
    p = lax.axis_index("pair")
    f = lax.axis_index("freq")
    me = 2 * r + p

    def group_at(s):
        rd = jnp.where(s < 2, 1 - r, r)
        pd = jnp.where(s % 2 == 0, 1 - p, p)
        return rd * 2 + pd

    def block_copy(n):
        size = rows // 4
        return pltpu.make_async_copy(
            block.at[pl.ds(n * size, size)], ext.at[pl.ds(HALO + n * size, size)], block_sem.at[n]
        )

    def row_table_copies(k, s):
        t = group_at(s)
        pairs = ((th0, bh0), (tl0, bl0)) if k == 0 else ((th1, bh1), (tl1, bl1))
        return [
            pltpu.make_async_copy(a.at[t], b.at[s], table_sem.at[k, n, s])
            for n, (a, b) in enumerate(pairs)
        ]

    def column_table_copy():
        return pltpu.make_async_copy(ctab, col_tab, table_sem.at[2, 0, 0])

    def psf_copy():
        return pltpu.make_async_copy(psf_rows.at[me], prow, table_sem.at[2, 0, 2])

    def halo_copies():
        up = lax.rem(f + 1, freqs)
        down = lax.rem(f + freqs - 1, freqs)
        return (
            pltpu.make_async_remote_copy(
                src_ref=block.at[pl.ds(rows - HALO, HALO)], dst_ref=ext.at[pl.ds(0, HALO)],
                send_sem=halo_send.at[0], recv_sem=halo_recv.at[0],
                device_id={"freq": up}, device_id_type=MESH,
            ),
            pltpu.make_async_remote_copy(
                src_ref=block.at[pl.ds(0, HALO)], dst_ref=ext.at[pl.ds(HALO + rows, HALO)],
                send_sem=halo_send.at[1], recv_sem=halo_recv.at[1],
                device_id={"freq": down}, device_id_type=MESH,
            ),
        )

    chunk = rows // CHUNKS

    def pair_copy(k, n, c):
        part = pl.ds(pl.multiple_of(c * chunk, chunk), chunk)
        return pltpu.make_async_remote_copy(
            src_ref=work.at[k, 2 * n, part], dst_ref=pair_in.at[k, n, part],
            send_sem=pair_send.at[k, n, c], recv_sem=pair_recv.at[k, n, c],
            device_id={"pair": 1 - p}, device_id_type=MESH,
        )

    def read_copy(k, c):
        part = pl.ds(pl.multiple_of(c * chunk, chunk), chunk)
        return pltpu.make_async_remote_copy(
            src_ref=work.at[k, 1, part], dst_ref=read_in.at[k, part],
            send_sem=read_send.at[k, c], recv_sem=read_recv.at[k, c],
            device_id={"read": 1 - r}, device_id_type=MESH,
        )

    def freq_copy(k, d, c):
        part = pl.ds(2 * c, 2)
        to = lax.rem(f + d, freqs)
        return pltpu.make_async_remote_copy(
            src_ref=freq_out.at[k, to, part], dst_ref=freq_in.at[k, f, part],
            send_sem=freq_send.at[k, d - 1, c], recv_sem=freq_recv.at[k, d - 1, c],
            device_id={"freq": to}, device_id_type=MESH,
        )

    def col_copy(k, n):
        rd = jnp.where(n > 0, 1 - r, r)
        pd = jnp.where(n == 1, p, 1 - p)
        return pltpu.make_async_remote_copy(
            src_ref=col_out.at[k, 2 * rd + pd], dst_ref=col_in.at[k, me],
            send_sem=col_send.at[k, n], recv_sem=col_recv.at[k, n],
            device_id={"read": rd, "pair": pd}, device_id_type=MESH,
        )

    barrier = pltpu.get_barrier_semaphore()
    for d in range(1, freqs):
        pl.semaphore_signal(
            barrier, inc=1, device_id={"freq": lax.rem(f + d, freqs)}, device_id_type=MESH
        )
    for rd, pd in ((r, 1 - p), (1 - r, p), (1 - r, 1 - p)):
        pl.semaphore_signal(
            barrier, inc=1, device_id={"read": rd, "pair": pd}, device_id_type=MESH
        )
    for n in range(4):
        block_copy(n).start()
    for s in range(2):
        for copy in row_table_copies(0, s):
            copy.start()

    mine = assign[me]
    first_row = footprint[0, mine]
    last_row = footprint[1, mine]
    scale = 1.0 / math.sqrt(height * width)
    top = accept[mine].astype(F32) * zero_point[mine] * scale
    side = stamps.shape[1]
    stamp = stamps[mine] * (jnp.full((side, side), top, F32) / jnp.full((side, side), noise_var[mine], F32))
    every = jnp.dot(stamp, tap_table[...], precision=HIGHEST, preferred_element_type=F32)
    for t in range(8):
        for n in range(2):
            taps[t, n] = every[:, (2 * t + n) * LANES : (2 * t + n + 1) * LANES]

    pl.semaphore_wait(barrier, freqs + 2)
    for copy in halo_copies():
        copy.start()

    edge = lax.broadcasted_iota(jnp.int32, (16, LANES), 1)
    last_lane = width - LANES

    def clean_at(at, rim):
        piece = ext[pl.ds(at, 32), :]
        mid = piece[8:24]
        ids = f * rows - 8 + at + lax.broadcasted_iota(jnp.int32, (16, 1), 0)
        up, down = piece[7:23], piece[9:25]
        if rim:
            ids = jnp.where(ids < 0, ids + height, ids)
            ids = jnp.where(ids >= height, ids - height, ids)
            up = jnp.where(ids == 0, 0.0, up)
            down = jnp.where(ids == height - 1, 0.0, down)
        left = pltpu.roll(mid, 1, 1)
        left = jnp.concatenate(
            [jnp.where(edge == 0, 0.0, left[:, :LANES]), left[:, LANES:]], axis=1
        )
        right = pltpu.roll(mid, width - 1, 1)
        right = jnp.concatenate(
            [right[:, :last_lane], jnp.where(edge == LANES - 1, 0.0, right[:, last_lane:])], axis=1
        )
        inside = (ids >= first_row) & (ids < last_row)
        cell = jnp.where(inside, mid - 0.25 * (up + down + left + right), 0.0)
        total = cell[:, :half] + cell[:, half:]
        here = pl.ds(at, 16)
        odd[0, here, :], odd[1, here, :] = split(cell[:, :half] - cell[:, half:])
        even[0, 0, here, :], even[0, 1, here, :] = split(total[:, :quarter] + total[:, quarter:])
        even[1, 0, here, :], even[1, 1, here, :] = split(total[:, :quarter] - total[:, quarter:])

    for n in range(4):
        block_copy(n).wait()
    for s in range(2, 4):
        for copy in row_table_copies(0, s):
            copy.start()
    for s in range(4):
        for copy in row_table_copies(1, s):
            copy.start()
    column_table_copy().start()
    psf_copy().start()

    lanes = lax.broadcasted_iota(jnp.int32, (32, LANES), 1)

    def pack(k, c):
        pair_copy(k, 1, c).wait_recv()

        def body(n, carry):
            b = 2 * c + n
            quads = []
            for g in range(2):
                here = pl.ds(pl.multiple_of(b * 64 + g * 32, 32), 32)
                total = work[k, 3, here, :] + pair_in[k, 1, here, :] + read_in[k, here, :]
                quads += [total[:, :LANES], total[:, LANES:]]
            for to, value in enumerate(turn(quads, lanes)):
                freq_out[k, to, b] = value.reshape(4, 8, LANES)
            return carry

        lax.fori_loop(0, 2, body, 0)
        for d in range(1, freqs):
            freq_copy(k, d, c).start()

    def wait_tables(k, s):
        for copy in row_table_copies(k, s):
            copy.wait()

    def store_grid(xh, xl, wh, wl):
        both = dot(xh, wh) + dot(xh, wl) + dot(xl, wh)
        grid[0] = both[:, :LANES]
        grid[1] = both[:, LANES:]

    def multiply(k, s):
        @pl.when(k == 0)
        def _():
            wait_tables(0, s)
            kind = group_at(s) % 2
            store_grid(even[kind, 0], even[kind, 1], bh0[s], bl0[s])

        @pl.when(k == 1)
        def _():
            wait_tables(1, s)
            store_grid(odd[0], odd[1], bh1[s], bl1[s])

    def fir(k, s, c):
        t = 4 * k + group_at(s)
        for n in range(2):
            at = pl.multiple_of(c * chunk + n * 64, 64)
            sums = [[jnp.zeros((8, LANES), F32), jnp.zeros((8, LANES), F32)] for _ in range(8)]
            for a in range(16):
                qr = taps[t, 0, a : a + 1, :]
                qi = taps[t, 1, a : a + 1, :]
                for g in range(8):
                    here = pl.ds(at + g + a, 8, stride=8)
                    xr = grid[0, here, :]
                    xi = grid[1, here, :]
                    sums[g][0] = sums[g][0] + (qr * xr + qi * xi)
                    sums[g][1] = sums[g][1] + (qr * xi - qi * xr)
            for g in range(8):
                work[k, s, pl.ds(at + 8 * g, 8), :LANES] = sums[g][0]
                work[k, s, pl.ds(at + 8 * g, 8), LANES:] = sums[g][1]

    def sum_pair(k, c):
        pair_copy(k, 0, c).wait_recv()
        part = pl.ds(pl.multiple_of(c * chunk, chunk), chunk)
        work[k, 1, part, :] = work[k, 1, part, :] + pair_in[k, 0, part, :]

    def group(n, carry):
        k, s = n // 4, n % 4
        multiply(k, s)

        def body(c, inner):
            fir(k, s, c)

            @pl.when(s % 2 == 0)
            def _():
                pair_copy(k, s // 2, c).start()

            @pl.when(s == 1)
            def _():
                sum_pair(k, c)

                @pl.when(c < 2)
                def _():
                    read_copy(k, c).start()

            return inner

        lax.fori_loop(0, CHUNKS, body, 0)

        @pl.when(n == 2)
        def _():
            read_copy(0, 2).wait_recv()
            read_copy(0, 0).start()

        @pl.when((n == 5) | (n == 6))
        def _():
            read_copy(0, lax.rem(n + 2, 4)).wait_recv()

        @pl.when((n == 5) | (n == 6))
        def _():
            read_copy(1, n - 3).start()

        @pl.when((n > 2) & (n < 7))
        def _():
            pack(0, lax.rem(n + 2, 4))

        return carry

    def times_j(x, at):
        real = at % 64 < 32
        return jnp.where(real, pltpu.roll(x, 96, 1), -pltpu.roll(x, 32, 1))

    def columns(k):
        for d in range(1, freqs):
            for c in range(CHUNKS):
                freq_copy(k, d, c).wait_recv()
        freq_in[k, f] = freq_out[k, f]
        tall = lax.broadcasted_iota(jnp.int32, (256, LANES), 1)

        def residue(gg, carry):
            x = freq_in[k, :, :, gg].reshape(256, LANES)
            hi, lo = split(jnp.concatenate([x, times_j(x, tall)], axis=0))
            res = dot(col_tab[gg], jnp.concatenate([hi, lo], axis=1))
            sides = [
                res[n : n + 256, :LANES] + res[n : n + 256, LANES:] + res[n + 512 : n + 768, :LANES]
                for n in (0, 256)
            ]
            both = jnp.where(tall < 64, sides[0], sides[1])
            both = pltpu.roll(both, 64, 1) + both * twiddle[gg, 3:4, :]
            mixed[gg] = (
                both * twiddle[gg, 0:1, :]
                + pltpu.roll(both, 96, 1) * twiddle[gg, 1:2, :]
                + pltpu.roll(both, 32, 1) * twiddle[gg, 2:3, :]
            )
            return carry

        lax.fori_loop(0, 4, residue, 0, unroll=True)

        def last(i, carry):
            here = pl.ds(pl.multiple_of(i * 32, 32), 32)
            e = [mixed[gg, here, :] for gg in range(4)]
            a, b = e[0] + e[2], e[1] + e[3]
            c, d = e[0] - e[2], times_j(e[1] - e[3], lanes)
            col_out[k, 0, here, :] = a + b
            col_out[k, 1, here, :] = c + d
            col_out[k, 2, here, :] = a - b
            col_out[k, 3, here, :] = c - d
            return carry

        lax.fori_loop(0, 8, last, 0, unroll=2)

    def denominator():
        psf_copy().wait()
        count = stamps.shape[0]
        sides = []
        weights = []
        for e in range(count):
            q = jnp.dot(stamps[e], psf_cols[f], precision=HIGHEST, preferred_element_type=F32)
            turned = jnp.concatenate([q[:, 256:], -q[:, :256]], axis=1)
            hi, lo = split(jnp.concatenate([q, turned], axis=0))
            sides.append(jnp.concatenate([hi, hi, lo, jnp.zeros_like(hi)], axis=0))
            value = accept[e].astype(F32) * zero_point[e] * zero_point[e]
            weights.append(jnp.full((1, 256), value, F32) / jnp.full((1, 256), noise_var[e], F32))
        for n in range(4):
            here = pl.ds(n * 128, 128)
            total = jnp.zeros((128, 256), F32)
            for e in range(count):
                psf = dot(prow[here, :], sides[e])
                re, im = psf[:, :256], psf[:, 256:]
                total = total + weights[e] * (re * re + im * im)
            inverse[here, :] = lax.rsqrt(total)

    def open_half(i, carry):
        c0 = 1 + 2 * i

        def piece(t, inner):
            at = jnp.where(i == 0, 8 + t, jnp.where(t < 7, 25 + t, t - 6))
            clean_at(pl.multiple_of(at * 16, 16), False)
            return inner

        lax.fori_loop(0, 17 - 3 * i, piece, 0)

        @pl.when(i == 1)
        def _():
            for copy in halo_copies():
                copy.wait_recv()

            def rim(t, inner):
                clean_at(pl.multiple_of(t * rows, rows), True)
                return inner

            lax.fori_loop(0, 2, rim, 0)

        def two(s, inner):
            @pl.when(i == 0)
            def _():
                wait_tables(0, s)

            kind = group_at(s) % 2
            spots = [
                pl.ds(pl.multiple_of(lax.rem(c0 + n, CHUNKS) * chunk, chunk), chunk + 16)
                for n in range(2)
            ]
            xh = jnp.concatenate([even[kind, 0, here, :] for here in spots], axis=0)
            xl = jnp.concatenate([even[kind, 1, here, :] for here in spots], axis=0)
            both = dot(xh, bh0[s]) + dot(xh, bl0[s]) + dot(xl, bh0[s])
            for n, here in enumerate(spots):
                part = both[n * (chunk + 16) : (n + 1) * (chunk + 16)]
                grid[0, here, :] = part[:, :LANES]
                grid[1, here, :] = part[:, LANES:]

            def body(n, inner2):
                c = lax.rem(c0 + n, CHUNKS)
                fir(0, s, c)

                @pl.when(s == 0)
                def _():
                    pair_copy(0, 0, c).start()

                @pl.when(s == 1)
                def _():
                    sum_pair(0, c)

                    @pl.when(i == 0)
                    def _():
                        read_copy(0, c).start()

                return inner2

            lax.fori_loop(0, 2, body, 0)
            return inner

        lax.fori_loop(0, 2, two, 0)
        return carry

    lax.fori_loop(0, 2, open_half, 0)
    read_copy(0, 1).wait_recv()
    read_copy(0, 3).start()
    lax.fori_loop(2, 8, group, 0)

    def receive(c, carry):
        read_copy(1, c).wait_recv()

        @pl.when(c == 3)
        def _():
            col_copy(0, 1).start()
            col_copy(0, 2).start()

        pack(1, c)
        return carry

    column_table_copy().wait()

    def ending(k, carry):
        lax.fori_loop(3 * k, 3 + k, receive, 0)

        @pl.when(k == 1)
        def _():
            denominator()

        columns(k)
        col_copy(k, 0).start()

        @pl.when(k == 1)
        def _():
            col_copy(1, 1).start()
            col_copy(1, 2).start()

        return carry

    lax.fori_loop(0, 2, ending, 0)
    for k in range(2):
        col_in[k, me] = col_out[k, me]
        for n in range(3):
            col_copy(k, n).wait_recv()

    wide = lax.broadcasted_iota(jnp.int32, (64, LANES), 1)

    def finish(i, carry):
        at = pl.multiple_of(i * 64, 64)
        parts = []
        for k in range(2):
            quads = [col_in[k, n, pl.ds(at, 64), :] for n in range(4)]
            parts.append(jnp.concatenate(turn(quads, wide), axis=0))
        hi, lo = split(jnp.concatenate(parts, axis=1))
        result = dot(hi, order[...]) + dot(lo, order[...])
        for q in range(4):
            here = pl.ds(256 * (q // 2) + at, 64)
            out[q % 2, here, :] = result[64 * q : 64 * (q + 1)] * inverse[here, :]
        return carry

    lax.fori_loop(0, 4, finish, 0, unroll=True)

    for copy in halo_copies():
        copy.wait_send()
    for k in range(2):
        for c in range(CHUNKS):
            for n in range(2):
                pair_copy(k, n, c).wait_send()
            read_copy(k, c).wait_send()
            for d in range(1, freqs):
                freq_copy(k, d, c).wait_send()
        for n in range(3):
            col_copy(k, n).wait_send()


def joint(block, stamps, zero_point, noise_var, footprint, accept, assign):
    rows, width = block.shape
    height = 4 * rows
    stamp_len = stamps.shape[1]
    ids = joint_columns(width)
    th0, tl0, th1, tl1 = joint_row_tables(ids, width)
    psf_rows, psf_cols = joint_psf_tables(height, width, stamp_len)
    vmem = pl.BlockSpec(memory_space=pltpu.VMEM)
    smem = pl.BlockSpec(memory_space=pltpu.SMEM)
    anywhere = pl.BlockSpec(memory_space=pltpu.HBM)
    dma = pltpu.SemaphoreType.DMA
    half, quarter = width // 2, width // 4
    return pl.pallas_call(
        joint_kernel,
        out_shape=jax.ShapeDtypeStruct((2, rows, 256), F32),
        in_specs=[smem] * 5
        + [vmem, anywhere, vmem]
        + [anywhere] * 5
        + [vmem, vmem, anywhere, vmem],
        out_specs=vmem,
        scratch_shapes=[
            pltpu.VMEM((rows + 2 * HALO, width), F32),
            pltpu.VMEM((2, 2, rows + 16, quarter), BF16),
            pltpu.VMEM((2, rows + 16, half), BF16),
            pltpu.VMEM((2, rows + 16, LANES), F32),
            pltpu.VMEM((8, 2, 16, LANES), F32),
            pltpu.VMEM((4, quarter, 256), BF16),
            pltpu.VMEM((4, quarter, 256), BF16),
            pltpu.VMEM((4, half, 256), BF16),
            pltpu.VMEM((4, half, 256), BF16),
            pltpu.VMEM((4, 1024, 512), BF16),
            pltpu.VMEM((rows, LANES), BF16),
            pltpu.VMEM((rows, 256), F32),
            pltpu.VMEM((2, 4, rows, 256), F32),
            pltpu.VMEM((2, 2, rows, 256), F32),
            pltpu.VMEM((2, rows, 256), F32),
            pltpu.VMEM((2, 4, 8, 4, 8, LANES), F32),
            pltpu.VMEM((2, 4, 8, 4, 8, LANES), F32),
            pltpu.VMEM((4, 256, LANES), F32),
            pltpu.VMEM((2, 4, 256, LANES), F32),
            pltpu.VMEM((2, 4, 256, LANES), F32),
            dma((4,)),
            dma((3, 2, 4)),
            dma((2,)),
            dma((2,)),
            dma((2, 2, CHUNKS)),
            dma((2, 2, CHUNKS)),
            dma((2, CHUNKS)),
            dma((2, CHUNKS)),
            dma((2, 3, CHUNKS)),
            dma((2, 3, CHUNKS)),
            dma((2, 3)),
            dma((2, 3)),
        ],
        compiler_params=pltpu.CompilerParams(
            collective_id=0, has_side_effects=True, vmem_limit_bytes=56 * 1024 * 1024
        ),
        cost_estimate=pl.CostEstimate(flops=7 * 10**9, bytes_accessed=18 * 2**20, transcendentals=0),
        name="joint",
    )(
        zero_point, noise_var, footprint.T, accept, assign, stamps, block,
        joint_tap_table(ids, width, stamp_len),
        th0, tl0, th1, tl1, joint_column_tables(height), joint_twiddles(), joint_order(ids, width), psf_rows, psf_cols,
    )


def column_tables(height):
    quarter = height // 4
    inner = np.arange(quarter)
    parts = []
    for j in range(4):
        phase = angles(4 * np.arange(quarter) + j, inner, height)
        parts.append(np.concatenate([np.cos(phase), np.sin(phase)], axis=1))
    return split_np(np.stack(parts))


def order_matrix(share):
    size = 2 * share
    table = np.zeros((size, 2 * size), np.float32)
    for part in range(2):
        for parity in range(2):
            for j in range(share // 2):
                source = part * share + parity * (share // 2) + j
                place = 2 * j + parity
                table[source, part * share + place] = 1.0
                table[source, size + (1 - part) * share + place] = -1.0 if part == 0 else 1.0
    return table.astype(ml_dtypes.bfloat16)


def column_kernel(x, order, th, tl, out):
    height, lanes = x.shape
    quarter = height // 4
    step = pl.program_id(0)
    for j in range(4):

        @pl.when(step == j)
        def _(j=j):
            parts = []
            for f in range(4):
                hi, lo = split(x[f * quarter : (f + 1) * quarter])
                parts.append(dot(hi, order[...]) + dot(lo, order[...]))
            if j % 2 == 0:
                even, odd = parts[0] + parts[2], parts[1] + parts[3]
                mix = even + odd if j == 0 else even - odd
                top, low = mix[:, :lanes], mix[:, lanes:]
            else:
                even, odd = parts[0] - parts[2], parts[1] - parts[3]
                sign = 1.0 if j == 1 else -1.0
                top = even[:, :lanes] + sign * odd[:, lanes:]
                low = even[:, lanes:] - sign * odd[:, :lanes]
            both = jnp.concatenate([top, low], axis=0)
            hi, lo = split(both)
            wide = dot(th[0], jnp.concatenate([hi, lo], axis=1))
            result = wide[:, :lanes] + wide[:, lanes:] + dot(tl[0], hi)
            out[pl.ds(j, quarter, stride=4), :] = result


def columns(x, order, tables):
    height, lanes = x.shape
    quarter = height // 4
    table_spec = pl.BlockSpec((1, quarter, 2 * quarter), lambda j: (j, 0, 0))
    return pl.pallas_call(
        column_kernel,
        grid=(4,),
        out_shape=jax.ShapeDtypeStruct((height, lanes), F32),
        in_specs=[
            pl.BlockSpec((height, lanes), lambda j: (0, 0)),
            pl.BlockSpec((lanes, 2 * lanes), lambda j: (0, 0)),
            table_spec,
            table_spec,
        ],
        out_specs=pl.BlockSpec((height, lanes), lambda j: (0, 0)),
        compiler_params=pltpu.CompilerParams(vmem_limit_bytes=48 * 1024 * 1024),
        name="columns",
    )(x, order, *tables)


def denom_kernel(weight, rows, cols, out):
    count = cols.shape[0]
    lanes = out.shape[1]
    total = jnp.zeros(out.shape, F32)
    rh, rl = split(rows[...])
    for e in range(count):
        chh, cll = split(cols[e])
        psf = dot(rh, chh) + dot(rh, cll) + dot(rl, chh)
        total = total + weight[e] * (psf[:, :lanes] * psf[:, :lanes] + psf[:, lanes:] * psf[:, lanes:])
    out[...] = lax.rsqrt(total)


def per_device(exposures, stamps, zero_point, noise_var, footprint, accept, assign):
    exp_dev, rows_dev, width = exposures.shape
    freqs = lax.axis_size("freq")
    readers = lax.axis_size(READERS)
    height = rows_dev * freqs
    per_freq = width // 2 // freqs
    share = per_freq // readers
    out_rows = height // readers
    stamp_len = stamps.shape[1]
    count_all = assign.shape[0]
    freq_at = lax.axis_index("freq")
    reader_at = lax.axis_index(READERS)
    sizes = (lax.axis_size("read"), lax.axis_size("pair"), freqs)
    if sizes == (2, 2, 4) and (rows_dev, width, stamp_len, count_all) == (512, 2048, 16, 4):
        return joint(exposures[0], stamps, zero_point, noise_var, footprint, accept, assign)
    ids = column_order(width, freqs, readers)
    tiles = ids.shape[1]
    offsets = np.arange(stamp_len) - stamp_len // 2

    block = exposures[0]
    forward = [(i, (i + 1) % freqs) for i in range(freqs)]
    backward = [(t, s) for s, t in forward]
    low = lax.ppermute(block[rows_dev - HALO :], "freq", forward)
    high = lax.ppermute(block[:HALO], "freq", backward)

    labels = jnp.arange(count_all, dtype=jnp.int32)
    owner = jnp.sum(jnp.where(labels == reader_at, assign, 0))
    chosen = labels == owner
    low_row = jnp.sum(jnp.where(chosen, footprint[:, 0], 0))
    high_row = jnp.sum(jnp.where(chosen, footprint[:, 1], 0))
    accepted = accept.astype(F32)
    numer_weight = accepted * zero_point / noise_var
    denom_weight = accepted * zero_point * zero_point / noise_var
    scale = 1.0 / math.sqrt(height * width)
    weight = jnp.sum(jnp.where(chosen, numer_weight, 0.0)) * scale
    stamp = jnp.sum(jnp.where(chosen[:, None, None], stamps, 0.0), axis=0) * weight
    tap_phase = angles(offsets, ids.reshape(-1), width)
    tap_table = np.stack([np.cos(tap_phase), -np.sin(tap_phase)]).astype(np.float32)
    taps = jnp.einsum("ab,cbp->cap", stamp, tap_table, precision=HIGHEST)
    taps = taps.reshape(2, stamp_len, 2, tiles, TILE).transpose(3, 2, 0, 1, 4)
    info = jnp.stack([freq_at * rows_dev, low_row, high_row, jnp.int32(height)]).astype(jnp.int32)

    tables = row_tables(ids, width)
    terms = front(info, low, block, high, taps, tables)
    if tiles != readers:
        terms = terms.reshape(tiles, rows_dev, 2, 2, readers // tiles, TILE * tiles // readers)
        terms = terms.transpose(0, 4, 1, 2, 3, 5).reshape(readers, rows_dev, -1)
    summed = lax.psum_scatter(terms, READERS, scatter_dimension=0, tiled=True)
    summed = summed.reshape(rows_dev, 2, 2, freqs, share // 2)
    summed = summed.transpose(3, 0, 2, 1, 4).reshape(freqs, rows_dev, 2 * share)
    gathered = lax.all_to_all(summed, "freq", split_axis=0, concat_axis=0, tiled=True)
    grid = columns(gathered.reshape(height, 2 * share), order_matrix(share), column_tables(height))
    grid = lax.all_to_all(
        grid.reshape(readers, out_rows, 2 * share), READERS, split_axis=0, concat_axis=0, tiled=True
    )
    numer = grid.reshape(readers, out_rows, 2, share).transpose(2, 1, 0, 3)
    numer = numer.reshape(2, out_rows, per_freq)

    all_u = angles(np.arange(height), offsets, height)
    all_rows = np.concatenate([np.cos(all_u), np.sin(all_u)], axis=1).astype(np.float32)
    psf_rows = lax.dynamic_slice_in_dim(jnp.asarray(all_rows), reader_at * out_rows, out_rows, 0)
    all_v = angles(offsets, np.arange(width // 2), width)
    all_cols = np.stack([np.cos(all_v), -np.sin(all_v)]).astype(np.float32)
    own_cols = lax.dynamic_slice_in_dim(jnp.asarray(all_cols), freq_at * per_freq, per_freq, 2)
    q = jnp.einsum("nab,cbp->cnap", stamps, own_cols, precision=HIGHEST)
    psf_cols = jnp.concatenate(
        [jnp.concatenate([q[0], q[1]], axis=2), jnp.concatenate([q[1], -q[0]], axis=2)], axis=1
    )
    inverse = pl.pallas_call(
        denom_kernel,
        out_shape=jax.ShapeDtypeStruct((out_rows, per_freq), F32),
        in_specs=[
            pl.BlockSpec(memory_space=pltpu.SMEM),
            pl.BlockSpec(memory_space=pltpu.VMEM),
            pl.BlockSpec(memory_space=pltpu.VMEM),
        ],
        out_specs=pl.BlockSpec(memory_space=pltpu.VMEM),
        compiler_params=pltpu.CompilerParams(vmem_limit_bytes=32 * 1024 * 1024),
        name="denom",
    )(denom_weight, psf_rows, psf_cols)
    return numer * inverse


def solution(mesh):
    in_specs = (
        P(("groups", "read", "pair"), "freq", None),
        P("groups", None, None),
        P("groups"),
        P("groups"),
        P("groups", None),
        P("groups"),
        P("groups"),
    )
    out_specs = P(None, ("groups", "read", "pair"), "freq")
    return jax.shard_map(
        per_device, mesh=mesh, in_specs=in_specs, out_specs=out_specs, check_vma=False
    )
```

```python
import functools
import math

import jax
import jax.numpy as jnp
import ml_dtypes
import numpy as np
from jax import lax
from jax.experimental import pallas as pl
from jax.experimental.pallas import tpu as pltpu
from jax.sharding import PartitionSpec as P

HIGHEST = lax.Precision.HIGHEST
TWO_PI = 2.0 * math.pi
HALO = 16
TILE = 128
BF16 = jnp.bfloat16
F32 = jnp.float32
READERS = ("read", "pair")


def split_np(table):
    hi = table.astype(np.float32).astype(ml_dtypes.bfloat16)
    lo = (table - hi.astype(np.float64)).astype(np.float32).astype(ml_dtypes.bfloat16)
    return hi, lo


def split(value):
    hi = value.astype(BF16)
    return hi, (value - hi.astype(F32)).astype(BF16)


def angles(left, right, modulus):
    return (np.outer(left, right) % modulus).astype(np.float64) * (TWO_PI / modulus)


def dot(left, right):
    return jnp.dot(left, right, preferred_element_type=F32)


def column_order(width, freqs, readers):
    share = width // 2 // freqs // readers
    parity = np.arange(2)[:, None, None, None]
    reader = np.arange(readers)[None, :, None, None]
    freq = np.arange(freqs)[None, None, :, None]
    inner = np.arange(share // 2)[None, None, None, :]
    ids = freq * (share * readers) + reader * share + 2 * inner + parity
    return ids.reshape(2, -1, TILE)


def row_tables(ids, width):
    half = np.arange(width // 2)
    parts = []
    for tile in range(ids.shape[1]):
        both = []
        for parity in range(2):
            phase = angles(half, ids[parity, tile], width)
            both.append(np.concatenate([np.cos(phase), -np.sin(phase)], axis=1))
        parts.append(np.stack(both))
    return split_np(np.stack(parts))


def front_kernel(info, low, block, high, taps, th, tl, out, ext, ch, cl, grid):
    rows, width = block.shape
    half = width // 2
    height = info[3]

    @pl.when(pl.program_id(0) == 0)
    def _():
        ext[:HALO] = low[...]
        ext[HALO : HALO + rows] = block[...]
        ext[HALO + rows :] = high[...]
        cols = lax.broadcasted_iota(jnp.int32, (16, width), 1)

        def clean(i, carry):
            at = pl.multiple_of(i * 16, 16)
            piece = ext[pl.ds(at, 32), :]
            mid = piece[8:24]
            ids = info[0] - 8 + at + lax.broadcasted_iota(jnp.int32, (16, 1), 0)
            ids = jnp.where(ids < 0, ids + height, ids)
            ids = jnp.where(ids >= height, ids - height, ids)
            up = jnp.where(ids == 0, 0.0, piece[7:23])
            down = jnp.where(ids == height - 1, 0.0, piece[9:25])
            left = jnp.where(cols == 0, 0.0, pltpu.roll(mid, 1, 1))
            right = jnp.where(cols == width - 1, 0.0, pltpu.roll(mid, width - 1, 1))
            inside = (ids >= info[1]) & (ids < info[2])
            cell = jnp.where(inside, mid - 0.25 * (up + down + left + right), 0.0)
            for parity in range(2):
                if parity == 0:
                    fold = cell[:, :half] + cell[:, half:]
                else:
                    fold = cell[:, :half] - cell[:, half:]
                hi, lo = split(fold)
                ch[parity, pl.ds(at, 16), :] = hi
                cl[parity, pl.ds(at, 16), :] = lo
            return carry

        lax.fori_loop(0, (rows + 16) // 16, clean, 0)

    for parity in range(2):
        grid[parity] = (
            dot(ch[parity], th[0, parity])
            + dot(ch[parity], tl[0, parity])
            + dot(cl[parity], th[0, parity])
        )

    def fir(i, carry):
        at = pl.multiple_of(i * 32, 32)
        for parity in range(2):
            re = grid[parity, pl.ds(at, 48), :TILE]
            im = grid[parity, pl.ds(at, 48), TILE:]
            sum_re = jnp.zeros((32, TILE), F32)
            sum_im = jnp.zeros((32, TILE), F32)
            for k in range(8):
                shift_re = re[k : k + 40]
                shift_im = im[k : k + 40]
                for a in (k, k + 8):
                    qr = taps[0, parity, 0, a : a + 1, :]
                    qi = taps[0, parity, 1, a : a + 1, :]
                    xr = shift_re[a - k : a - k + 32]
                    xi = shift_im[a - k : a - k + 32]
                    sum_re = sum_re + (qr * xr + qi * xi)
                    sum_im = sum_im + (qr * xi - qi * xr)
            lane = parity * 2 * TILE
            out[0, pl.ds(at, 32), lane : lane + TILE] = sum_re
            out[0, pl.ds(at, 32), lane + TILE : lane + 2 * TILE] = sum_im
        return carry

    lax.fori_loop(0, rows // 32, fir, 0)


def front(info, low, block, high, taps, tables):
    rows, width = block.shape
    tiles = tables[0].shape[0]
    whole = lambda shape: pl.BlockSpec(shape, lambda t: (0,) * len(shape))
    table_spec = pl.BlockSpec((1, 2, width // 2, 2 * TILE), lambda t: (t, 0, 0, 0))
    return pl.pallas_call(
        front_kernel,
        grid=(tiles,),
        out_shape=jax.ShapeDtypeStruct((tiles, rows, 4 * TILE), F32),
        in_specs=[
            pl.BlockSpec(memory_space=pltpu.SMEM),
            whole((HALO, width)),
            whole((rows, width)),
            whole((HALO, width)),
            pl.BlockSpec((1, 2, 2, taps.shape[3], TILE), lambda t: (t, 0, 0, 0, 0)),
            table_spec,
            table_spec,
        ],
        out_specs=pl.BlockSpec((1, rows, 4 * TILE), lambda t: (t, 0, 0)),
        scratch_shapes=[
            pltpu.VMEM((rows + 2 * HALO, width), F32),
            pltpu.VMEM((2, rows + 16, width // 2), BF16),
            pltpu.VMEM((2, rows + 16, width // 2), BF16),
            pltpu.VMEM((2, rows + 16, 2 * TILE), F32),
        ],
        compiler_params=pltpu.CompilerParams(vmem_limit_bytes=48 * 1024 * 1024),
        name="front",
    )(info, low, block, high, taps, *tables)


MESH = pl.DeviceIdType.MESH
CHUNKS = 4
LANES = 128


def joint_columns(width):
    per_freq = width // 2 // 4
    freq = np.arange(4)[:, None] * per_freq
    inner = np.arange(32)[None, :]
    groups = []
    for k in range(2):
        for rd in range(2):
            for pd in range(2):
                if k == 0:
                    ids = freq + 4 * (32 * rd + inner) + 2 * pd
                else:
                    ids = freq + 64 * (2 * rd + pd) + 2 * inner + 1
                groups.append(ids.reshape(-1))
    return np.stack(groups)


def joint_row_tables(ids, width):
    even, odd = [], []
    for t in range(8):
        depth = width // 4 if t < 4 else width // 2
        phase = angles(np.arange(depth), ids[t], width)
        table = np.concatenate([np.cos(phase), -np.sin(phase)], axis=1)
        (even if t < 4 else odd).append(table)
    return split_np(np.stack(even)) + split_np(np.stack(odd))


def joint_column_tables(height):
    inner = np.arange(256)
    parts = []
    for g in range(8):
        phase = angles(np.arange(256), 8 * inner + g, height)
        parts.append(np.concatenate([np.cos(phase), np.sin(phase)], axis=1))
    tables = np.stack(split_np(np.stack(parts).reshape(2, 4, 256, 512)))
    return tables.transpose(2, 0, 1, 3, 4).reshape(4, 1024, 512)


def joint_twiddles():
    lane = np.arange(LANES)
    table = np.zeros((4, 8, LANES), np.float32)
    for gg in range(4):
        angle = np.where(lane >= 64, TWO_PI * gg / 8, 0.0)
        real = lane % 64 < 32
        table[gg, 0] = np.cos(angle)
        table[gg, 1] = np.where(real, np.sin(angle), 0.0)
        table[gg, 2] = np.where(real, 0.0, -np.sin(angle))
        table[gg, 3] = np.where(lane < 64, 1.0, -1.0)
    return table


def joint_order(ids, width):
    per_freq = width // 2 // 4
    table = np.zeros((256, 256), np.float32)
    for k in range(2):
        for reader in range(4):
            for i in range(32):
                table[k * LANES + reader * 32 + i, ids[4 * k + reader, i] % per_freq] = 1.0
    return table.astype(ml_dtypes.bfloat16)


def joint_psf_tables(height, width, stamp_len):
    offsets = np.arange(stamp_len) - stamp_len // 2
    all_u = angles(np.arange(height), offsets, height)
    hi, lo = split_np(np.concatenate([np.cos(all_u), np.sin(all_u)], axis=1))
    rows = np.concatenate([hi, lo, hi, np.zeros_like(hi)], axis=1).reshape(4, height // 4, LANES)
    all_v = angles(offsets, np.arange(width // 2), width).reshape(stamp_len, 4, -1)
    cols = np.concatenate([np.cos(all_v), -np.sin(all_v)], axis=2).astype(np.float32)
    return rows, cols.transpose(1, 0, 2)


def joint_tap_table(ids, width, stamp_len):
    offsets = np.arange(stamp_len) - stamp_len // 2
    phase = [angles(offsets, ids[t], width) for t in range(8)]
    return np.concatenate(
        [np.concatenate([np.cos(x), -np.sin(x)], axis=1) for x in phase], axis=1
    ).astype(np.float32)


def turn(quads, lanes):
    low = lanes < 64
    first = [None] * 4
    for q in range(2):
        first[q] = jnp.where(low, quads[q], pltpu.roll(quads[q + 2], 64, 1))
        first[q + 2] = jnp.where(low, pltpu.roll(quads[q], 64, 1), quads[q + 2])
    even = lanes % 64 < 32
    result = [None] * 4
    for q in (0, 2):
        result[q] = jnp.where(even, first[q], pltpu.roll(first[q + 1], 32, 1))
        result[q + 1] = jnp.where(even, pltpu.roll(first[q], 96, 1), first[q + 1])
    return result


def joint_kernel(
    zero_point, noise_var, footprint, accept, assign, stamps, block, tap_table,
    th0, tl0, th1, tl1, ctab, twiddle, order, psf_rows, psf_cols, out,
    ext, even, odd, grid, taps,
    bh0, bl0, bh1, bl1, col_tab, prow, inverse,
    work, pair_in, read_in, freq_out, freq_in, mixed, col_out, col_in,
    block_sem, table_sem, halo_send, halo_recv, pair_send, pair_recv,
    read_send, read_recv, freq_send, freq_recv, col_send, col_recv,
):
    rows, width = block.shape
    freqs = 4
    height = rows * freqs
    quarter = width // 4
    half = width // 2
    r = lax.axis_index("read")
    p = lax.axis_index("pair")
    f = lax.axis_index("freq")
    me = 2 * r + p

    def group_at(s):
        rd = jnp.where(s < 2, 1 - r, r)
        pd = jnp.where(s % 2 == 0, 1 - p, p)
        return rd * 2 + pd

    def block_copy(n):
        size = rows // 4
        return pltpu.make_async_copy(
            block.at[pl.ds(n * size, size)], ext.at[pl.ds(HALO + n * size, size)], block_sem.at[n]
        )

    def row_table_copies(k, s):
        t = group_at(s)
        pairs = ((th0, bh0), (tl0, bl0)) if k == 0 else ((th1, bh1), (tl1, bl1))
        return [
            pltpu.make_async_copy(a.at[t], b.at[s], table_sem.at[k, n, s])
            for n, (a, b) in enumerate(pairs)
        ]

    def column_table_copy():
        return pltpu.make_async_copy(ctab, col_tab, table_sem.at[2, 0, 0])

    def psf_copy():
        return pltpu.make_async_copy(psf_rows.at[me], prow, table_sem.at[2, 0, 2])

    def halo_copies():
        up = lax.rem(f + 1, freqs)
        down = lax.rem(f + freqs - 1, freqs)
        return (
            pltpu.make_async_remote_copy(
                src_ref=block.at[pl.ds(rows - HALO, HALO)], dst_ref=ext.at[pl.ds(0, HALO)],
                send_sem=halo_send.at[0], recv_sem=halo_recv.at[0],
                device_id={"freq": up}, device_id_type=MESH,
            ),
            pltpu.make_async_remote_copy(
                src_ref=block.at[pl.ds(0, HALO)], dst_ref=ext.at[pl.ds(HALO + rows, HALO)],
                send_sem=halo_send.at[1], recv_sem=halo_recv.at[1],
                device_id={"freq": down}, device_id_type=MESH,
            ),
        )

    chunk = rows // CHUNKS

    def pair_copy(k, n, c):
        part = pl.ds(pl.multiple_of(c * chunk, chunk), chunk)
        return pltpu.make_async_remote_copy(
            src_ref=work.at[k, 2 * n, part], dst_ref=pair_in.at[k, n, part],
            send_sem=pair_send.at[k, n, c], recv_sem=pair_recv.at[k, n, c],
            device_id={"pair": 1 - p}, device_id_type=MESH,
        )

    def read_copy(k, c):
        part = pl.ds(pl.multiple_of(c * chunk, chunk), chunk)
        return pltpu.make_async_remote_copy(
            src_ref=work.at[k, 1, part], dst_ref=read_in.at[k, part],
            send_sem=read_send.at[k, c], recv_sem=read_recv.at[k, c],
            device_id={"read": 1 - r}, device_id_type=MESH,
        )

    def freq_copy(k, d, c):
        part = pl.ds(2 * c, 2)
        to = lax.rem(f + d, freqs)
        return pltpu.make_async_remote_copy(
            src_ref=freq_out.at[k, to, part], dst_ref=freq_in.at[k, f, part],
            send_sem=freq_send.at[k, d - 1, c], recv_sem=freq_recv.at[k, d - 1, c],
            device_id={"freq": to}, device_id_type=MESH,
        )

    def col_copy(k, n):
        rd = jnp.where(n > 0, 1 - r, r)
        pd = jnp.where(n == 1, p, 1 - p)
        return pltpu.make_async_remote_copy(
            src_ref=col_out.at[k, 2 * rd + pd], dst_ref=col_in.at[k, me],
            send_sem=col_send.at[k, n], recv_sem=col_recv.at[k, n],
            device_id={"read": rd, "pair": pd}, device_id_type=MESH,
        )

    barrier = pltpu.get_barrier_semaphore()
    for d in range(1, freqs):
        pl.semaphore_signal(
            barrier, inc=1, device_id={"freq": lax.rem(f + d, freqs)}, device_id_type=MESH
        )
    for rd, pd in ((r, 1 - p), (1 - r, p), (1 - r, 1 - p)):
        pl.semaphore_signal(
            barrier, inc=1, device_id={"read": rd, "pair": pd}, device_id_type=MESH
        )
    for n in range(4):
        block_copy(n).start()
    for s in range(2):
        for copy in row_table_copies(0, s):
            copy.start()

    mine = assign[me]
    first_row = footprint[0, mine]
    last_row = footprint[1, mine]
    scale = 1.0 / math.sqrt(height * width)
    top = accept[mine].astype(F32) * zero_point[mine] * scale
    side = stamps.shape[1]
    stamp = stamps[mine] * (jnp.full((side, side), top, F32) / jnp.full((side, side), noise_var[mine], F32))
    every = jnp.dot(stamp, tap_table[...], precision=HIGHEST, preferred_element_type=F32)
    for t in range(8):
        for n in range(2):
            taps[t, n] = every[:, (2 * t + n) * LANES : (2 * t + n + 1) * LANES]

    pl.semaphore_wait(barrier, freqs + 2)
    for copy in halo_copies():
        copy.start()

    edge = lax.broadcasted_iota(jnp.int32, (16, LANES), 1)
    last_lane = width - LANES

    def clean_at(at, rim):
        piece = ext[pl.ds(at, 32), :]
        mid = piece[8:24]
        ids = f * rows - 8 + at + lax.broadcasted_iota(jnp.int32, (16, 1), 0)
        up, down = piece[7:23], piece[9:25]
        if rim:
            ids = jnp.where(ids < 0, ids + height, ids)
            ids = jnp.where(ids >= height, ids - height, ids)
            up = jnp.where(ids == 0, 0.0, up)
            down = jnp.where(ids == height - 1, 0.0, down)
        left = pltpu.roll(mid, 1, 1)
        left = jnp.concatenate(
            [jnp.where(edge == 0, 0.0, left[:, :LANES]), left[:, LANES:]], axis=1
        )
        right = pltpu.roll(mid, width - 1, 1)
        right = jnp.concatenate(
            [right[:, :last_lane], jnp.where(edge == LANES - 1, 0.0, right[:, last_lane:])], axis=1
        )
        inside = (ids >= first_row) & (ids < last_row)
        cell = jnp.where(inside, mid - 0.25 * (up + down + left + right), 0.0)
        total = cell[:, :half] + cell[:, half:]
        here = pl.ds(at, 16)
        odd[0, here, :], odd[1, here, :] = split(cell[:, :half] - cell[:, half:])
        even[0, 0, here, :], even[0, 1, here, :] = split(total[:, :quarter] + total[:, quarter:])
        even[1, 0, here, :], even[1, 1, here, :] = split(total[:, :quarter] - total[:, quarter:])

    for n in range(4):
        block_copy(n).wait()
    for s in range(2, 4):
        for copy in row_table_copies(0, s):
            copy.start()
    for s in range(4):
        for copy in row_table_copies(1, s):
            copy.start()
    column_table_copy().start()
    psf_copy().start()

    lanes = lax.broadcasted_iota(jnp.int32, (32, LANES), 1)

    def pack(k, c):
        pair_copy(k, 1, c).wait_recv()

        def body(n, carry):
            b = 2 * c + n
            quads = []
            for g in range(2):
                here = pl.ds(pl.multiple_of(b * 64 + g * 32, 32), 32)
                total = work[k, 3, here, :] + pair_in[k, 1, here, :] + read_in[k, here, :]
                quads += [total[:, :LANES], total[:, LANES:]]
            for to, value in enumerate(turn(quads, lanes)):
                freq_out[k, to, b] = value.reshape(4, 8, LANES)
            return carry

        lax.fori_loop(0, 2, body, 0)
        for d in range(1, freqs):
            freq_copy(k, d, c).start()

    def wait_tables(k, s):
        for copy in row_table_copies(k, s):
            copy.wait()

    def store_grid(xh, xl, wh, wl):
        both = dot(xh, wh) + dot(xh, wl) + dot(xl, wh)
        grid[0] = both[:, :LANES]
        grid[1] = both[:, LANES:]

    def multiply(k, s):
        @pl.when(k == 0)
        def _():
            wait_tables(0, s)
            kind = group_at(s) % 2
            store_grid(even[kind, 0], even[kind, 1], bh0[s], bl0[s])

        @pl.when(k == 1)
        def _():
            wait_tables(1, s)
            store_grid(odd[0], odd[1], bh1[s], bl1[s])

    def fir(k, s, c):
        t = 4 * k + group_at(s)
        for n in range(2):
            at = pl.multiple_of(c * chunk + n * 64, 64)
            sums = [[jnp.zeros((8, LANES), F32), jnp.zeros((8, LANES), F32)] for _ in range(8)]
            for a in range(16):
                qr = taps[t, 0, a : a + 1, :]
                qi = taps[t, 1, a : a + 1, :]
                for g in range(8):
                    here = pl.ds(at + g + a, 8, stride=8)
                    xr = grid[0, here, :]
                    xi = grid[1, here, :]
                    sums[g][0] = sums[g][0] + (qr * xr + qi * xi)
                    sums[g][1] = sums[g][1] + (qr * xi - qi * xr)
            for g in range(8):
                work[k, s, pl.ds(at + 8 * g, 8), :LANES] = sums[g][0]
                work[k, s, pl.ds(at + 8 * g, 8), LANES:] = sums[g][1]

    def sum_pair(k, c):
        pair_copy(k, 0, c).wait_recv()
        part = pl.ds(pl.multiple_of(c * chunk, chunk), chunk)
        work[k, 1, part, :] = work[k, 1, part, :] + pair_in[k, 0, part, :]

    def group(n, carry):
        k, s = n // 4, n % 4
        multiply(k, s)

        def body(c, inner):
            fir(k, s, c)

            @pl.when(s % 2 == 0)
            def _():
                pair_copy(k, s // 2, c).start()

            @pl.when(s == 1)
            def _():
                sum_pair(k, c)

                @pl.when(c < 2)
                def _():
                    read_copy(k, c).start()

            return inner

        lax.fori_loop(0, CHUNKS, body, 0)

        @pl.when(n == 2)
        def _():
            read_copy(0, 2).wait_recv()
            read_copy(0, 0).start()

        @pl.when((n == 5) | (n == 6))
        def _():
            read_copy(0, lax.rem(n + 2, 4)).wait_recv()

        @pl.when((n == 5) | (n == 6))
        def _():
            read_copy(1, n - 3).start()

        @pl.when((n > 2) & (n < 7))
        def _():
            pack(0, lax.rem(n + 2, 4))

        return carry

    def times_j(x, at):
        real = at % 64 < 32
        return jnp.where(real, pltpu.roll(x, 96, 1), -pltpu.roll(x, 32, 1))

    def columns(k):
        for d in range(1, freqs):
            for c in range(CHUNKS):
                freq_copy(k, d, c).wait_recv()
        freq_in[k, f] = freq_out[k, f]
        tall = lax.broadcasted_iota(jnp.int32, (256, LANES), 1)

        def residue(gg, carry):
            x = freq_in[k, :, :, gg].reshape(256, LANES)
            hi, lo = split(jnp.concatenate([x, times_j(x, tall)], axis=0))
            res = dot(col_tab[gg], jnp.concatenate([hi, lo], axis=1))
            sides = [
                res[n : n + 256, :LANES] + res[n : n + 256, LANES:] + res[n + 512 : n + 768, :LANES]
                for n in (0, 256)
            ]
            both = jnp.where(tall < 64, sides[0], sides[1])
            both = pltpu.roll(both, 64, 1) + both * twiddle[gg, 3:4, :]
            mixed[gg] = (
                both * twiddle[gg, 0:1, :]
                + pltpu.roll(both, 96, 1) * twiddle[gg, 1:2, :]
                + pltpu.roll(both, 32, 1) * twiddle[gg, 2:3, :]
            )
            return carry

        lax.fori_loop(0, 4, residue, 0, unroll=True)

        def last(i, carry):
            here = pl.ds(pl.multiple_of(i * 32, 32), 32)
            e = [mixed[gg, here, :] for gg in range(4)]
            a, b = e[0] + e[2], e[1] + e[3]
            c, d = e[0] - e[2], times_j(e[1] - e[3], lanes)
            col_out[k, 0, here, :] = a + b
            col_out[k, 1, here, :] = c + d
            col_out[k, 2, here, :] = a - b
            col_out[k, 3, here, :] = c - d
            return carry

        lax.fori_loop(0, 8, last, 0, unroll=2)

    def denominator():
        psf_copy().wait()
        count = stamps.shape[0]
        sides = []
        weights = []
        for e in range(count):
            q = jnp.dot(stamps[e], psf_cols[f], precision=HIGHEST, preferred_element_type=F32)
            turned = jnp.concatenate([q[:, 256:], -q[:, :256]], axis=1)
            hi, lo = split(jnp.concatenate([q, turned], axis=0))
            sides.append(jnp.concatenate([hi, hi, lo, jnp.zeros_like(hi)], axis=0))
            value = accept[e].astype(F32) * zero_point[e] * zero_point[e]
            weights.append(jnp.full((1, 256), value, F32) / jnp.full((1, 256), noise_var[e], F32))
        for n in range(4):
            here = pl.ds(n * 128, 128)
            total = jnp.zeros((128, 256), F32)
            for e in range(count):
                psf = dot(prow[here, :], sides[e])
                re, im = psf[:, :256], psf[:, 256:]
                total = total + weights[e] * (re * re + im * im)
            inverse[here, :] = lax.rsqrt(total)

    def open_half(i, carry):
        c0 = 1 + 2 * i

        def piece(t, inner):
            at = jnp.where(i == 0, 8 + t, jnp.where(t < 7, 25 + t, t - 6))
            clean_at(pl.multiple_of(at * 16, 16), False)
            return inner

        lax.fori_loop(0, 17 - 3 * i, piece, 0)

        @pl.when(i == 1)
        def _():
            for copy in halo_copies():
                copy.wait_recv()

            def rim(t, inner):
                clean_at(pl.multiple_of(t * rows, rows), True)
                return inner

            lax.fori_loop(0, 2, rim, 0)

        def two(s, inner):
            @pl.when(i == 0)
            def _():
                wait_tables(0, s)

            kind = group_at(s) % 2
            spots = [
                pl.ds(pl.multiple_of(lax.rem(c0 + n, CHUNKS) * chunk, chunk), chunk + 16)
                for n in range(2)
            ]
            xh = jnp.concatenate([even[kind, 0, here, :] for here in spots], axis=0)
            xl = jnp.concatenate([even[kind, 1, here, :] for here in spots], axis=0)
            both = dot(xh, bh0[s]) + dot(xh, bl0[s]) + dot(xl, bh0[s])
            for n, here in enumerate(spots):
                part = both[n * (chunk + 16) : (n + 1) * (chunk + 16)]
                grid[0, here, :] = part[:, :LANES]
                grid[1, here, :] = part[:, LANES:]

            def body(n, inner2):
                c = lax.rem(c0 + n, CHUNKS)
                fir(0, s, c)

                @pl.when(s == 0)
                def _():
                    pair_copy(0, 0, c).start()

                @pl.when(s == 1)
                def _():
                    sum_pair(0, c)

                    @pl.when(i == 0)
                    def _():
                        read_copy(0, c).start()

                return inner2

            lax.fori_loop(0, 2, body, 0)
            return inner

        lax.fori_loop(0, 2, two, 0)
        return carry

    lax.fori_loop(0, 2, open_half, 0)
    read_copy(0, 1).wait_recv()
    read_copy(0, 3).start()
    lax.fori_loop(2, 8, group, 0)

    def receive(c, carry):
        read_copy(1, c).wait_recv()

        @pl.when(c == 3)
        def _():
            col_copy(0, 1).start()
            col_copy(0, 2).start()

        pack(1, c)
        return carry

    column_table_copy().wait()

    def ending(k, carry):
        lax.fori_loop(3 * k, 3 + k, receive, 0)

        @pl.when(k == 1)
        def _():
            denominator()

        columns(k)
        col_copy(k, 0).start()

        @pl.when(k == 1)
        def _():
            col_copy(1, 1).start()
            col_copy(1, 2).start()

        return carry

    lax.fori_loop(0, 2, ending, 0)
    wide = lax.broadcasted_iota(jnp.int32, (64, LANES), 1)
    for k in range(2):
        col_in[k, me] = col_out[k, me]
        for n in range(3):
            col_copy(k, n).wait_recv()
        place = order[k * LANES : (k + 1) * LANES, :]

        def finish(i, carry, k=k, place=place):
            at = pl.multiple_of(i * 64, 64)
            quads = [col_in[k, n, pl.ds(at, 64), :] for n in range(4)]
            hi, lo = split(jnp.concatenate(turn(quads, wide), axis=0))
            result = dot(hi, place) + dot(lo, place)
            for q in range(4):
                here = pl.ds(256 * (q // 2) + at, 64)
                value = result[64 * q : 64 * (q + 1)]
                if k == 0:
                    out[q % 2, here, :] = value
                else:
                    out[q % 2, here, :] = (out[q % 2, here, :] + value) * inverse[here, :]
            return carry

        lax.fori_loop(0, 4, finish, 0, unroll=True)

    for copy in halo_copies():
        copy.wait_send()
    for k in range(2):
        for c in range(CHUNKS):
            for n in range(2):
                pair_copy(k, n, c).wait_send()
            read_copy(k, c).wait_send()
            for d in range(1, freqs):
                freq_copy(k, d, c).wait_send()
        for n in range(3):
            col_copy(k, n).wait_send()


def joint(block, stamps, zero_point, noise_var, footprint, accept, assign):
    rows, width = block.shape
    height = 4 * rows
    stamp_len = stamps.shape[1]
    ids = joint_columns(width)
    th0, tl0, th1, tl1 = joint_row_tables(ids, width)
    psf_rows, psf_cols = joint_psf_tables(height, width, stamp_len)
    vmem = pl.BlockSpec(memory_space=pltpu.VMEM)
    smem = pl.BlockSpec(memory_space=pltpu.SMEM)
    anywhere = pl.BlockSpec(memory_space=pltpu.HBM)
    dma = pltpu.SemaphoreType.DMA
    half, quarter = width // 2, width // 4
    return pl.pallas_call(
        joint_kernel,
        out_shape=jax.ShapeDtypeStruct((2, rows, 256), F32),
        in_specs=[smem] * 5
        + [vmem, anywhere, vmem]
        + [anywhere] * 5
        + [vmem, vmem, anywhere, vmem],
        out_specs=vmem,
        scratch_shapes=[
            pltpu.VMEM((rows + 2 * HALO, width), F32),
            pltpu.VMEM((2, 2, rows + 16, quarter), BF16),
            pltpu.VMEM((2, rows + 16, half), BF16),
            pltpu.VMEM((2, rows + 16, LANES), F32),
            pltpu.VMEM((8, 2, 16, LANES), F32),
            pltpu.VMEM((4, quarter, 256), BF16),
            pltpu.VMEM((4, quarter, 256), BF16),
            pltpu.VMEM((4, half, 256), BF16),
            pltpu.VMEM((4, half, 256), BF16),
            pltpu.VMEM((4, 1024, 512), BF16),
            pltpu.VMEM((rows, LANES), BF16),
            pltpu.VMEM((rows, 256), F32),
            pltpu.VMEM((2, 4, rows, 256), F32),
            pltpu.VMEM((2, 2, rows, 256), F32),
            pltpu.VMEM((2, rows, 256), F32),
            pltpu.VMEM((2, 4, 8, 4, 8, LANES), F32),
            pltpu.VMEM((2, 4, 8, 4, 8, LANES), F32),
            pltpu.VMEM((4, 256, LANES), F32),
            pltpu.VMEM((2, 4, 256, LANES), F32),
            pltpu.VMEM((2, 4, 256, LANES), F32),
            dma((4,)),
            dma((3, 2, 4)),
            dma((2,)),
            dma((2,)),
            dma((2, 2, CHUNKS)),
            dma((2, 2, CHUNKS)),
            dma((2, CHUNKS)),
            dma((2, CHUNKS)),
            dma((2, 3, CHUNKS)),
            dma((2, 3, CHUNKS)),
            dma((2, 3)),
            dma((2, 3)),
        ],
        compiler_params=pltpu.CompilerParams(
            collective_id=0, has_side_effects=True, vmem_limit_bytes=56 * 1024 * 1024
        ),
        cost_estimate=pl.CostEstimate(flops=7 * 10**9, bytes_accessed=18 * 2**20, transcendentals=0),
        name="joint",
    )(
        zero_point, noise_var, footprint.T, accept, assign, stamps, block,
        joint_tap_table(ids, width, stamp_len),
        th0, tl0, th1, tl1, joint_column_tables(height), joint_twiddles(), joint_order(ids, width), psf_rows, psf_cols,
    )


def column_tables(height):
    quarter = height // 4
    inner = np.arange(quarter)
    parts = []
    for j in range(4):
        phase = angles(4 * np.arange(quarter) + j, inner, height)
        parts.append(np.concatenate([np.cos(phase), np.sin(phase)], axis=1))
    return split_np(np.stack(parts))


def order_matrix(share):
    size = 2 * share
    table = np.zeros((size, 2 * size), np.float32)
    for part in range(2):
        for parity in range(2):
            for j in range(share // 2):
                source = part * share + parity * (share // 2) + j
                place = 2 * j + parity
                table[source, part * share + place] = 1.0
                table[source, size + (1 - part) * share + place] = -1.0 if part == 0 else 1.0
    return table.astype(ml_dtypes.bfloat16)


def column_kernel(x, order, th, tl, out):
    height, lanes = x.shape
    quarter = height // 4
    step = pl.program_id(0)
    for j in range(4):

        @pl.when(step == j)
        def _(j=j):
            parts = []
            for f in range(4):
                hi, lo = split(x[f * quarter : (f + 1) * quarter])
                parts.append(dot(hi, order[...]) + dot(lo, order[...]))
            if j % 2 == 0:
                even, odd = parts[0] + parts[2], parts[1] + parts[3]
                mix = even + odd if j == 0 else even - odd
                top, low = mix[:, :lanes], mix[:, lanes:]
            else:
                even, odd = parts[0] - parts[2], parts[1] - parts[3]
                sign = 1.0 if j == 1 else -1.0
                top = even[:, :lanes] + sign * odd[:, lanes:]
                low = even[:, lanes:] - sign * odd[:, :lanes]
            both = jnp.concatenate([top, low], axis=0)
            hi, lo = split(both)
            wide = dot(th[0], jnp.concatenate([hi, lo], axis=1))
            result = wide[:, :lanes] + wide[:, lanes:] + dot(tl[0], hi)
            out[pl.ds(j, quarter, stride=4), :] = result


def columns(x, order, tables):
    height, lanes = x.shape
    quarter = height // 4
    table_spec = pl.BlockSpec((1, quarter, 2 * quarter), lambda j: (j, 0, 0))
    return pl.pallas_call(
        column_kernel,
        grid=(4,),
        out_shape=jax.ShapeDtypeStruct((height, lanes), F32),
        in_specs=[
            pl.BlockSpec((height, lanes), lambda j: (0, 0)),
            pl.BlockSpec((lanes, 2 * lanes), lambda j: (0, 0)),
            table_spec,
            table_spec,
        ],
        out_specs=pl.BlockSpec((height, lanes), lambda j: (0, 0)),
        compiler_params=pltpu.CompilerParams(vmem_limit_bytes=48 * 1024 * 1024),
        name="columns",
    )(x, order, *tables)


def denom_kernel(weight, rows, cols, out):
    count = cols.shape[0]
    lanes = out.shape[1]
    total = jnp.zeros(out.shape, F32)
    rh, rl = split(rows[...])
    for e in range(count):
        chh, cll = split(cols[e])
        psf = dot(rh, chh) + dot(rh, cll) + dot(rl, chh)
        total = total + weight[e] * (psf[:, :lanes] * psf[:, :lanes] + psf[:, lanes:] * psf[:, lanes:])
    out[...] = lax.rsqrt(total)


def per_device(exposures, stamps, zero_point, noise_var, footprint, accept, assign):
    exp_dev, rows_dev, width = exposures.shape
    freqs = lax.axis_size("freq")
    readers = lax.axis_size(READERS)
    height = rows_dev * freqs
    per_freq = width // 2 // freqs
    share = per_freq // readers
    out_rows = height // readers
    stamp_len = stamps.shape[1]
    count_all = assign.shape[0]
    freq_at = lax.axis_index("freq")
    reader_at = lax.axis_index(READERS)
    sizes = (lax.axis_size("read"), lax.axis_size("pair"), freqs)
    if sizes == (2, 2, 4) and (rows_dev, width, stamp_len, count_all) == (512, 2048, 16, 4):
        return joint(exposures[0], stamps, zero_point, noise_var, footprint, accept, assign)
    ids = column_order(width, freqs, readers)
    tiles = ids.shape[1]
    offsets = np.arange(stamp_len) - stamp_len // 2

    block = exposures[0]
    forward = [(i, (i + 1) % freqs) for i in range(freqs)]
    backward = [(t, s) for s, t in forward]
    low = lax.ppermute(block[rows_dev - HALO :], "freq", forward)
    high = lax.ppermute(block[:HALO], "freq", backward)

    labels = jnp.arange(count_all, dtype=jnp.int32)
    owner = jnp.sum(jnp.where(labels == reader_at, assign, 0))
    chosen = labels == owner
    low_row = jnp.sum(jnp.where(chosen, footprint[:, 0], 0))
    high_row = jnp.sum(jnp.where(chosen, footprint[:, 1], 0))
    accepted = accept.astype(F32)
    numer_weight = accepted * zero_point / noise_var
    denom_weight = accepted * zero_point * zero_point / noise_var
    scale = 1.0 / math.sqrt(height * width)
    weight = jnp.sum(jnp.where(chosen, numer_weight, 0.0)) * scale
    stamp = jnp.sum(jnp.where(chosen[:, None, None], stamps, 0.0), axis=0) * weight
    tap_phase = angles(offsets, ids.reshape(-1), width)
    tap_table = np.stack([np.cos(tap_phase), -np.sin(tap_phase)]).astype(np.float32)
    taps = jnp.einsum("ab,cbp->cap", stamp, tap_table, precision=HIGHEST)
    taps = taps.reshape(2, stamp_len, 2, tiles, TILE).transpose(3, 2, 0, 1, 4)
    info = jnp.stack([freq_at * rows_dev, low_row, high_row, jnp.int32(height)]).astype(jnp.int32)

    tables = row_tables(ids, width)
    terms = front(info, low, block, high, taps, tables)
    if tiles != readers:
        terms = terms.reshape(tiles, rows_dev, 2, 2, readers // tiles, TILE * tiles // readers)
        terms = terms.transpose(0, 4, 1, 2, 3, 5).reshape(readers, rows_dev, -1)
    summed = lax.psum_scatter(terms, READERS, scatter_dimension=0, tiled=True)
    summed = summed.reshape(rows_dev, 2, 2, freqs, share // 2)
    summed = summed.transpose(3, 0, 2, 1, 4).reshape(freqs, rows_dev, 2 * share)
    gathered = lax.all_to_all(summed, "freq", split_axis=0, concat_axis=0, tiled=True)
    grid = columns(gathered.reshape(height, 2 * share), order_matrix(share), column_tables(height))
    grid = lax.all_to_all(
        grid.reshape(readers, out_rows, 2 * share), READERS, split_axis=0, concat_axis=0, tiled=True
    )
    numer = grid.reshape(readers, out_rows, 2, share).transpose(2, 1, 0, 3)
    numer = numer.reshape(2, out_rows, per_freq)

    all_u = angles(np.arange(height), offsets, height)
    all_rows = np.concatenate([np.cos(all_u), np.sin(all_u)], axis=1).astype(np.float32)
    psf_rows = lax.dynamic_slice_in_dim(jnp.asarray(all_rows), reader_at * out_rows, out_rows, 0)
    all_v = angles(offsets, np.arange(width // 2), width)
    all_cols = np.stack([np.cos(all_v), -np.sin(all_v)]).astype(np.float32)
    own_cols = lax.dynamic_slice_in_dim(jnp.asarray(all_cols), freq_at * per_freq, per_freq, 2)
    q = jnp.einsum("nab,cbp->cnap", stamps, own_cols, precision=HIGHEST)
    psf_cols = jnp.concatenate(
        [jnp.concatenate([q[0], q[1]], axis=2), jnp.concatenate([q[1], -q[0]], axis=2)], axis=1
    )
    inverse = pl.pallas_call(
        denom_kernel,
        out_shape=jax.ShapeDtypeStruct((out_rows, per_freq), F32),
        in_specs=[
            pl.BlockSpec(memory_space=pltpu.SMEM),
            pl.BlockSpec(memory_space=pltpu.VMEM),
            pl.BlockSpec(memory_space=pltpu.VMEM),
        ],
        out_specs=pl.BlockSpec(memory_space=pltpu.VMEM),
        compiler_params=pltpu.CompilerParams(vmem_limit_bytes=32 * 1024 * 1024),
        name="denom",
    )(denom_weight, psf_rows, psf_cols)
    return numer * inverse


def solution(mesh):
    in_specs = (
        P(("groups", "read", "pair"), "freq", None),
        P("groups", None, None),
        P("groups"),
        P("groups"),
        P("groups", None),
        P("groups"),
        P("groups"),
    )
    out_specs = P(None, ("groups", "read", "pair"), "freq")
    return jax.shard_map(
        per_device, mesh=mesh, in_specs=in_specs, out_specs=out_specs, check_vma=False
    )
```

```python
import functools
import math

import jax
import jax.numpy as jnp
import ml_dtypes
import numpy as np
from jax import lax
from jax.experimental import pallas as pl
from jax.experimental.pallas import tpu as pltpu
from jax.sharding import PartitionSpec as P

HIGHEST = lax.Precision.HIGHEST
TWO_PI = 2.0 * math.pi
HALO = 16
TILE = 128
BF16 = jnp.bfloat16
F32 = jnp.float32
READERS = ("read", "pair")


def split_np(table):
    hi = table.astype(np.float32).astype(ml_dtypes.bfloat16)
    lo = (table - hi.astype(np.float64)).astype(np.float32).astype(ml_dtypes.bfloat16)
    return hi, lo


def split(value):
    hi = value.astype(BF16)
    return hi, (value - hi.astype(F32)).astype(BF16)


def angles(left, right, modulus):
    return (np.outer(left, right) % modulus).astype(np.float64) * (TWO_PI / modulus)


def dot(left, right):
    return jnp.dot(left, right, preferred_element_type=F32)


def column_order(width, freqs, readers):
    share = width // 2 // freqs // readers
    parity = np.arange(2)[:, None, None, None]
    reader = np.arange(readers)[None, :, None, None]
    freq = np.arange(freqs)[None, None, :, None]
    inner = np.arange(share // 2)[None, None, None, :]
    ids = freq * (share * readers) + reader * share + 2 * inner + parity
    return ids.reshape(2, -1, TILE)


def row_tables(ids, width):
    half = np.arange(width // 2)
    parts = []
    for tile in range(ids.shape[1]):
        both = []
        for parity in range(2):
            phase = angles(half, ids[parity, tile], width)
            both.append(np.concatenate([np.cos(phase), -np.sin(phase)], axis=1))
        parts.append(np.stack(both))
    return split_np(np.stack(parts))


def front_kernel(info, low, block, high, taps, th, tl, out, ext, ch, cl, grid):
    rows, width = block.shape
    half = width // 2
    height = info[3]

    @pl.when(pl.program_id(0) == 0)
    def _():
        ext[:HALO] = low[...]
        ext[HALO : HALO + rows] = block[...]
        ext[HALO + rows :] = high[...]
        cols = lax.broadcasted_iota(jnp.int32, (16, width), 1)

        def clean(i, carry):
            at = pl.multiple_of(i * 16, 16)
            piece = ext[pl.ds(at, 32), :]
            mid = piece[8:24]
            ids = info[0] - 8 + at + lax.broadcasted_iota(jnp.int32, (16, 1), 0)
            ids = jnp.where(ids < 0, ids + height, ids)
            ids = jnp.where(ids >= height, ids - height, ids)
            up = jnp.where(ids == 0, 0.0, piece[7:23])
            down = jnp.where(ids == height - 1, 0.0, piece[9:25])
            left = jnp.where(cols == 0, 0.0, pltpu.roll(mid, 1, 1))
            right = jnp.where(cols == width - 1, 0.0, pltpu.roll(mid, width - 1, 1))
            inside = (ids >= info[1]) & (ids < info[2])
            cell = jnp.where(inside, mid - 0.25 * (up + down + left + right), 0.0)
            for parity in range(2):
                if parity == 0:
                    fold = cell[:, :half] + cell[:, half:]
                else:
                    fold = cell[:, :half] - cell[:, half:]
                hi, lo = split(fold)
                ch[parity, pl.ds(at, 16), :] = hi
                cl[parity, pl.ds(at, 16), :] = lo
            return carry

        lax.fori_loop(0, (rows + 16) // 16, clean, 0)

    for parity in range(2):
        grid[parity] = (
            dot(ch[parity], th[0, parity])
            + dot(ch[parity], tl[0, parity])
            + dot(cl[parity], th[0, parity])
        )

    def fir(i, carry):
        at = pl.multiple_of(i * 32, 32)
        for parity in range(2):
            re = grid[parity, pl.ds(at, 48), :TILE]
            im = grid[parity, pl.ds(at, 48), TILE:]
            sum_re = jnp.zeros((32, TILE), F32)
            sum_im = jnp.zeros((32, TILE), F32)
            for k in range(8):
                shift_re = re[k : k + 40]
                shift_im = im[k : k + 40]
                for a in (k, k + 8):
                    qr = taps[0, parity, 0, a : a + 1, :]
                    qi = taps[0, parity, 1, a : a + 1, :]
                    xr = shift_re[a - k : a - k + 32]
                    xi = shift_im[a - k : a - k + 32]
                    sum_re = sum_re + (qr * xr + qi * xi)
                    sum_im = sum_im + (qr * xi - qi * xr)
            lane = parity * 2 * TILE
            out[0, pl.ds(at, 32), lane : lane + TILE] = sum_re
            out[0, pl.ds(at, 32), lane + TILE : lane + 2 * TILE] = sum_im
        return carry

    lax.fori_loop(0, rows // 32, fir, 0)


def front(info, low, block, high, taps, tables):
    rows, width = block.shape
    tiles = tables[0].shape[0]
    whole = lambda shape: pl.BlockSpec(shape, lambda t: (0,) * len(shape))
    table_spec = pl.BlockSpec((1, 2, width // 2, 2 * TILE), lambda t: (t, 0, 0, 0))
    return pl.pallas_call(
        front_kernel,
        grid=(tiles,),
        out_shape=jax.ShapeDtypeStruct((tiles, rows, 4 * TILE), F32),
        in_specs=[
            pl.BlockSpec(memory_space=pltpu.SMEM),
            whole((HALO, width)),
            whole((rows, width)),
            whole((HALO, width)),
            pl.BlockSpec((1, 2, 2, taps.shape[3], TILE), lambda t: (t, 0, 0, 0, 0)),
            table_spec,
            table_spec,
        ],
        out_specs=pl.BlockSpec((1, rows, 4 * TILE), lambda t: (t, 0, 0)),
        scratch_shapes=[
            pltpu.VMEM((rows + 2 * HALO, width), F32),
            pltpu.VMEM((2, rows + 16, width // 2), BF16),
            pltpu.VMEM((2, rows + 16, width // 2), BF16),
            pltpu.VMEM((2, rows + 16, 2 * TILE), F32),
        ],
        compiler_params=pltpu.CompilerParams(vmem_limit_bytes=48 * 1024 * 1024),
        name="front",
    )(info, low, block, high, taps, *tables)


MESH = pl.DeviceIdType.MESH
CHUNKS = 4
LANES = 128


def joint_columns(width):
    per_freq = width // 2 // 4
    freq = np.arange(4)[:, None] * per_freq
    inner = np.arange(32)[None, :]
    groups = []
    for k in range(2):
        for rd in range(2):
            for pd in range(2):
                if k == 0:
                    ids = freq + 4 * (32 * rd + inner) + 2 * pd
                else:
                    ids = freq + 64 * (2 * rd + pd) + 2 * inner + 1
                groups.append(ids.reshape(-1))
    return np.stack(groups)


def joint_row_tables(ids, width):
    even, odd = [], []
    for t in range(8):
        depth = width // 4 if t < 4 else width // 2
        phase = angles(np.arange(depth), ids[t], width)
        table = np.concatenate([np.cos(phase), -np.sin(phase)], axis=1)
        (even if t < 4 else odd).append(table)
    return split_np(np.stack(even)) + split_np(np.stack(odd))


def joint_column_tables(height):
    inner = np.arange(256)
    parts = []
    for g in range(8):
        phase = angles(np.arange(256), 8 * inner + g, height)
        parts.append(np.concatenate([np.cos(phase), np.sin(phase)], axis=1))
    tables = np.stack(split_np(np.stack(parts).reshape(2, 4, 256, 512)))
    return tables.transpose(2, 0, 1, 3, 4).reshape(4, 1024, 512)


def joint_twiddles():
    lane = np.arange(LANES)
    table = np.zeros((4, 8, LANES), np.float32)
    for gg in range(4):
        angle = np.where(lane >= 64, TWO_PI * gg / 8, 0.0)
        real = lane % 64 < 32
        table[gg, 0] = np.cos(angle)
        table[gg, 1] = np.where(real, np.sin(angle), 0.0)
        table[gg, 2] = np.where(real, 0.0, -np.sin(angle))
        table[gg, 3] = np.where(lane < 64, 1.0, -1.0)
    return table


def joint_order(ids, width):
    per_freq = width // 2 // 4
    table = np.zeros((256, 256), np.float32)
    for k in range(2):
        for reader in range(4):
            for i in range(32):
                table[k * LANES + reader * 32 + i, ids[4 * k + reader, i] % per_freq] = 1.0
    return table.astype(ml_dtypes.bfloat16)


def joint_psf_tables(height, width, stamp_len):
    offsets = np.arange(stamp_len) - stamp_len // 2
    all_u = angles(np.arange(height), offsets, height)
    hi, lo = split_np(np.concatenate([np.cos(all_u), np.sin(all_u)], axis=1))
    rows = np.concatenate([hi, lo, hi, np.zeros_like(hi)], axis=1).reshape(4, height // 4, LANES)
    all_v = angles(offsets, np.arange(width // 2), width).reshape(stamp_len, 4, -1)
    cols = np.concatenate([np.cos(all_v), -np.sin(all_v)], axis=2).astype(np.float32)
    return rows, cols.transpose(1, 0, 2)


def joint_tap_table(ids, width, stamp_len):
    offsets = np.arange(stamp_len) - stamp_len // 2
    phase = [angles(offsets, ids[t], width) for t in range(8)]
    return np.concatenate(
        [np.concatenate([np.cos(x), -np.sin(x)], axis=1) for x in phase], axis=1
    ).astype(np.float32)


def turn(quads, lanes):
    low = lanes < 64
    first = [None] * 4
    for q in range(2):
        first[q] = jnp.where(low, quads[q], pltpu.roll(quads[q + 2], 64, 1))
        first[q + 2] = jnp.where(low, pltpu.roll(quads[q], 64, 1), quads[q + 2])
    even = lanes % 64 < 32
    result = [None] * 4
    for q in (0, 2):
        result[q] = jnp.where(even, first[q], pltpu.roll(first[q + 1], 32, 1))
        result[q + 1] = jnp.where(even, pltpu.roll(first[q], 96, 1), first[q + 1])
    return result


def joint_kernel(
    zero_point, noise_var, footprint, accept, assign, stamps, block, tap_table,
    th0, tl0, th1, tl1, ctab, twiddle, order, psf_rows, psf_cols, out,
    ext, even, odd, grid, taps,
    bh0, bl0, bh1, bl1, col_tab, prow, inverse,
    work, pair_in, read_in, freq_out, freq_in, mixed, col_out, col_in,
    block_sem, table_sem, halo_send, halo_recv, pair_send, pair_recv,
    read_send, read_recv, freq_send, freq_recv, col_send, col_recv,
):
    rows, width = block.shape
    freqs = 4
    height = rows * freqs
    quarter = width // 4
    half = width // 2
    r = lax.axis_index("read")
    p = lax.axis_index("pair")
    f = lax.axis_index("freq")
    me = 2 * r + p

    def group_at(s):
        rd = jnp.where(s < 2, 1 - r, r)
        pd = jnp.where(s % 2 == 0, 1 - p, p)
        return rd * 2 + pd

    def block_copy(n):
        size = rows // 4
        return pltpu.make_async_copy(
            block.at[pl.ds(n * size, size)], ext.at[pl.ds(HALO + n * size, size)], block_sem.at[n]
        )

    def row_table_copies(k, s):
        t = group_at(s)
        pairs = ((th0, bh0), (tl0, bl0)) if k == 0 else ((th1, bh1), (tl1, bl1))
        return [
            pltpu.make_async_copy(a.at[t], b.at[s], table_sem.at[k, n, s])
            for n, (a, b) in enumerate(pairs)
        ]

    def column_table_copy():
        return pltpu.make_async_copy(ctab, col_tab, table_sem.at[2, 0, 0])

    def psf_copy():
        return pltpu.make_async_copy(psf_rows.at[me], prow, table_sem.at[2, 0, 2])

    def halo_copies():
        up = lax.rem(f + 1, freqs)
        down = lax.rem(f + freqs - 1, freqs)
        return (
            pltpu.make_async_remote_copy(
                src_ref=block.at[pl.ds(rows - HALO, HALO)], dst_ref=ext.at[pl.ds(0, HALO)],
                send_sem=halo_send.at[0], recv_sem=halo_recv.at[0],
                device_id={"freq": up}, device_id_type=MESH,
            ),
            pltpu.make_async_remote_copy(
                src_ref=block.at[pl.ds(0, HALO)], dst_ref=ext.at[pl.ds(HALO + rows, HALO)],
                send_sem=halo_send.at[1], recv_sem=halo_recv.at[1],
                device_id={"freq": down}, device_id_type=MESH,
            ),
        )

    chunk = rows // CHUNKS

    def pair_copy(k, n, c):
        part = pl.ds(pl.multiple_of(c * chunk, chunk), chunk)
        return pltpu.make_async_remote_copy(
            src_ref=work.at[k, 2 * n, part], dst_ref=pair_in.at[k, n, part],
            send_sem=pair_send.at[k, n, c], recv_sem=pair_recv.at[k, n, c],
            device_id={"pair": 1 - p}, device_id_type=MESH,
        )

    def read_copy(k, c):
        part = pl.ds(pl.multiple_of(c * chunk, chunk), chunk)
        return pltpu.make_async_remote_copy(
            src_ref=work.at[k, 1, part], dst_ref=read_in.at[k, part],
            send_sem=read_send.at[k, c], recv_sem=read_recv.at[k, c],
            device_id={"read": 1 - r}, device_id_type=MESH,
        )

    def freq_copy(k, d, c):
        part = pl.ds(2 * c, 2)
        to = lax.rem(f + d, freqs)
        return pltpu.make_async_remote_copy(
            src_ref=freq_out.at[k, to, part], dst_ref=freq_in.at[k, f, part],
            send_sem=freq_send.at[k, d - 1, c], recv_sem=freq_recv.at[k, d - 1, c],
            device_id={"freq": to}, device_id_type=MESH,
        )

    def col_copy(k, n):
        rd = jnp.where(n > 0, 1 - r, r)
        pd = jnp.where(n == 1, p, 1 - p)
        return pltpu.make_async_remote_copy(
            src_ref=col_out.at[k, 2 * rd + pd], dst_ref=col_in.at[k, me],
            send_sem=col_send.at[k, n], recv_sem=col_recv.at[k, n],
            device_id={"read": rd, "pair": pd}, device_id_type=MESH,
        )

    barrier = pltpu.get_barrier_semaphore()
    for d in range(1, freqs):
        pl.semaphore_signal(
            barrier, inc=1, device_id={"freq": lax.rem(f + d, freqs)}, device_id_type=MESH
        )
    for rd, pd in ((r, 1 - p), (1 - r, p), (1 - r, 1 - p)):
        pl.semaphore_signal(
            barrier, inc=1, device_id={"read": rd, "pair": pd}, device_id_type=MESH
        )
    for n in range(4):
        block_copy(n).start()
    for s in range(2):
        for copy in row_table_copies(0, s):
            copy.start()

    mine = assign[me]
    first_row = footprint[0, mine]
    last_row = footprint[1, mine]
    scale = 1.0 / math.sqrt(height * width)
    top = accept[mine].astype(F32) * zero_point[mine] * scale
    side = stamps.shape[1]
    stamp = stamps[mine] * (jnp.full((side, side), top, F32) / jnp.full((side, side), noise_var[mine], F32))
    every = jnp.dot(stamp, tap_table[...], precision=HIGHEST, preferred_element_type=F32)
    for t in range(8):
        for n in range(2):
            taps[t, n] = every[:, (2 * t + n) * LANES : (2 * t + n + 1) * LANES]

    pl.semaphore_wait(barrier, freqs + 2)
    for copy in halo_copies():
        copy.start()

    edge = lax.broadcasted_iota(jnp.int32, (16, LANES), 1)
    last_lane = width - LANES

    def clean_at(at, rim):
        piece = ext[pl.ds(at, 32), :]
        mid = piece[8:24]
        ids = f * rows - 8 + at + lax.broadcasted_iota(jnp.int32, (16, 1), 0)
        up, down = piece[7:23], piece[9:25]
        if rim:
            ids = jnp.where(ids < 0, ids + height, ids)
            ids = jnp.where(ids >= height, ids - height, ids)
            up = jnp.where(ids == 0, 0.0, up)
            down = jnp.where(ids == height - 1, 0.0, down)
        left = pltpu.roll(mid, 1, 1)
        left = jnp.concatenate(
            [jnp.where(edge == 0, 0.0, left[:, :LANES]), left[:, LANES:]], axis=1
        )
        right = pltpu.roll(mid, width - 1, 1)
        right = jnp.concatenate(
            [right[:, :last_lane], jnp.where(edge == LANES - 1, 0.0, right[:, last_lane:])], axis=1
        )
        inside = (ids >= first_row) & (ids < last_row)
        cell = jnp.where(inside, mid - 0.25 * (up + down + left + right), 0.0)
        total = cell[:, :half] + cell[:, half:]
        here = pl.ds(at, 16)
        odd[0, here, :], odd[1, here, :] = split(cell[:, :half] - cell[:, half:])
        even[0, 0, here, :], even[0, 1, here, :] = split(total[:, :quarter] + total[:, quarter:])
        even[1, 0, here, :], even[1, 1, here, :] = split(total[:, :quarter] - total[:, quarter:])

    for n in range(4):
        block_copy(n).wait()
    for s in range(2, 4):
        for copy in row_table_copies(0, s):
            copy.start()
    for s in range(4):
        for copy in row_table_copies(1, s):
            copy.start()
    column_table_copy().start()
    psf_copy().start()

    lanes = lax.broadcasted_iota(jnp.int32, (32, LANES), 1)

    def pack(k, c):
        pair_copy(k, 1, c).wait_recv()

        def body(n, carry):
            b = 2 * c + n
            quads = []
            for g in range(2):
                here = pl.ds(pl.multiple_of(b * 64 + g * 32, 32), 32)
                total = work[k, 3, here, :] + pair_in[k, 1, here, :] + read_in[k, here, :]
                quads += [total[:, :LANES], total[:, LANES:]]
            for to, value in enumerate(turn(quads, lanes)):
                freq_out[k, to, b] = value.reshape(4, 8, LANES)
            return carry

        lax.fori_loop(0, 2, body, 0, unroll=True)
        for d in range(1, freqs):
            freq_copy(k, d, c).start()

    def wait_tables(k, s):
        for copy in row_table_copies(k, s):
            copy.wait()

    def store_grid(xh, xl, wh, wl):
        both = dot(xh, wh) + dot(xh, wl) + dot(xl, wh)
        grid[0] = both[:, :LANES]
        grid[1] = both[:, LANES:]

    def multiply(k, s):
        @pl.when(k == 0)
        def _():
            wait_tables(0, s)
            kind = group_at(s) % 2
            store_grid(even[kind, 0], even[kind, 1], bh0[s], bl0[s])

        @pl.when(k == 1)
        def _():
            wait_tables(1, s)
            store_grid(odd[0], odd[1], bh1[s], bl1[s])

    def fir(k, s, c):
        t = 4 * k + group_at(s)
        for n in range(2):
            at = pl.multiple_of(c * chunk + n * 64, 64)
            sums = [[jnp.zeros((8, LANES), F32), jnp.zeros((8, LANES), F32)] for _ in range(8)]
            for a in range(16):
                qr = taps[t, 0, a : a + 1, :]
                qi = taps[t, 1, a : a + 1, :]
                for g in range(8):
                    here = pl.ds(at + g + a, 8, stride=8)
                    xr = grid[0, here, :]
                    xi = grid[1, here, :]
                    sums[g][0] = sums[g][0] + (qr * xr + qi * xi)
                    sums[g][1] = sums[g][1] + (qr * xi - qi * xr)
            for g in range(8):
                work[k, s, pl.ds(at + 8 * g, 8), :LANES] = sums[g][0]
                work[k, s, pl.ds(at + 8 * g, 8), LANES:] = sums[g][1]

    def sum_pair(k, c):
        pair_copy(k, 0, c).wait_recv()
        part = pl.ds(pl.multiple_of(c * chunk, chunk), chunk)
        work[k, 1, part, :] = work[k, 1, part, :] + pair_in[k, 0, part, :]

    def group(n, carry):
        k, s = n // 4, n % 4
        multiply(k, s)

        def body(c, inner):
            fir(k, s, c)

            @pl.when(s % 2 == 0)
            def _():
                pair_copy(k, s // 2, c).start()

            @pl.when(s == 1)
            def _():
                sum_pair(k, c)

                @pl.when(c < 2)
                def _():
                    read_copy(k, c).start()

            return inner

        lax.fori_loop(0, CHUNKS, body, 0)

        @pl.when(n == 2)
        def _():
            read_copy(0, 2).wait_recv()
            read_copy(0, 0).start()

        @pl.when((n == 5) | (n == 6))
        def _():
            read_copy(0, lax.rem(n + 2, 4)).wait_recv()

        @pl.when((n == 5) | (n == 6))
        def _():
            read_copy(1, n - 3).start()

        @pl.when((n > 2) & (n < 7))
        def _():
            pack(0, lax.rem(n + 2, 4))

        return carry

    def times_j(x, at):
        real = at % 64 < 32
        return jnp.where(real, pltpu.roll(x, 96, 1), -pltpu.roll(x, 32, 1))

    def columns(k):
        for d in range(1, freqs):
            for c in range(CHUNKS):
                freq_copy(k, d, c).wait_recv()
        freq_in[k, f] = freq_out[k, f]
        tall = lax.broadcasted_iota(jnp.int32, (256, LANES), 1)

        def residue(gg, carry):
            x = freq_in[k, :, :, gg].reshape(256, LANES)
            hi, lo = split(jnp.concatenate([x, times_j(x, tall)], axis=0))
            res = dot(col_tab[gg], jnp.concatenate([hi, lo], axis=1))
            sides = [
                res[n : n + 256, :LANES] + res[n : n + 256, LANES:] + res[n + 512 : n + 768, :LANES]
                for n in (0, 256)
            ]
            both = jnp.where(tall < 64, sides[0], sides[1])
            both = pltpu.roll(both, 64, 1) + both * twiddle[gg, 3:4, :]
            mixed[gg] = (
                both * twiddle[gg, 0:1, :]
                + pltpu.roll(both, 96, 1) * twiddle[gg, 1:2, :]
                + pltpu.roll(both, 32, 1) * twiddle[gg, 2:3, :]
            )
            return carry

        lax.fori_loop(0, 4, residue, 0, unroll=True)

        def last(i, carry):
            here = pl.ds(pl.multiple_of(i * 32, 32), 32)
            e = [mixed[gg, here, :] for gg in range(4)]
            a, b = e[0] + e[2], e[1] + e[3]
            c, d = e[0] - e[2], times_j(e[1] - e[3], lanes)
            col_out[k, 0, here, :] = a + b
            col_out[k, 1, here, :] = c + d
            col_out[k, 2, here, :] = a - b
            col_out[k, 3, here, :] = c - d
            return carry

        lax.fori_loop(0, 8, last, 0, unroll=True)

    def denominator():
        psf_copy().wait()
        count = stamps.shape[0]
        sides = []
        weights = []
        for e in range(count):
            q = jnp.dot(stamps[e], psf_cols[f], precision=HIGHEST, preferred_element_type=F32)
            turned = jnp.concatenate([q[:, 256:], -q[:, :256]], axis=1)
            hi, lo = split(jnp.concatenate([q, turned], axis=0))
            sides.append(jnp.concatenate([hi, hi, lo, jnp.zeros_like(hi)], axis=0))
            value = accept[e].astype(F32) * zero_point[e] * zero_point[e]
            weights.append(jnp.full((1, 256), value, F32) / jnp.full((1, 256), noise_var[e], F32))
        for n in range(4):
            here = pl.ds(n * 128, 128)
            total = jnp.zeros((128, 256), F32)
            for e in range(count):
                psf = dot(prow[here, :], sides[e])
                re, im = psf[:, :256], psf[:, 256:]
                total = total + weights[e] * (re * re + im * im)
            inverse[here, :] = lax.rsqrt(total)

    def open_half(i, carry):
        c0 = 1 + 2 * i

        def piece(t, inner):
            at = jnp.where(i == 0, 8 + t, jnp.where(t < 7, 25 + t, t - 6))
            clean_at(pl.multiple_of(at * 16, 16), False)
            return inner

        lax.fori_loop(0, 17 - 3 * i, piece, 0)

        @pl.when(i == 1)
        def _():
            for copy in halo_copies():
                copy.wait_recv()

            def rim(t, inner):
                clean_at(pl.multiple_of(t * rows, rows), True)
                return inner

            lax.fori_loop(0, 2, rim, 0)

        def two(s, inner):
            @pl.when(i == 0)
            def _():
                wait_tables(0, s)

            kind = group_at(s) % 2
            spots = [
                pl.ds(pl.multiple_of(lax.rem(c0 + n, CHUNKS) * chunk, chunk), chunk + 16)
                for n in range(2)
            ]
            xh = jnp.concatenate([even[kind, 0, here, :] for here in spots], axis=0)
            xl = jnp.concatenate([even[kind, 1, here, :] for here in spots], axis=0)
            both = dot(xh, bh0[s]) + dot(xh, bl0[s]) + dot(xl, bh0[s])
            for n, here in enumerate(spots):
                part = both[n * (chunk + 16) : (n + 1) * (chunk + 16)]
                grid[0, here, :] = part[:, :LANES]
                grid[1, here, :] = part[:, LANES:]

            def body(n, inner2):
                c = lax.rem(c0 + n, CHUNKS)
                fir(0, s, c)

                @pl.when(s == 0)
                def _():
                    pair_copy(0, 0, c).start()

                @pl.when(s == 1)
                def _():
                    sum_pair(0, c)

                    @pl.when(i == 0)
                    def _():
                        read_copy(0, c).start()

                return inner2

            lax.fori_loop(0, 2, body, 0)
            return inner

        lax.fori_loop(0, 2, two, 0)
        return carry

    lax.fori_loop(0, 2, open_half, 0)
    read_copy(0, 1).wait_recv()
    read_copy(0, 3).start()
    lax.fori_loop(2, 8, group, 0)

    def receive(c, carry):
        read_copy(1, c).wait_recv()

        @pl.when(c == 3)
        def _():
            col_copy(0, 1).start()
            col_copy(0, 2).start()

        pack(1, c)
        return carry

    column_table_copy().wait()

    def ending(k, carry):
        lax.fori_loop(3 * k, 3 + k, receive, 0)

        @pl.when(k == 1)
        def _():
            denominator()

        columns(k)
        col_copy(k, 0).start()

        @pl.when(k == 1)
        def _():
            col_copy(1, 1).start()
            col_copy(1, 2).start()

        return carry

    lax.fori_loop(0, 2, ending, 0)
    wide = lax.broadcasted_iota(jnp.int32, (64, LANES), 1)
    for k in range(2):
        col_in[k, me] = col_out[k, me]
        for n in range(3):
            col_copy(k, n).wait_recv()
        place = order[k * LANES : (k + 1) * LANES, :]

        def finish(i, carry, k=k, place=place):
            at = pl.multiple_of(i * 64, 64)
            quads = [col_in[k, n, pl.ds(at, 64), :] for n in range(4)]
            hi, lo = split(jnp.concatenate(turn(quads, wide), axis=0))
            result = dot(hi, place) + dot(lo, place)
            for q in range(4):
                here = pl.ds(256 * (q // 2) + at, 64)
                value = result[64 * q : 64 * (q + 1)]
                if k == 0:
                    out[q % 2, here, :] = value
                else:
                    out[q % 2, here, :] = (out[q % 2, here, :] + value) * inverse[here, :]
            return carry

        lax.fori_loop(0, 4, finish, 0, unroll=True)

    for copy in halo_copies():
        copy.wait_send()
    for k in range(2):
        for c in range(CHUNKS):
            for n in range(2):
                pair_copy(k, n, c).wait_send()
            read_copy(k, c).wait_send()
            for d in range(1, freqs):
                freq_copy(k, d, c).wait_send()
        for n in range(3):
            col_copy(k, n).wait_send()


def joint(block, stamps, zero_point, noise_var, footprint, accept, assign):
    rows, width = block.shape
    height = 4 * rows
    stamp_len = stamps.shape[1]
    ids = joint_columns(width)
    th0, tl0, th1, tl1 = joint_row_tables(ids, width)
    psf_rows, psf_cols = joint_psf_tables(height, width, stamp_len)
    vmem = pl.BlockSpec(memory_space=pltpu.VMEM)
    smem = pl.BlockSpec(memory_space=pltpu.SMEM)
    anywhere = pl.BlockSpec(memory_space=pltpu.HBM)
    dma = pltpu.SemaphoreType.DMA
    half, quarter = width // 2, width // 4
    return pl.pallas_call(
        joint_kernel,
        out_shape=jax.ShapeDtypeStruct((2, rows, 256), F32),
        in_specs=[smem] * 5
        + [vmem, anywhere, vmem]
        + [anywhere] * 5
        + [vmem, vmem, anywhere, vmem],
        out_specs=vmem,
        scratch_shapes=[
            pltpu.VMEM((rows + 2 * HALO, width), F32),
            pltpu.VMEM((2, 2, rows + 16, quarter), BF16),
            pltpu.VMEM((2, rows + 16, half), BF16),
            pltpu.VMEM((2, rows + 16, LANES), F32),
            pltpu.VMEM((8, 2, 16, LANES), F32),
            pltpu.VMEM((4, quarter, 256), BF16),
            pltpu.VMEM((4, quarter, 256), BF16),
            pltpu.VMEM((4, half, 256), BF16),
            pltpu.VMEM((4, half, 256), BF16),
            pltpu.VMEM((4, 1024, 512), BF16),
            pltpu.VMEM((rows, LANES), BF16),
            pltpu.VMEM((rows, 256), F32),
            pltpu.VMEM((2, 4, rows, 256), F32),
            pltpu.VMEM((2, 2, rows, 256), F32),
            pltpu.VMEM((2, rows, 256), F32),
            pltpu.VMEM((2, 4, 8, 4, 8, LANES), F32),
            pltpu.VMEM((2, 4, 8, 4, 8, LANES), F32),
            pltpu.VMEM((4, 256, LANES), F32),
            pltpu.VMEM((2, 4, 256, LANES), F32),
            pltpu.VMEM((2, 4, 256, LANES), F32),
            dma((4,)),
            dma((3, 2, 4)),
            dma((2,)),
            dma((2,)),
            dma((2, 2, CHUNKS)),
            dma((2, 2, CHUNKS)),
            dma((2, CHUNKS)),
            dma((2, CHUNKS)),
            dma((2, 3, CHUNKS)),
            dma((2, 3, CHUNKS)),
            dma((2, 3)),
            dma((2, 3)),
        ],
        compiler_params=pltpu.CompilerParams(
            collective_id=0, has_side_effects=True, vmem_limit_bytes=56 * 1024 * 1024
        ),
        cost_estimate=pl.CostEstimate(flops=7 * 10**9, bytes_accessed=18 * 2**20, transcendentals=0),
        name="joint",
    )(
        zero_point, noise_var, footprint.T, accept, assign, stamps, block,
        joint_tap_table(ids, width, stamp_len),
        th0, tl0, th1, tl1, joint_column_tables(height), joint_twiddles(), joint_order(ids, width), psf_rows, psf_cols,
    )


def column_tables(height):
    quarter = height // 4
    inner = np.arange(quarter)
    parts = []
    for j in range(4):
        phase = angles(4 * np.arange(quarter) + j, inner, height)
        parts.append(np.concatenate([np.cos(phase), np.sin(phase)], axis=1))
    return split_np(np.stack(parts))


def order_matrix(share):
    size = 2 * share
    table = np.zeros((size, 2 * size), np.float32)
    for part in range(2):
        for parity in range(2):
            for j in range(share // 2):
                source = part * share + parity * (share // 2) + j
                place = 2 * j + parity
                table[source, part * share + place] = 1.0
                table[source, size + (1 - part) * share + place] = -1.0 if part == 0 else 1.0
    return table.astype(ml_dtypes.bfloat16)


def column_kernel(x, order, th, tl, out):
    height, lanes = x.shape
    quarter = height // 4
    step = pl.program_id(0)
    for j in range(4):

        @pl.when(step == j)
        def _(j=j):
            parts = []
            for f in range(4):
                hi, lo = split(x[f * quarter : (f + 1) * quarter])
                parts.append(dot(hi, order[...]) + dot(lo, order[...]))
            if j % 2 == 0:
                even, odd = parts[0] + parts[2], parts[1] + parts[3]
                mix = even + odd if j == 0 else even - odd
                top, low = mix[:, :lanes], mix[:, lanes:]
            else:
                even, odd = parts[0] - parts[2], parts[1] - parts[3]
                sign = 1.0 if j == 1 else -1.0
                top = even[:, :lanes] + sign * odd[:, lanes:]
                low = even[:, lanes:] - sign * odd[:, :lanes]
            both = jnp.concatenate([top, low], axis=0)
            hi, lo = split(both)
            wide = dot(th[0], jnp.concatenate([hi, lo], axis=1))
            result = wide[:, :lanes] + wide[:, lanes:] + dot(tl[0], hi)
            out[pl.ds(j, quarter, stride=4), :] = result


def columns(x, order, tables):
    height, lanes = x.shape
    quarter = height // 4
    table_spec = pl.BlockSpec((1, quarter, 2 * quarter), lambda j: (j, 0, 0))
    return pl.pallas_call(
        column_kernel,
        grid=(4,),
        out_shape=jax.ShapeDtypeStruct((height, lanes), F32),
        in_specs=[
            pl.BlockSpec((height, lanes), lambda j: (0, 0)),
            pl.BlockSpec((lanes, 2 * lanes), lambda j: (0, 0)),
            table_spec,
            table_spec,
        ],
        out_specs=pl.BlockSpec((height, lanes), lambda j: (0, 0)),
        compiler_params=pltpu.CompilerParams(vmem_limit_bytes=48 * 1024 * 1024),
        name="columns",
    )(x, order, *tables)


def denom_kernel(weight, rows, cols, out):
    count = cols.shape[0]
    lanes = out.shape[1]
    total = jnp.zeros(out.shape, F32)
    rh, rl = split(rows[...])
    for e in range(count):
        chh, cll = split(cols[e])
        psf = dot(rh, chh) + dot(rh, cll) + dot(rl, chh)
        total = total + weight[e] * (psf[:, :lanes] * psf[:, :lanes] + psf[:, lanes:] * psf[:, lanes:])
    out[...] = lax.rsqrt(total)


def per_device(exposures, stamps, zero_point, noise_var, footprint, accept, assign):
    exp_dev, rows_dev, width = exposures.shape
    freqs = lax.axis_size("freq")
    readers = lax.axis_size(READERS)
    height = rows_dev * freqs
    per_freq = width // 2 // freqs
    share = per_freq // readers
    out_rows = height // readers
    stamp_len = stamps.shape[1]
    count_all = assign.shape[0]
    freq_at = lax.axis_index("freq")
    reader_at = lax.axis_index(READERS)
    sizes = (lax.axis_size("read"), lax.axis_size("pair"), freqs)
    if sizes == (2, 2, 4) and (rows_dev, width, stamp_len, count_all) == (512, 2048, 16, 4):
        return joint(exposures[0], stamps, zero_point, noise_var, footprint, accept, assign)
    ids = column_order(width, freqs, readers)
    tiles = ids.shape[1]
    offsets = np.arange(stamp_len) - stamp_len // 2

    block = exposures[0]
    forward = [(i, (i + 1) % freqs) for i in range(freqs)]
    backward = [(t, s) for s, t in forward]
    low = lax.ppermute(block[rows_dev - HALO :], "freq", forward)
    high = lax.ppermute(block[:HALO], "freq", backward)

    labels = jnp.arange(count_all, dtype=jnp.int32)
    owner = jnp.sum(jnp.where(labels == reader_at, assign, 0))
    chosen = labels == owner
    low_row = jnp.sum(jnp.where(chosen, footprint[:, 0], 0))
    high_row = jnp.sum(jnp.where(chosen, footprint[:, 1], 0))
    accepted = accept.astype(F32)
    numer_weight = accepted * zero_point / noise_var
    denom_weight = accepted * zero_point * zero_point / noise_var
    scale = 1.0 / math.sqrt(height * width)
    weight = jnp.sum(jnp.where(chosen, numer_weight, 0.0)) * scale
    stamp = jnp.sum(jnp.where(chosen[:, None, None], stamps, 0.0), axis=0) * weight
    tap_phase = angles(offsets, ids.reshape(-1), width)
    tap_table = np.stack([np.cos(tap_phase), -np.sin(tap_phase)]).astype(np.float32)
    taps = jnp.einsum("ab,cbp->cap", stamp, tap_table, precision=HIGHEST)
    taps = taps.reshape(2, stamp_len, 2, tiles, TILE).transpose(3, 2, 0, 1, 4)
    info = jnp.stack([freq_at * rows_dev, low_row, high_row, jnp.int32(height)]).astype(jnp.int32)

    tables = row_tables(ids, width)
    terms = front(info, low, block, high, taps, tables)
    if tiles != readers:
        terms = terms.reshape(tiles, rows_dev, 2, 2, readers // tiles, TILE * tiles // readers)
        terms = terms.transpose(0, 4, 1, 2, 3, 5).reshape(readers, rows_dev, -1)
    summed = lax.psum_scatter(terms, READERS, scatter_dimension=0, tiled=True)
    summed = summed.reshape(rows_dev, 2, 2, freqs, share // 2)
    summed = summed.transpose(3, 0, 2, 1, 4).reshape(freqs, rows_dev, 2 * share)
    gathered = lax.all_to_all(summed, "freq", split_axis=0, concat_axis=0, tiled=True)
    grid = columns(gathered.reshape(height, 2 * share), order_matrix(share), column_tables(height))
    grid = lax.all_to_all(
        grid.reshape(readers, out_rows, 2 * share), READERS, split_axis=0, concat_axis=0, tiled=True
    )
    numer = grid.reshape(readers, out_rows, 2, share).transpose(2, 1, 0, 3)
    numer = numer.reshape(2, out_rows, per_freq)

    all_u = angles(np.arange(height), offsets, height)
    all_rows = np.concatenate([np.cos(all_u), np.sin(all_u)], axis=1).astype(np.float32)
    psf_rows = lax.dynamic_slice_in_dim(jnp.asarray(all_rows), reader_at * out_rows, out_rows, 0)
    all_v = angles(offsets, np.arange(width // 2), width)
    all_cols = np.stack([np.cos(all_v), -np.sin(all_v)]).astype(np.float32)
    own_cols = lax.dynamic_slice_in_dim(jnp.asarray(all_cols), freq_at * per_freq, per_freq, 2)
    q = jnp.einsum("nab,cbp->cnap", stamps, own_cols, precision=HIGHEST)
    psf_cols = jnp.concatenate(
        [jnp.concatenate([q[0], q[1]], axis=2), jnp.concatenate([q[1], -q[0]], axis=2)], axis=1
    )
    inverse = pl.pallas_call(
        denom_kernel,
        out_shape=jax.ShapeDtypeStruct((out_rows, per_freq), F32),
        in_specs=[
            pl.BlockSpec(memory_space=pltpu.SMEM),
            pl.BlockSpec(memory_space=pltpu.VMEM),
            pl.BlockSpec(memory_space=pltpu.VMEM),
        ],
        out_specs=pl.BlockSpec(memory_space=pltpu.VMEM),
        compiler_params=pltpu.CompilerParams(vmem_limit_bytes=32 * 1024 * 1024),
        name="denom",
    )(denom_weight, psf_rows, psf_cols)
    return numer * inverse


def solution(mesh):
    in_specs = (
        P(("groups", "read", "pair"), "freq", None),
        P("groups", None, None),
        P("groups"),
        P("groups"),
        P("groups", None),
        P("groups"),
        P("groups"),
    )
    out_specs = P(None, ("groups", "read", "pair"), "freq")
    return jax.shard_map(
        per_device, mesh=mesh, in_specs=in_specs, out_specs=out_specs, check_vma=False
    )
```
